32 devices in a mesh: groups: 2 (over y), row: 4 (over z), col: 4 (over x, core).
Axes of the slice: x: 2, y: 2, z: 4, core: 2. Of those that a mesh axis runs over, the one named last changes fastest.
Arguments:
- acts: bfloat16 [8, 512, 8192], P('groups', 'row'), parts along dimension 0, may hold values from -6 to 6
- grads: bfloat16 [8, 512, 32768], P('groups', 'row', 'col'), parts along dimension 0, may hold values from -0.26367188 to 0.26367188
- act_basis: bfloat16 [8192, 1024], P(None, 'col'), may hold values from -0.0625 to 0.0625
- grad_basis: bfloat16 [32768, 4096], P('col', 'row'), may hold values from -0.03125 to 0.03125
- eigenvalues: float32 [4096, 1024], P('row', 'col'), may hold values from 0.02 to 2.5
- query_rotated: bfloat16 [4, 4096, 1024], P(None, 'row', 'col'), may hold values from -0.0005836487 to 0.0005836487
- example_ids: int32 [8], P('groups'), parts along dimension 0, may hold values from 0 to 2047
- token_counts: int32 [2048], replicated, may hold values from 256 to 512
Outputs:
- rotated: float32 [8, 4096, 1024], P('groups', 'row', 'col'), parts along dimension 0
- scores: float32 [4, 8], P(None, 'groups'), parts along dimension 1
The draws below stay inside these ranges and needn't reach their ends.
There are 2 independent parts, one for each index of `groups`. The reference program is written for one: setup_inputs(seed, part) draws one part's arguments, and reference() takes and returns one part's arrays. A program takes and returns all parts, laid end to end along the dimension named above; an argument that names none is the same for every part. Nothing has to cross between parts.
All inputs are finite; a program needn't handle non-finite values.
Results may differ from the reference program's by a relative error of at most 0.0051.
Values may be sent and summed in bfloat16 or wider, within the bound.
No kernel may reach another device: no remote copies, remote signals or barrier semaphores. Data moves between devices by JAX's collectives and lax.ppermute only.
A program may use at most 192 MiB of HBM per device.

```python
import jax
import jax.numpy as jnp
from jax import lax

DIN = 8192
DOUT = 32768
KS = 4096
KA = 1024
SEQ = 512
QUERIES = 4
POOL = 2048
CAND = 4


def draw_eigenvalues(key, part):
    key = jax.random.fold_in(key, 11)
    first = jnp.arange(KS, dtype=jnp.float32)[:, None] / KS
    second = jnp.arange(KA, dtype=jnp.float32)[None, :] / KA
    trend = jnp.exp(-2.0 * first - second)
    rough = jnp.exp(jax.random.uniform(key, (KS, KA), jnp.float32, -0.7, 0.7))
    return (trend * rough).astype(jnp.float32)


def draw_token_counts(key, part):
    key = jax.random.fold_in(key, 23)
    first_key, second_key = jax.random.split(key)
    counts = jax.random.randint(first_key, (POOL,), SEQ // 2, SEQ + 1)
    chosen = jax.random.randint(second_key, (), 0, POOL)
    return jnp.where(jnp.arange(POOL) == chosen, SEQ, counts).astype(jnp.int32)


def touch_ends(result, stream_key, smallest, largest):
    index_at = [jax.random.randint(jax.random.fold_in(stream_key, axis), (), 0, length) for axis, length in enumerate(result.shape)]
    widest = result.shape.index(max(result.shape))
    beside = index_at[:widest] + [(index_at[widest] + 1) % result.shape[widest]] + index_at[widest + 1:]
    return result.at[tuple(index_at)].set(smallest).at[tuple(beside)].set(largest)


def block_levels(rng, shape, shards, smallest, largest):
    def one(position, blocks):
        heights = jax.random.uniform(jax.random.fold_in(jax.random.fold_in(rng, 6), position), (blocks,), jnp.float32, smallest / len(shards), largest / len(shards))
        return jnp.repeat(jnp.exp(heights), shape[position] // blocks).reshape((-1,) + (1,) * (len(shape) - position - 1))

    factor_of = one(*shards[0])
    for cut in shards[1:]:
        factor_of = factor_of * one(*cut)
    return factor_of


def normal_values(stream_key, extent, spread, bound, shards=(), kind=jnp.bfloat16):
    entries = spread * jax.random.normal(stream_key, extent, jnp.float32)
    if shards:
        entries = entries * block_levels(stream_key, extent, shards, -0.22, 0.18)
    return jnp.clip(entries, -bound, bound).astype(kind)


def setup_inputs(seed: int = 0, part: int = 0) -> dict:
    splits = jax.random.split(jax.random.key(seed), 9)
    part_splits = jax.random.split(jax.random.fold_in(splits[8], part), 9)
    acts = normal_values(part_splits[0], (CAND, SEQ, DIN), 1.0, 6.0, ((1, 4),))
    grads = normal_values(part_splits[1], (CAND, SEQ, DOUT), (SEQ ** -0.5), 0.26367188, ((1, 4), (2, 4)))
    act_basis = normal_values(splits[2], (DIN, KA), DIN ** -0.5, 0.0625, ((1, 4),))
    grad_basis = normal_values(splits[3], (DOUT, KS), DOUT ** -0.5, 0.03125, ((0, 4), (1, 4)))
    eigenvalues = draw_eigenvalues(jax.random.fold_in(splits[8], 71), part)
    query_rotated = normal_values(splits[5], (QUERIES, KS, KA), (0.2 * (KS * KA) ** -0.5), 0.0005836487, ((1, 4), (2, 4)))
    example_ids = touch_ends(jax.random.randint(part_splits[6], (CAND,), 0, POOL), jax.random.fold_in(part_splits[6], 1), 0, POOL - 1).astype(jnp.int32)
    token_counts = draw_token_counts(jax.random.fold_in(splits[8], 71), part)
    return dict(acts=acts, grads=grads, act_basis=act_basis, grad_basis=grad_basis, eigenvalues=eigenvalues, query_rotated=query_rotated, example_ids=example_ids, token_counts=token_counts)


DAMPING = 0.05


def candidate_lengths(example_ids, token_counts):
    table = jnp.arange(POOL, dtype=jnp.int32)
    hits = example_ids[:, None] == table[None, :]
    return jnp.sum(jnp.where(hits, token_counts[None, :], 0), axis=1).astype(jnp.int32)


def reference(acts, grads, act_basis, grad_basis, eigenvalues, query_rotated, example_ids, token_counts):
    lengths = candidate_lengths(example_ids, token_counts)
    positions = jnp.arange(SEQ, dtype=jnp.int32)
    live = (positions[None, :] < lengths[:, None]).astype(jnp.float32)
    act_flat = jnp.dot(acts.reshape(CAND * SEQ, DIN), act_basis, preferred_element_type=jnp.float32)
    act_rot = (act_flat.reshape(CAND, SEQ, KA) * live[:, :, None]).astype(jnp.bfloat16)
    grad_sum = jnp.dot(grads.reshape(CAND * SEQ, DOUT), grad_basis, preferred_element_type=jnp.float32)
    grad_rot = grad_sum.reshape(CAND, SEQ, KS).astype(jnp.bfloat16)
    rotated = jnp.einsum("ctj,ctk->cjk", grad_rot.astype(jnp.float32), act_rot.astype(jnp.float32), precision=lax.Precision.HIGHEST)
    weights = query_rotated.astype(jnp.float32) / (eigenvalues + DAMPING)
    scores = jnp.einsum("qjk,cjk->qc", weights, rotated, precision=lax.Precision.HIGHEST)
    return rotated, scores
```

```python
import jax
import jax.numpy as jnp
from jax import lax
from jax.experimental import pallas as pl
from jax.experimental.pallas import tpu as pltpu
from jax.sharding import PartitionSpec as P

DAMPING = 0.05
BF16 = jnp.bfloat16
F32 = jnp.float32


def candidate_lengths(example_ids, token_counts):
    pool_size = token_counts.shape[0]
    hits = example_ids[:, None] == jnp.arange(pool_size, dtype=jnp.int32)[None, :]
    return jnp.sum(jnp.where(hits, token_counts[None, :], 0), axis=1)


def local_activations(acts, act_basis, lengths):
    tok = acts.shape[1]
    positions = lax.axis_index("row") * tok + jnp.arange(tok, dtype=jnp.int32)
    live = (positions[None, :] < lengths[:, None]).astype(F32)
    rotated = jnp.einsum("ctd,dk->ctk", acts, act_basis, preferred_element_type=F32)
    return (rotated * live[:, :, None]).astype(BF16)


def final_kernel(grad_ref, act_ref, eig_ref, query_ref, out_ref, score_ref):
    cands, queries = grad_ref.shape[0], query_ref.shape[0]
    damped = eig_ref[...] + DAMPING
    weights = [query_ref[q].astype(F32) / damped for q in range(queries)]
    rows = []
    for c in range(cands):
        tile = lax.dot_general(
            grad_ref[c], act_ref[c], (((0,), (0,)), ((), ())), preferred_element_type=F32
        )
        out_ref[c] = tile
        rows.append([jnp.sum(weights[q] * tile, axis=0, keepdims=True) for q in range(queries)])
    score_ref[0] = jnp.concatenate(
        [rows[c][q] for q in range(queries) for c in range(cands)], axis=0
    )


def rotate_and_score(grad_rot, act_rot, eigenvalues, query_rotated):
    cands, seq, dirs = grad_rot.shape
    width = act_rot.shape[2]
    queries = query_rotated.shape[0]
    block = min(dirs, 256)
    steps = dirs // block
    rotated, partial_scores = pl.pallas_call(
        final_kernel,
        grid=(steps,),
        in_specs=[
            pl.BlockSpec((cands, seq, block), lambda i: (0, 0, i)),
            pl.BlockSpec((cands, seq, width), lambda i: (0, 0, 0)),
            pl.BlockSpec((block, width), lambda i: (i, 0)),
            pl.BlockSpec((queries, block, width), lambda i: (0, i, 0)),
        ],
        out_specs=[
            pl.BlockSpec((cands, block, width), lambda i: (0, i, 0)),
            pl.BlockSpec((1, queries * cands, width), lambda i: (i, 0, 0)),
        ],
        out_shape=[
            jax.ShapeDtypeStruct((cands, dirs, width), F32),
            jax.ShapeDtypeStruct((steps, queries * cands, width), F32),
        ],
        compiler_params=pltpu.CompilerParams(vmem_limit_bytes=32 * 2**20),
    )(grad_rot, act_rot, eigenvalues, query_rotated)
    scores = jnp.sum(partial_scores, axis=(0, 2)).reshape(queries, cands)
    return rotated, lax.psum(scores, ("row", "col"))


def gather_body(acts, grads, act_basis, grad_basis, eigenvalues, query_rotated, example_ids, token_counts):
    lengths = candidate_lengths(example_ids, token_counts)
    local_act = local_activations(acts, act_basis, lengths)
    partial_value = jnp.einsum(
        "ctd,dj->ctj",
        lax.all_gather(grads, "row", axis=1, tiled=True),
        grad_basis,
        preferred_element_type=F32,
    )
    every_act = lax.all_gather(local_act, "row", axis=1, tiled=True)
    rotated_grads = lax.psum(partial_value, "col").astype(BF16)
    return rotate_and_score(rotated_grads, every_act, eigenvalues, query_rotated)


def after(value, *earlier):
    return lax.optimization_barrier((value, *earlier))[0]


def chain_body(acts, grads, act_basis, grad_basis, eigenvalues, query_rotated, example_ids, token_counts):
    cands, tok, feats = grads.shape
    dirs = grad_basis.shape[1]
    group, row, col = (lax.axis_index(a) for a in ("groups", "row", "col"))
    sides, parts = 2, 4
    inward = [(0, 1), (3, 2)]
    across = [(1, 2), (2, 1)]
    outward = [(1, 0), (2, 3)]
    planes = 4
    swap = [(g * planes + r, (1 - g) * planes + r) for g in range(sides) for r in (1, 2)]
    at_end = (row == 0) | (row == planes - 1)

    other = lax.ppermute(grads, "row", across)

    half = dirs // sides
    pieces = 4
    deep = feats // pieces
    near, far = [], []
    for k in range(pieces):
        piece = lax.dynamic_slice(grad_basis, (k * deep, group * half), (deep, half))
        if k >= 2:
            piece = after(piece, near[k - 2])
        near.append(lax.ppermute(piece, "row", inward))
        far.append(lax.ppermute(near[k], ("groups", "row"), swap))

    spans = [(c, s, tok // 2) for c in range(cands) for s in (0, tok // 2)]
    started = list(near)
    first, second = [], []
    for c, s, n in spans:
        piece = after(lax.slice(grads, (c, s, 0), (c + 1, s + n, feats))[0], started[-2])
        first.append(lax.ppermute(piece, "row", inward))
        started.append(first[-1])
        second.append(lax.ppermute(first[-1], "row", across))

    lengths = candidate_lengths(example_ids, token_counts)
    local_act = local_activations(acts, act_basis, lengths)
    every_act = lax.all_gather(local_act, "row", axis=0)

    near_basis = jnp.concatenate(near, axis=0)
    far_basis = jnp.concatenate(far, axis=0)

    def multiply(tokens):
        def dot(basis):
            return lax.dot_general(
                tokens, basis, (((tokens.ndim - 1,), (0,)), ((), ())), preferred_element_type=F32
            ).astype(BF16)

        one, two = dot(near_basis), dot(far_basis)
        low = jnp.where(group == 0, one, two)
        high = jnp.where(group == 0, two, one)
        return jnp.concatenate([dot(grad_basis), low, high], axis=-1)

    def finish(value):
        held = lax.dynamic_index_in_dim(value, col, 0, keepdims=False).astype(F32)
        for d in range(1, parts):
            sent = lax.dynamic_index_in_dim(value, col ^ d, 0, keepdims=False)
            held = held + lax.ppermute(sent, "col", [(i, i ^ d) for i in range(parts)]).astype(F32)
        total = held.astype(BF16)
        back = lax.ppermute(total[:, dirs:], "row", outward)
        mine = jnp.where(at_end, back, total[:, :dirs])
        return [mine] + [
            lax.ppermute(mine, "col", [(i, i ^ d) for i in range(parts)]) for d in range(1, parts)
        ]

    sub = tok // parts
    both = jnp.stack([multiply(grads), multiply(other)])
    both = both.reshape(2, cands, parts, sub, 2 * dirs)
    both = jnp.moveaxis(both, 2, 0).reshape(parts, 2 * cands * sub, 2 * dirs)
    middle = jnp.stack([x.reshape(2, cands, sub, dirs) for x in finish(both)])
    middle = jnp.transpose(middle, (2, 0, 1, 3, 4)).reshape(cands, parts * 2 * sub, dirs)

    grad_by_cand = [[middle[c]] for c in range(cands)]
    act_order = {}
    for (c, s, n), one, two in zip(spans, first, second):
        value = multiply(jnp.stack([one, two])).reshape(2, parts, n // parts, 2 * dirs)
        value = jnp.moveaxis(value, 1, 0).reshape(parts, 2 * (n // parts), 2 * dirs)
        for d, x in enumerate(finish(value)):
            grad_by_cand[c].append(x)
    grad_rot = jnp.stack([jnp.concatenate(g, axis=0) for g in grad_by_cand])

    own_order = jnp.where(row < 2, every_act, every_act[::-1])

    def by_part(block, n):
        split = block.reshape(cands, parts, n // parts, -1)
        split = jnp.where((col & 1) == 1, split[:, jnp.array([1, 0, 3, 2])], split)
        split = jnp.where((col & 2) == 2, split[:, jnp.array([2, 3, 0, 1])], split)
        return jnp.moveaxis(split, 1, 0)

    width = every_act.shape[-1]
    inner = jnp.stack([by_part(own_order[1], tok), by_part(own_order[2], tok)])
    inner = jnp.transpose(inner, (2, 1, 0, 3, 4)).reshape(cands, parts * 2 * sub, width)
    act_by_cand = [[inner[c]] for c in range(cands)]
    for c, s, n in spans:
        pair = jnp.stack([by_part(own_order[e][:, s : s + n], n)[:, c] for e in (0, 3)])
        act_by_cand[c].append(jnp.moveaxis(pair, 1, 0).reshape(2 * n, width))
    act_rot = jnp.stack([jnp.concatenate(a, axis=0) for a in act_by_cand])
    return rotate_and_score(grad_rot, act_rot, eigenvalues, query_rotated)


def solution(mesh):
    placed = (
        P("groups", "row", None),
        P("groups", "row", "col"),
        P(None, "col"),
        P("col", "row"),
        P("row", "col"),
        P(None, "row", "col"),
        P("groups"),
        P(),
    )
    chain = mesh.shape["groups"] == 2 and mesh.shape["row"] == 4 and mesh.shape["col"] == 4
    return jax.shard_map(
        chain_body if chain else gather_body,
        mesh=mesh,
        in_specs=placed,
        out_specs=(P("groups", "row", "col"), P(None, "groups")),
        check_vma=False,
    )
```

```python
import functools

import jax
import jax.numpy as jnp
from jax import lax
from jax.experimental import pallas as pl
from jax.experimental.pallas import tpu as pltpu
from jax.sharding import PartitionSpec as P

DAMPING = 0.05
BF16 = jnp.bfloat16
F32 = jnp.float32


def candidate_lengths(example_ids, token_counts):
    pool_size = token_counts.shape[0]
    hits = example_ids[:, None] == jnp.arange(pool_size, dtype=jnp.int32)[None, :]
    return jnp.sum(jnp.where(hits, token_counts[None, :], 0), axis=1)


def local_activations(acts, act_basis, lengths):
    tok = acts.shape[1]
    positions = lax.axis_index("row") * tok + jnp.arange(tok, dtype=jnp.int32)
    live = (positions[None, :] < lengths[:, None]).astype(F32)
    rotated = jnp.einsum("ctd,dk->ctk", acts, act_basis, preferred_element_type=F32)
    return (rotated * live[:, :, None]).astype(BF16)


def final_kernel(counts, *refs):
    total = sum(counts)
    pieces = list(refs[:total])
    act_ref, eig_ref, query_ref, out_ref, score_ref = refs[total:]
    cands, queries = len(counts), query_ref.shape[0]
    damped = eig_ref[...] + DAMPING
    weights = [query_ref[q].astype(F32) / damped for q in range(queries)]
    rows = [[] for _ in range(queries)]
    for c in range(cands):
        tile, start = None, 0
        for _ in range(counts[c]):
            piece = pieces.pop(0)
            n = piece.shape[0]
            term = lax.dot_general(
                piece[...],
                act_ref[c, start : start + n],
                (((0,), (0,)), ((), ())),
                preferred_element_type=F32,
            )
            tile = term if tile is None else tile + term
            start += n
        out_ref[c] = tile
        for q in range(queries):
            rows[q].append(jnp.sum(weights[q] * tile, axis=0, keepdims=True))
    score_ref[0] = jnp.concatenate([r for one in rows for r in one], axis=0)


def rotate_and_score(pieces, act_rot, eigenvalues, query_rotated):
    counts = tuple(len(p) for p in pieces)
    flat = [x for p in pieces for x in p]
    cands, seq, width = act_rot.shape
    dirs = eigenvalues.shape[0]
    queries = query_rotated.shape[0]
    block = min(dirs, 256)
    steps = dirs // block
    rotated, partial_scores = pl.pallas_call(
        functools.partial(final_kernel, counts),
        grid=(steps,),
        in_specs=[pl.BlockSpec((x.shape[0], block), lambda i: (0, i)) for x in flat]
        + [
            pl.BlockSpec((cands, seq, width), lambda i: (0, 0, 0)),
            pl.BlockSpec((block, width), lambda i: (i, 0)),
            pl.BlockSpec((queries, block, width), lambda i: (0, i, 0)),
        ],
        out_specs=[
            pl.BlockSpec((cands, block, width), lambda i: (0, i, 0)),
            pl.BlockSpec((1, queries * cands, width), lambda i: (i, 0, 0)),
        ],
        out_shape=[
            jax.ShapeDtypeStruct((cands, dirs, width), F32),
            jax.ShapeDtypeStruct((steps, queries * cands, width), F32),
        ],
        compiler_params=pltpu.CompilerParams(vmem_limit_bytes=32 * 2**20),
    )(*flat, act_rot, eigenvalues, query_rotated)
    return rotated, jnp.sum(partial_scores, axis=(0, 2)).reshape(queries, cands)


def gather_body(acts, grads, act_basis, grad_basis, eigenvalues, query_rotated, example_ids, token_counts):
    lengths = candidate_lengths(example_ids, token_counts)
    local_act = local_activations(acts, act_basis, lengths)
    partial_value = jnp.einsum(
        "ctd,dj->ctj",
        lax.all_gather(grads, "row", axis=1, tiled=True),
        grad_basis,
        preferred_element_type=F32,
    )
    every_act = lax.all_gather(local_act, "row", axis=1, tiled=True)
    rotated_grads = lax.psum(partial_value, "col").astype(BF16)
    pieces = [[rotated_grads[c]] for c in range(acts.shape[0])]
    rotated, scores = rotate_and_score(pieces, every_act, eigenvalues, query_rotated)
    return rotated, lax.psum(scores, ("row", "col"))


def after(value, *earlier):
    return lax.optimization_barrier((value, *earlier))[0]


def project_kernel(count, *refs):
    tokens = refs[:count]
    own_ref, near_ref, far_ref, out_own, out_end, acc_own, acc_end = refs[count:]
    step = pl.program_id(0)

    @pl.when(step == 0)
    def _():
        acc_own[...] = jnp.zeros_like(acc_own)
        acc_end[...] = jnp.zeros_like(acc_end)

    rows = jnp.concatenate([t[...] for t in tokens], axis=0)
    half = near_ref.shape[1]
    acc_own[...] += jnp.dot(rows, own_ref[...], preferred_element_type=F32)
    acc_end[:, :half] += jnp.dot(rows, near_ref[...], preferred_element_type=F32)
    acc_end[:, half:] += jnp.dot(rows, far_ref[...], preferred_element_type=F32)

    @pl.when(step == pl.num_programs(0) - 1)
    def _():
        out_own[...] = acc_own[...].astype(BF16)
        out_end[...] = acc_end[...].astype(BF16)


def project(tokens, own, near, far):
    feats, dirs = own.shape
    block = 1024
    specs, total = [], 0
    for array, index in tokens:
        n = array.shape[-2]
        total += n
        if index is None:
            specs.append(pl.BlockSpec((n, block), lambda k: (0, k)))
        else:
            specs.append(pl.BlockSpec((None, n, block), lambda k, index=index: (index, 0, k)))
    half = near.shape[1]
    return pl.pallas_call(
        functools.partial(project_kernel, len(tokens)),
        grid=(feats // block,),
        in_specs=specs
        + [
            pl.BlockSpec((block, dirs), lambda k: (k, 0)),
            pl.BlockSpec((block, half), lambda k: (k, 0)),
            pl.BlockSpec((block, half), lambda k: (k, 0)),
        ],
        out_specs=[pl.BlockSpec((total, dirs), lambda k: (0, 0))] * 2,
        out_shape=[jax.ShapeDtypeStruct((total, dirs), BF16)] * 2,
        scratch_shapes=[pltpu.VMEM((total, dirs), F32)] * 2,
        compiler_params=pltpu.CompilerParams(vmem_limit_bytes=40 * 2**20),
        cost_estimate=pl.CostEstimate(
            flops=4 * total * feats * dirs,
            bytes_accessed=4 * feats * dirs + 2 * total * feats,
            transcendentals=0,
        ),
    )(*[array for array, _ in tokens], own, near, far)


def after(value, *earlier):
    return lax.optimization_barrier((value, *earlier))[0]


def exchange_sum(value, axis, size):
    total = value
    for d in range(1, size):
        total = total + lax.ppermute(value, axis, [(i, i ^ d) for i in range(size)])
    return total


def chain_body(acts, grads, act_basis, grad_basis, eigenvalues, query_rotated, example_ids, token_counts):
    cands, tok, feats = grads.shape
    dirs = grad_basis.shape[1]
    group, row = lax.axis_index("groups"), lax.axis_index("row")
    sides, planes, parts = 2, 4, 4
    inward = [(0, 1), (3, 2)]
    across = [(1, 2), (2, 1)]
    outward = [(1, 0), (2, 3)]
    swap = [(g * planes + r, (1 - g) * planes + r) for g in range(sides) for r in (1, 2)]
    at_end = (row == 0) | (row == planes - 1)

    lengths = candidate_lengths(example_ids, token_counts)
    local_act = local_activations(acts, act_basis, lengths)
    every_act = lax.all_gather(local_act, "row", axis=0)

    half = dirs // sides
    pieces = 8
    deep = feats // pieces
    half_cands = cands // 2
    other, near, far = [], [], []
    spans = [(0, 1), (1, 3), (3, 5), (5, 7), (7, 8)]
    for i, (a, b) in enumerate(spans):
        piece = lax.dynamic_slice(grad_basis, (a * deep, group * half), ((b - a) * deep, half))
        if i >= 2:
            piece = after(piece, near[i - 2], *other)
        near.append(lax.ppermute(piece, "row", inward))
        far.append(lax.ppermute(near[i], ("groups", "row"), swap))
        if i in (0, 2):
            part = grads[:half_cands] if i == 0 else grads[half_cands:]
            other.append(lax.ppermute(part if i == 0 else after(part, near[0]), "row", across))

    chunk = tok // 2
    started = list(near)
    first, second = [], []
    for c in range(cands):
        for s in range(0, tok, chunk):
            piece = after(grads[c, s : s + chunk], started[-2], *other)
            first.append(lax.ppermute(piece, "row", inward))
            started.append(first[-1])
            second.append(lax.ppermute(first[-1], "row", across))

    near_basis = jnp.concatenate(near, axis=0)
    far_basis = jnp.concatenate(far, axis=0)

    def reduce(tokens):
        own, end = project(tokens, grad_basis, near_basis, far_basis)
        back = lax.ppermute(end, "row", outward)
        swapped = jnp.concatenate([back[:, half:], back[:, :half]], axis=1)
        mine = jnp.where(at_end, jnp.where(group == 0, back, swapped), own)
        total = mine.astype(F32)
        for d in range(1, parts):
            total = total + lax.ppermute(mine, "col", [(i, i ^ d) for i in range(parts)]).astype(F32)
        return total.astype(BF16)

    pieces_of = []
    for c in range(cands):
        inner = reduce([(grads, c), (other[c // half_cands], c % half_cands)])
        pieces_of.append([inner])
    for c in range(cands):
        if c < cands - 1:
            k = 2 * c
            pieces_of[c].append(
                reduce([(first[k], None), (second[k], None), (first[k + 1], None), (second[k + 1], None)])
            )
        else:
            for k in (2 * c, 2 * c + 1):
                pieces_of[c].append(reduce([(first[k], None), (second[k], None)]))

    blocks = jnp.where(row < 2, every_act, every_act[::-1])
    order = [blocks[1], blocks[2]]
    for s in range(0, tok, chunk):
        order += [blocks[0][:, s : s + chunk], blocks[3][:, s : s + chunk]]
    act_rot = jnp.concatenate(order, axis=1)
    rotated, scores = rotate_and_score(pieces_of, act_rot, eigenvalues, query_rotated)
    scores = exchange_sum(exchange_sum(scores, "col", parts), "row", planes)
    return rotated, scores


def solution(mesh):
    placed = (
        P("groups", "row", None),
        P("groups", "row", "col"),
        P(None, "col"),
        P("col", "row"),
        P("row", "col"),
        P(None, "row", "col"),
        P("groups"),
        P(),
    )
    chain = mesh.shape["groups"] == 2 and mesh.shape["row"] == 4 and mesh.shape["col"] == 4
    return jax.shard_map(
        chain_body if chain else gather_body,
        mesh=mesh,
        in_specs=placed,
        out_specs=(P("groups", "row", "col"), P(None, "groups")),
        check_vma=False,
    )
```

```python
import functools

import jax
import jax.numpy as jnp
from jax import lax
from jax.experimental import pallas as pl
from jax.experimental.pallas import tpu as pltpu
from jax.sharding import PartitionSpec as P

DAMPING = 0.05
BF16 = jnp.bfloat16
F32 = jnp.float32


def candidate_lengths(example_ids, token_counts):
    pool_size = token_counts.shape[0]
    hits = example_ids[:, None] == jnp.arange(pool_size, dtype=jnp.int32)[None, :]
    return jnp.sum(jnp.where(hits, token_counts[None, :], 0), axis=1)


def local_activations(acts, act_basis, lengths):
    tok = acts.shape[1]
    positions = lax.axis_index("row") * tok + jnp.arange(tok, dtype=jnp.int32)
    live = (positions[None, :] < lengths[:, None]).astype(F32)
    rotated = jnp.einsum("ctd,dk->ctk", acts, act_basis, preferred_element_type=F32)
    return (rotated * live[:, :, None]).astype(BF16)


def final_kernel(counts, *refs):
    total = sum(counts)
    pieces = list(refs[:total])
    act_ref, eig_ref, query_ref, out_ref, score_ref = refs[total:]
    cands, queries = len(counts), query_ref.shape[0]
    damped = eig_ref[...] + DAMPING
    weights = [query_ref[q].astype(F32) / damped for q in range(queries)]
    rows = [[] for _ in range(queries)]
    for c in range(cands):
        tile, start = None, 0
        for _ in range(counts[c]):
            piece = pieces.pop(0)
            n = piece.shape[0]
            term = lax.dot_general(
                piece[...],
                act_ref[c, start : start + n],
                (((0,), (0,)), ((), ())),
                preferred_element_type=F32,
            )
            tile = term if tile is None else tile + term
            start += n
        out_ref[c] = tile
        for q in range(queries):
            rows[q].append(jnp.sum(weights[q] * tile, axis=0, keepdims=True))
    score_ref[0] = jnp.concatenate([r for one in rows for r in one], axis=0)


def rotate_and_score(pieces, act_rot, eigenvalues, query_rotated):
    counts = tuple(len(p) for p in pieces)
    flat = [x for p in pieces for x in p]
    cands, seq, width = act_rot.shape
    dirs = eigenvalues.shape[0]
    queries = query_rotated.shape[0]
    block = min(dirs, 256)
    steps = dirs // block
    rotated, partial_scores = pl.pallas_call(
        functools.partial(final_kernel, counts),
        grid=(steps,),
        in_specs=[pl.BlockSpec((x.shape[0], block), lambda i: (0, i)) for x in flat]
        + [
            pl.BlockSpec((cands, seq, width), lambda i: (0, 0, 0)),
            pl.BlockSpec((block, width), lambda i: (i, 0)),
            pl.BlockSpec((queries, block, width), lambda i: (0, i, 0)),
        ],
        out_specs=[
            pl.BlockSpec((cands, block, width), lambda i: (0, i, 0)),
            pl.BlockSpec((1, queries * cands, width), lambda i: (i, 0, 0)),
        ],
        out_shape=[
            jax.ShapeDtypeStruct((cands, dirs, width), F32),
            jax.ShapeDtypeStruct((steps, queries * cands, width), F32),
        ],
        compiler_params=pltpu.CompilerParams(vmem_limit_bytes=32 * 2**20),
    )(*flat, act_rot, eigenvalues, query_rotated)
    return rotated, jnp.sum(partial_scores, axis=(0, 2)).reshape(queries, cands)


def gather_body(acts, grads, act_basis, grad_basis, eigenvalues, query_rotated, example_ids, token_counts):
    lengths = candidate_lengths(example_ids, token_counts)
    local_act = local_activations(acts, act_basis, lengths)
    partial_value = jnp.einsum(
        "ctd,dj->ctj",
        lax.all_gather(grads, "row", axis=1, tiled=True),
        grad_basis,
        preferred_element_type=F32,
    )
    every_act = lax.all_gather(local_act, "row", axis=1, tiled=True)
    rotated_grads = lax.psum(partial_value, "col").astype(BF16)
    pieces = [[rotated_grads[c]] for c in range(acts.shape[0])]
    rotated, scores = rotate_and_score(pieces, every_act, eigenvalues, query_rotated)
    return rotated, lax.psum(scores, ("row", "col"))


def after(value, *earlier):
    return lax.optimization_barrier((value, *earlier))[0]


def assemble_kernel(bounds, group_ref, *refs):
    count = len(bounds)
    near, far, out, sems = refs[:count], refs[count : 2 * count], refs[2 * count], refs[2 * count + 1]
    half = near[0].shape[1]
    group = group_ref[0]
    copies = []
    for i, (a, b) in enumerate(bounds):
        for j, (ref, place) in enumerate(((near[i], group), (far[i], 1 - group))):
            columns = pl.ds(pl.multiple_of(place * half, half), half)
            copies.append(pltpu.make_async_copy(ref, out.at[pl.ds(a, b - a), columns], sems.at[i, j]))
    for copy in copies:
        copy.start()
    for copy in copies:
        copy.wait()


def assemble(near, far, group):
    bounds, start = [], 0
    for x in near:
        bounds.append((start, start + x.shape[0]))
        start += x.shape[0]
    return pl.pallas_call(
        functools.partial(assemble_kernel, tuple(bounds)),
        in_specs=[pl.BlockSpec(memory_space=pltpu.SMEM)]
        + [pl.BlockSpec(memory_space=pl.ANY)] * (2 * len(near)),
        out_specs=pl.BlockSpec(memory_space=pl.ANY),
        out_shape=jax.ShapeDtypeStruct((start, 2 * near[0].shape[1]), BF16),
        scratch_shapes=[pltpu.SemaphoreType.DMA((len(near), 2))],
        compiler_params=pltpu.CompilerParams(vmem_limit_bytes=32 * 2**20),
        cost_estimate=pl.CostEstimate(
            flops=0, bytes_accessed=start * near[0].shape[1], transcendentals=0
        ),
    )(group.reshape(1), *near, *far)


def project_kernel(count, bases, *refs):
    tokens = refs[:count]
    basis = refs[count : count + bases]
    outs = refs[count + bases : count + 2 * bases]
    accs = refs[count + 2 * bases :]
    step = pl.program_id(0)
    rows = jnp.concatenate([t[...] for t in tokens], axis=0) if count > 1 else tokens[0][...]
    for ref, out, acc in zip(basis, outs, accs):
        term = jnp.dot(rows, ref[...], preferred_element_type=F32)

        @pl.when(step == 0)
        def _(term=term, acc=acc):
            acc[...] = term

        @pl.when(step > 0)
        def _(term=term, acc=acc):
            acc[...] += term

        @pl.when(step == pl.num_programs(0) - 1)
        def _(out=out, acc=acc):
            out[...] = acc[...].astype(BF16)


def project(tokens, bases):
    feats, dirs = bases[0].shape
    block = 1024
    specs, total = [], 0
    for array, index in tokens:
        n = array.shape[-2]
        total += n
        if index is None:
            specs.append(pl.BlockSpec((n, block), lambda k: (0, k)))
        else:
            specs.append(pl.BlockSpec((None, n, block), lambda k, index=index: (index, 0, k)))
    count = len(bases)
    return pl.pallas_call(
        functools.partial(project_kernel, len(tokens), count),
        grid=(feats // block,),
        in_specs=specs + [pl.BlockSpec((block, dirs), lambda k: (k, 0))] * count,
        out_specs=[pl.BlockSpec((total, dirs), lambda k: (0, 0))] * count,
        out_shape=[jax.ShapeDtypeStruct((total, dirs), BF16)] * count,
        scratch_shapes=[pltpu.VMEM((total, dirs), F32)] * count,
        compiler_params=pltpu.CompilerParams(vmem_limit_bytes=40 * 2**20),
        cost_estimate=pl.CostEstimate(
            flops=count * total * feats * dirs // 16,
            bytes_accessed=(count * feats * dirs + total * feats) // 16,
            transcendentals=0,
        ),
    )(*[array for array, _ in tokens], *bases)


def after(value, *earlier):
    return lax.optimization_barrier((value, *earlier))[0]


def exchange_sum(value, axis, size):
    total = value
    for d in range(1, size):
        total = total + lax.ppermute(value, axis, [(i, i ^ d) for i in range(size)])
    return total


def chain_body(acts, grads, act_basis, grad_basis, eigenvalues, query_rotated, example_ids, token_counts):
    cands, tok, feats = grads.shape
    dirs = grad_basis.shape[1]
    group, row = lax.axis_index("groups"), lax.axis_index("row")
    sides, planes, parts = 2, 4, 4
    inward = [(0, 1), (3, 2)]
    across = [(1, 2), (2, 1)]
    outward = [(1, 0), (2, 3)]
    swap = [(g * planes + r, (1 - g) * planes + r) for g in range(sides) for r in (1, 2)]
    at_end = (row == 0) | (row == planes - 1)

    lengths = candidate_lengths(example_ids, token_counts)
    local_act = local_activations(acts, act_basis, lengths)
    every_act = lax.all_gather(local_act, "row", axis=0)

    half = dirs // sides
    flat = grads.reshape(cands * tok, feats)
    units, deep, slab = 8, feats // 8, cands * tok // 8
    near, far, other = [], [], []
    own_own, = project([(flat, None)], [grad_basis])
    for i, (a, b) in enumerate([(0, 1), (1, 3), (3, 5), (5, 7), (7, units)]):
        piece = lax.dynamic_slice(grad_basis, (a * deep, group * half), ((b - a) * deep, half))
        tokens = flat[a * slab : b * slab]
        if i >= 2:
            tie = [near[i - 2], other[i - 2]] + ([own_own, local_act] if i == 2 else [])
            piece, tokens = after(piece, *tie), after(tokens, *tie)
        other.append(lax.ppermute(tokens, "row", across))
        near.append(lax.ppermute(piece, "row", inward))
        far.append(lax.ppermute(near[i], ("groups", "row"), swap))

    chunk = tok // 2
    halves = [(c, s) for c in range(cands) for s in range(0, tok, chunk)]
    first, second, ties = [], [], {}
    ties[0] = [near[3], far[1], other[3]]
    ties[1] = [near[4], far[2], other[4]]
    ties[2] = [far[3]]
    ties[3] = [far[4]]
    end_basis = assemble(near, far, group)
    outer = []
    for k, (c, s) in enumerate(halves):
        tie = ties.get(k, [])
        if k >= 2:
            tie = tie + [first[k - 2]]
        if k >= 3:
            tie = tie + [second[k - 3]]
        first.append(lax.ppermute(after(grads[c, s : s + chunk], *tie), "row", inward))
        second.append(lax.ppermute(first[k], "row", across))
        if k == 0:
            other_own, = project([(x, None) for x in other], [after(grad_basis, first[0])])
            ties[3].append(other_own)
        if k == 1:
            own_end, = project([(flat, None)], [after(end_basis, first[1], other_own)])
            ties[4] = [own_end]
        if k == 2:
            other_end, = project([(x, None) for x in other], [after(end_basis, first[2], own_end)])
            ties[5] = [other_end]
        if k in (4, 5, 7):
            i = 2 * len(outer)
            last = outer[-1][0] if outer else other_end
            sources = [(x, None) for x in (first[i], second[i], first[i + 1], second[i + 1])]
            outer.append(project(sources, [grad_basis, after(end_basis, *first[k - 1 :], last)]))
            ties[k + 3] = [outer[-1][0]]
    sources = [(x, None) for x in (first[6], second[6], first[7], second[7])]
    outer.append(project(sources, [grad_basis, end_basis]))

    def settle(own, end):
        return jnp.where(at_end, lax.ppermute(end, "row", outward), own)

    def gather(own, end):
        every = lax.all_gather(settle(own, end), "col", axis=0)
        return jnp.sum(every.astype(F32), axis=0).astype(BF16)

    def exchange(own, end):
        mine = settle(own, end)
        total = mine.astype(F32)
        for d in range(1, parts):
            total = total + lax.ppermute(mine, "col", [(i, i ^ d) for i in range(parts)]).astype(F32)
        return total.astype(BF16)

    own_sum = gather(own_own, own_end)
    other_sum = gather(other_own, other_end)
    pieces_of = [[own_sum[c * tok : (c + 1) * tok], other_sum[c * tok : (c + 1) * tok]] for c in range(cands)]
    for c, products in enumerate(outer):
        pieces_of[c].append(gather(*products) if c < cands - 1 else exchange(*products))

    blocks = jnp.where(row < 2, every_act, every_act[::-1])
    order = [blocks[1], blocks[2]]
    for s in range(0, tok, chunk):
        order += [blocks[0][:, s : s + chunk], blocks[3][:, s : s + chunk]]
    act_rot = jnp.concatenate(order, axis=1)
    rotated, scores = rotate_and_score(pieces_of, act_rot, eigenvalues, query_rotated)
    scores = exchange_sum(exchange_sum(scores, "col", parts), "row", planes)
    return rotated, scores


def solution(mesh):
    placed = (
        P("groups", "row", None),
        P("groups", "row", "col"),
        P(None, "col"),
        P("col", "row"),
        P("row", "col"),
        P(None, "row", "col"),
        P("groups"),
        P(),
    )
    chain = mesh.shape["groups"] == 2 and mesh.shape["row"] == 4 and mesh.shape["col"] == 4
    return jax.shard_map(
        chain_body if chain else gather_body,
        mesh=mesh,
        in_specs=placed,
        out_specs=(P("groups", "row", "col"), P(None, "groups")),
        check_vma=False,
    )
```

```python
import functools

import jax
import jax.numpy as jnp
from jax import lax
from jax.experimental import pallas as pl
from jax.experimental.pallas import tpu as pltpu
from jax.sharding import PartitionSpec as P

DAMPING = 0.05
BF16 = jnp.bfloat16
F32 = jnp.float32


def candidate_lengths(example_ids, token_counts):
    pool_size = token_counts.shape[0]
    hits = example_ids[:, None] == jnp.arange(pool_size, dtype=jnp.int32)[None, :]
    return jnp.sum(jnp.where(hits, token_counts[None, :], 0), axis=1)


def local_activations(acts, act_basis, lengths):
    tok = acts.shape[1]
    positions = lax.axis_index("row") * tok + jnp.arange(tok, dtype=jnp.int32)
    live = (positions[None, :] < lengths[:, None]).astype(F32)
    rotated = jnp.einsum("ctd,dk->ctk", acts, act_basis, preferred_element_type=F32)
    return (rotated * live[:, :, None]).astype(BF16)


def final_kernel(counts, *refs):
    total = sum(counts)
    pieces = list(refs[:total])
    act_ref, eig_ref, query_ref, out_ref, score_ref = refs[total:]
    cands, queries = len(counts), query_ref.shape[0]
    damped = eig_ref[...] + DAMPING
    weights = [query_ref[q].astype(F32) / damped for q in range(queries)]
    rows = [[] for _ in range(queries)]
    for c in range(cands):
        tile, start = None, 0
        for _ in range(counts[c]):
            piece = pieces.pop(0)
            n = piece.shape[0]
            term = lax.dot_general(
                piece[...],
                act_ref[c, start : start + n],
                (((0,), (0,)), ((), ())),
                preferred_element_type=F32,
            )
            tile = term if tile is None else tile + term
            start += n
        out_ref[c] = tile
        for q in range(queries):
            rows[q].append(jnp.sum(weights[q] * tile, axis=0, keepdims=True))
    score_ref[0] = jnp.concatenate([r for one in rows for r in one], axis=0)


def rotate_and_score(pieces, act_rot, eigenvalues, query_rotated):
    counts = tuple(len(p) for p in pieces)
    flat = [x for p in pieces for x in p]
    cands, seq, width = act_rot.shape
    dirs = eigenvalues.shape[0]
    queries = query_rotated.shape[0]
    block = min(dirs, 256)
    steps = dirs // block
    rotated, partial_scores = pl.pallas_call(
        functools.partial(final_kernel, counts),
        grid=(steps,),
        in_specs=[pl.BlockSpec((x.shape[0], block), lambda i: (0, i)) for x in flat]
        + [
            pl.BlockSpec((cands, seq, width), lambda i: (0, 0, 0)),
            pl.BlockSpec((block, width), lambda i: (i, 0)),
            pl.BlockSpec((queries, block, width), lambda i: (0, i, 0)),
        ],
        out_specs=[
            pl.BlockSpec((cands, block, width), lambda i: (0, i, 0)),
            pl.BlockSpec((1, queries * cands, width), lambda i: (i, 0, 0)),
        ],
        out_shape=[
            jax.ShapeDtypeStruct((cands, dirs, width), F32),
            jax.ShapeDtypeStruct((steps, queries * cands, width), F32),
        ],
        compiler_params=pltpu.CompilerParams(vmem_limit_bytes=32 * 2**20),
    )(*flat, act_rot, eigenvalues, query_rotated)
    return rotated, jnp.sum(partial_scores, axis=(0, 2)).reshape(queries, cands)


def gather_body(acts, grads, act_basis, grad_basis, eigenvalues, query_rotated, example_ids, token_counts):
    lengths = candidate_lengths(example_ids, token_counts)
    local_act = local_activations(acts, act_basis, lengths)
    partial_value = jnp.einsum(
        "ctd,dj->ctj",
        lax.all_gather(grads, "row", axis=1, tiled=True),
        grad_basis,
        preferred_element_type=F32,
    )
    every_act = lax.all_gather(local_act, "row", axis=1, tiled=True)
    rotated_grads = lax.psum(partial_value, "col").astype(BF16)
    pieces = [[rotated_grads[c]] for c in range(acts.shape[0])]
    rotated, scores = rotate_and_score(pieces, every_act, eigenvalues, query_rotated)
    return rotated, lax.psum(scores, ("row", "col"))


def after(value, *earlier):
    return lax.optimization_barrier((value, *earlier))[0]


def project_kernel(count, widths, *refs):
    flags, refs = refs[0], refs[1:]
    tokens, basis, out, acc = refs[:count], refs[count:-2], refs[-2], refs[-1]
    step = pl.program_id(0)
    rows = tokens[0][...]
    if count == 2:
        rows = jnp.where(flags[0] == 1, rows, tokens[1][...])
    start, spans = 0, []
    for width in widths:
        spans.append((start, start + width))
        start += width

    @pl.when(step == 0)
    def _():
        acc[...] = jnp.zeros_like(acc)

    for ref, (a, b) in zip(basis, spans):
        acc[:, a:b] += jnp.dot(rows, ref[...], preferred_element_type=F32)

    @pl.when(step == pl.num_programs(0) - 1)
    def _():
        if len(basis) == 1:
            out[...] = acc[...].astype(BF16)
        else:
            (c, d), (e, f) = spans[-2:]
            if c > 0:
                out[:, :c] = acc[:, :c].astype(BF16)

            @pl.when(flags[1] == 0)
            def _():
                out[:, c:f] = acc[:, c:f].astype(BF16)

            @pl.when(flags[1] != 0)
            def _():
                out[:, c:d] = acc[:, e:f].astype(BF16)
                out[:, e:f] = acc[:, c:d].astype(BF16)


def project(flags, tokens, bases):
    feats = bases[0].shape[0]
    widths = tuple(x.shape[1] for x in bases)
    block, total = 1024, sum(widths)
    rows = tokens[0][2]
    specs = [
        pl.BlockSpec((rows, block), lambda k, i=start // rows: (i, k)) for _, start, _ in tokens
    ]
    return pl.pallas_call(
        functools.partial(project_kernel, len(tokens), widths),
        grid=(feats // block,),
        in_specs=[pl.BlockSpec(memory_space=pltpu.SMEM)]
        + specs
        + [pl.BlockSpec((block, w), lambda k: (k, 0)) for w in widths],
        out_specs=pl.BlockSpec((rows, total), lambda k: (0, 0)),
        out_shape=jax.ShapeDtypeStruct((rows, total), BF16),
        scratch_shapes=[pltpu.VMEM((rows, total), F32)],
        compiler_params=pltpu.CompilerParams(vmem_limit_bytes=40 * 2**20),
        cost_estimate=pl.CostEstimate(
            flops=rows * feats * total // 8,
            bytes_accessed=feats * (total + rows) // 8,
            transcendentals=0,
        ),
    )(flags, *[array for array, _, _ in tokens], *bases)


def after(value, *earlier):
    return lax.optimization_barrier((value, *earlier))[0]


def exchange_sum(value, axis, size):
    total = value
    for d in range(1, size):
        total = total + lax.ppermute(value, axis, [(i, i ^ d) for i in range(size)])
    return total


def chain_body(acts, grads, act_basis, grad_basis, eigenvalues, query_rotated, example_ids, token_counts):
    cands, tok, feats = grads.shape
    dirs = grad_basis.shape[1]
    group, row, col = (lax.axis_index(a) for a in ("groups", "row", "col"))
    sides, planes, parts = 2, 4, 4
    middle, ends = [(1, 2), (2, 1)], [(0, 3), (3, 0)]
    beside = [(i, i ^ 1) for i in range(planes)]
    at_end = (row == 0) | (row == planes - 1)
    flags = jnp.stack([at_end.astype(jnp.int32), group.astype(jnp.int32)])

    lengths = candidate_lengths(example_ids, token_counts)
    local_act = local_activations(acts, act_basis, lengths)
    every_act = lax.all_gather(local_act, "row", axis=0)

    half, flat = dirs // sides, grads.reshape(cands * tok, feats)
    units, deep = 8, feats // 8
    near, far, other = [], [], []
    own_own = project(flags, [(flat, 0, cands * tok)], [grad_basis])
    for i, (a, b) in enumerate([(0, 1), (1, 3), (3, 5), (5, 7), (7, units)]):
        piece = lax.dynamic_slice(grad_basis, (a * deep, group * half), ((b - a) * deep, half))
        if i >= 2:
            piece = after(piece, near[i - 2], *([own_own, local_act] if i == 2 else []))
        if i in (0, 2):
            part = flat[: cands * tok // 2] if i == 0 else after(flat[cands * tok // 2 :], near[0])
            other.append(lax.ppermute(part, "row", middle))
        near.append(lax.ppermute(piece, "row", beside))
        far.append(lax.ppermute(near[i], "groups", [(0, 1), (1, 0)]))
    near_basis = jnp.concatenate(near, axis=0)
    far_basis = jnp.concatenate(far, axis=0)

    spans = [(c * tok, tok) for c in range(cands - 1)]
    spans += [((cands - 1) * tok + s, tok // 2) for s in (0, tok // 2)]
    ties = {0: [near[3], far[1], other[0]], 1: [near[4], far[2], other[1]], 2: [far[4]]}
    partner, products = [], []
    for k, (start, n) in enumerate(spans):
        tie = ties.get(k, []) + ([partner[k - 2]] if k >= 2 else [])
        partner.append(lax.ppermute(after(flat[start : start + n], *tie), "row", ends))
        if k == 0:
            own_end = project(flags, [(flat, 0, cands * tok)], [near_basis, after(far_basis, partner[0])])
            ties[3] = [own_end]
        inner = other[2 * start // (cands * tok)]
        products.append(
            project(
                flags,
                [(partner[k], 0, n), (inner, start % (cands * tok // 2), n)],
                [grad_basis, near_basis, far_basis],
            )
        )
        ties[k + 3] = ties.get(k + 3, []) + [products[k]]

    def scatter_sum(value):
        value = value.reshape(parts, -1, 2 * dirs)
        total = lax.dynamic_index_in_dim(value, col, 0, keepdims=False).astype(F32)
        for d in range(1, parts):
            sent = lax.dynamic_index_in_dim(value, col ^ d, 0, keepdims=False)
            total = total + lax.ppermute(sent, "col", [(i, i ^ d) for i in range(parts)]).astype(F32)
        total = total.astype(BF16)
        return jnp.stack([total[:, :dirs], lax.ppermute(total[:, dirs:], "row", beside)])

    act = [
        lax.dynamic_index_in_dim(every_act, i, 0, keepdims=False)
        for i in (row, row ^ 1, planes - 1 - row, planes - 1 - (row ^ 1))
    ]
    pieces, act_order = [[] for _ in range(cands)], [[] for _ in range(cands)]
    own = lax.all_gather(scatter_sum(jnp.concatenate([own_own, own_end], axis=1)), "col", axis=0)
    for c in range(cands):
        pieces[c].append(own[c].reshape(2 * tok, dirs))
        act_order[c] += [act[0][c], act[1][c]]
    for k, (start, n) in enumerate(spans):
        c, s = start // tok, start % tok
        mine = scatter_sum(products[k])
        tokens = jnp.stack([x[c, s : s + n].reshape(parts, n // parts, -1) for x in act[2:]], axis=1)
        if k < len(spans) - 1:
            every = lax.all_gather(mine, "col", axis=0)
            pieces[c].append(every.reshape(2 * n, dirs))
            act_order[c].append(tokens.reshape(2 * n, -1))
        else:
            for d in range(parts):
                got = lax.ppermute(mine, "col", [(i, i ^ d) for i in range(parts)]) if d else mine
                pieces[c].append(got.reshape(2 * n // parts, dirs))
                sub = lax.dynamic_index_in_dim(tokens, col ^ d, 0, keepdims=False)
                act_order[c].append(sub.reshape(2 * n // parts, -1))
    act_rot = jnp.stack([jnp.concatenate(x, axis=0) for x in act_order])
    rotated, scores = rotate_and_score(pieces, act_rot, eigenvalues, query_rotated)
    scores = exchange_sum(exchange_sum(scores, "col", parts), "row", planes)
    return rotated, scores


def solution(mesh):
    placed = (
        P("groups", "row", None),
        P("groups", "row", "col"),
        P(None, "col"),
        P("col", "row"),
        P("row", "col"),
        P(None, "row", "col"),
        P("groups"),
        P(),
    )
    chain = mesh.shape["groups"] == 2 and mesh.shape["row"] == 4 and mesh.shape["col"] == 4
    return jax.shard_map(
        chain_body if chain else gather_body,
        mesh=mesh,
        in_specs=placed,
        out_specs=(P("groups", "row", "col"), P(None, "groups")),
        check_vma=False,
    )
```

```python
import functools

import jax
import jax.numpy as jnp
from jax import lax
from jax.experimental import pallas as pl
from jax.experimental.pallas import tpu as pltpu
from jax.sharding import PartitionSpec as P

DAMPING = 0.05
BF16 = jnp.bfloat16
F32 = jnp.float32


def candidate_lengths(example_ids, token_counts):
    pool_size = token_counts.shape[0]
    hits = example_ids[:, None] == jnp.arange(pool_size, dtype=jnp.int32)[None, :]
    return jnp.sum(jnp.where(hits, token_counts[None, :], 0), axis=1)


def local_activations(acts, act_basis, lengths):
    tok = acts.shape[1]
    positions = lax.axis_index("row") * tok + jnp.arange(tok, dtype=jnp.int32)
    live = (positions[None, :] < lengths[:, None]).astype(F32)
    rotated = jnp.einsum("ctd,dk->ctk", acts, act_basis, preferred_element_type=F32)
    return (rotated * live[:, :, None]).astype(BF16)


def final_kernel(layout, count, *refs):
    arrays = refs[:count]
    act_ref, eig_ref, query_ref, out_ref, score_ref = refs[count:]
    queries = query_ref.shape[0]
    damped = eig_ref[...] + DAMPING
    weights = [query_ref[q].astype(F32) / damped for q in range(queries)]
    rows = [[] for _ in range(queries)]
    for c, segments in enumerate(layout):
        tokens = jnp.concatenate([arrays[i][s : s + n] for i, s, n in segments], axis=0)
        tile = lax.dot_general(
            tokens, act_ref[c], (((0,), (0,)), ((), ())), preferred_element_type=F32
        )
        out_ref[c] = tile
        for q in range(queries):
            rows[q].append(jnp.sum(weights[q] * tile, axis=0, keepdims=True))
    score_ref[0] = jnp.concatenate([r for one in rows for r in one], axis=0)


def rotate_and_score(arrays, layout, act_rot, eigenvalues, query_rotated):
    cands, seq, width = act_rot.shape
    dirs = eigenvalues.shape[0]
    queries = query_rotated.shape[0]
    block = min(dirs, 256)
    steps = dirs // block
    rotated, partial_scores = pl.pallas_call(
        functools.partial(final_kernel, layout, len(arrays)),
        grid=(steps,),
        in_specs=[pl.BlockSpec((x.shape[0], block), lambda i: (0, i)) for x in arrays]
        + [
            pl.BlockSpec((cands, seq, width), lambda i: (0, 0, 0)),
            pl.BlockSpec((block, width), lambda i: (i, 0)),
            pl.BlockSpec((queries, block, width), lambda i: (0, i, 0)),
        ],
        out_specs=[
            pl.BlockSpec((cands, block, width), lambda i: (0, i, 0)),
            pl.BlockSpec((1, queries * cands, width), lambda i: (i, 0, 0)),
        ],
        out_shape=[
            jax.ShapeDtypeStruct((cands, dirs, width), F32),
            jax.ShapeDtypeStruct((steps, queries * cands, width), F32),
        ],
        compiler_params=pltpu.CompilerParams(vmem_limit_bytes=32 * 2**20),
    )(*arrays, act_rot, eigenvalues, query_rotated)
    return rotated, jnp.sum(partial_scores, axis=(0, 2)).reshape(queries, cands)


def gather_body(acts, grads, act_basis, grad_basis, eigenvalues, query_rotated, example_ids, token_counts):
    lengths = candidate_lengths(example_ids, token_counts)
    local_act = local_activations(acts, act_basis, lengths)
    partial_value = jnp.einsum(
        "ctd,dj->ctj",
        lax.all_gather(grads, "row", axis=1, tiled=True),
        grad_basis,
        preferred_element_type=F32,
    )
    every_act = lax.all_gather(local_act, "row", axis=1, tiled=True)
    rotated_grads = lax.psum(partial_value, "col").astype(BF16)
    cands, seq = rotated_grads.shape[:2]
    arrays = [rotated_grads[c] for c in range(cands)]
    layout = tuple(((c, 0, seq),) for c in range(cands))
    rotated, scores = rotate_and_score(arrays, layout, every_act, eigenvalues, query_rotated)
    return rotated, lax.psum(scores, ("row", "col"))


def after(value, *earlier):
    return lax.optimization_barrier((value, *earlier))[0]


def project_kernel(count, widths, *refs):
    flags, refs = refs[0], refs[1:]
    tokens, basis, out, acc = refs[:count], refs[count:-2], refs[-2], refs[-1]
    step = pl.program_id(0)
    rows = [t[...] for t in tokens]
    if count > 1:
        joined = jnp.concatenate(rows[:-1], axis=0) if count > 2 else rows[0]
        rows = [jnp.where(flags[0] == 1, joined, rows[-1])]
    rows = rows[0]
    start, spans = 0, []
    for width in widths:
        spans.append((start, start + width))
        start += width

    @pl.when(step == 0)
    def _():
        acc[...] = jnp.zeros_like(acc)

    for ref, (a, b) in zip(basis, spans):
        acc[:, a:b] += jnp.dot(rows, ref[...], preferred_element_type=F32)

    @pl.when(step == pl.num_programs(0) - 1)
    def _():
        if len(basis) == 1:
            out[...] = acc[...].astype(BF16)
        else:
            (c, d), (e, f) = spans[-2:]
            if c > 0:
                out[:, :c] = acc[:, :c].astype(BF16)

            @pl.when(flags[1] == 0)
            def _():
                out[:, c:f] = acc[:, c:f].astype(BF16)

            @pl.when(flags[1] != 0)
            def _():
                out[:, c:d] = acc[:, e:f].astype(BF16)
                out[:, e:f] = acc[:, c:d].astype(BF16)


def project(flags, tokens, bases):
    feats = bases[0].shape[0]
    widths = tuple(x.shape[1] for x in bases)
    block, total = 1024, sum(widths)
    rows = tokens[-1][2]
    specs = []
    for _, start, n in tokens:
        assert start % n == 0
        specs.append(pl.BlockSpec((n, block), lambda k, i=start // n: (i, k)))
    return pl.pallas_call(
        functools.partial(project_kernel, len(tokens), widths),
        grid=(feats // block,),
        in_specs=[pl.BlockSpec(memory_space=pltpu.SMEM)]
        + specs
        + [pl.BlockSpec((block, w), lambda k: (k, 0)) for w in widths],
        out_specs=pl.BlockSpec((rows, total), lambda k: (0, 0)),
        out_shape=jax.ShapeDtypeStruct((rows, total), BF16),
        scratch_shapes=[pltpu.VMEM((rows, total), F32)],
        compiler_params=pltpu.CompilerParams(vmem_limit_bytes=40 * 2**20),
        cost_estimate=pl.CostEstimate(
            flops=rows * feats * total // 8,
            bytes_accessed=feats * (total + rows) // 8,
            transcendentals=0,
        ),
    )(flags, *[array for array, _, _ in tokens], *bases)


def after(value, *earlier):
    return lax.optimization_barrier((value, *earlier))[0]


def exchange_sum(value, axis, size):
    total = value
    for d in range(1, size):
        total = total + lax.ppermute(value, axis, [(i, i ^ d) for i in range(size)])
    return total


def chain_body(acts, grads, act_basis, grad_basis, eigenvalues, query_rotated, example_ids, token_counts):
    cands, tok, feats = grads.shape
    dirs = grad_basis.shape[1]
    group, row, col = (lax.axis_index(a) for a in ("groups", "row", "col"))
    sides, planes, parts = 2, 4, 4
    middle, ends = [(1, 2), (2, 1)], [(0, 3), (3, 0)]
    beside = [(i, i ^ 1) for i in range(planes)]
    at_end = (row == 0) | (row == planes - 1)
    flags = jnp.stack([at_end.astype(jnp.int32), group.astype(jnp.int32)])

    lengths = candidate_lengths(example_ids, token_counts)
    local_act = local_activations(acts, act_basis, lengths)
    every_act = lax.all_gather(local_act, "row", axis=0)

    half, flat = dirs // sides, grads.reshape(cands * tok, feats)
    units, deep, slab = 8, feats // 8, cands * tok // 8
    near, far, other = [], [], []
    spans = [(0, 1), (1, 3), (3, 5), (5, 7), (7, units)]
    batches = [(0, 1), (2,), (3, 4)]
    ranges = [(spans[x[0]][0] * slab, spans[x[-1]][1] * slab) for x in batches]
    own_own = project(flags, [(flat, 0, cands * tok)], [grad_basis])
    for i, (a, b) in enumerate(spans):
        piece = lax.dynamic_slice(grad_basis, (a * deep, group * half), ((b - a) * deep, half))
        if i >= 2:
            early = [own_own, local_act] if i == 2 else [other[i - 3]]
            piece = after(piece, near[i - 2], *early)
        if i < len(ranges):
            rows = flat[slice(*ranges[i])]
            other.append(lax.ppermute(after(rows, near[i - 1]) if i else rows, "row", middle))
        near.append(lax.ppermute(piece, "row", beside))
        far.append(lax.ppermute(near[i], "groups", [(0, 1), (1, 0)]))
    near_basis = jnp.concatenate(near, axis=0)
    far_basis = jnp.concatenate(far, axis=0)

    ties = {0: [near[3], far[1]], 1: [near[3], far[2]], 2: [near[4], other[2]]}
    partner = []
    for k, (a, b) in enumerate(spans):
        tie = ties.get(k, []) + ([partner[k - 2]] if k >= 2 else [])
        piece = flat[a * slab : b * slab]
        partner.append(lax.ppermute(after(piece, *tie), "row", ends))
    own_end = project(flags, [(flat, 0, cands * tok)], [near_basis, after(far_basis, partner[0])])
    products = []
    for batch, inner, (first, last) in zip(batches, other, ranges):
        tokens = [(partner[k], 0, (spans[k][1] - spans[k][0]) * slab) for k in batch]
        tokens.append((inner, 0, last - first))
        products.append(project(flags, tokens, [grad_basis, near_basis, far_basis]))

    def scatter_sum(value):
        value = value.reshape(parts, -1, 2 * dirs)
        total = lax.dynamic_index_in_dim(value, col, 0, keepdims=False).astype(F32)
        for d in range(1, parts):
            sent = lax.dynamic_index_in_dim(value, col ^ d, 0, keepdims=False)
            total = total + lax.ppermute(sent, "col", [(i, i ^ d) for i in range(parts)]).astype(F32)
        total = total.astype(BF16)
        return jnp.stack([total[:, :dirs], lax.ppermute(total[:, dirs:], "row", beside)])

    act = [
        lax.dynamic_index_in_dim(every_act, i, 0, keepdims=False)
        for i in (row, row ^ 1, planes - 1 - row, planes - 1 - (row ^ 1))
    ]
    arrays, segments, act_order = [], [[] for _ in range(cands)], [[] for _ in range(cands)]

    def place(value, start, sources):
        every = lax.all_gather(scatter_sum(value), "col", axis=0)
        n = every.shape[2]
        for p in range(parts):
            for j, source in enumerate(sources):
                at, row_at = start + p * n, (p * 2 + j) * n
                while at < start + (p + 1) * n:
                    c, s = at // tok, at % tok
                    length = min(tok - s, start + (p + 1) * n - at)
                    segments[c].append((len(arrays), row_at, length))
                    act_order[c].append(source[c, s : s + length])
                    at, row_at = at + length, row_at + length
        arrays.append(every.reshape(parts * 2 * n, dirs))

    place(jnp.concatenate([own_own, own_end], axis=1), 0, act[:2])
    for (first, _), product in zip(ranges, products):
        place(product, first, act[2:])
    act_rot = jnp.stack([jnp.concatenate(x, axis=0) for x in act_order])
    layout = tuple(tuple(s) for s in segments)
    rotated, scores = rotate_and_score(arrays, layout, act_rot, eigenvalues, query_rotated)
    scores = exchange_sum(exchange_sum(scores, "col", parts), "row", planes)
    return rotated, scores


def solution(mesh):
    placed = (
        P("groups", "row", None),
        P("groups", "row", "col"),
        P(None, "col"),
        P("col", "row"),
        P("row", "col"),
        P(None, "row", "col"),
        P("groups"),
        P(),
    )
    chain = mesh.shape["groups"] == 2 and mesh.shape["row"] == 4 and mesh.shape["col"] == 4
    return jax.shard_map(
        chain_body if chain else gather_body,
        mesh=mesh,
        in_specs=placed,
        out_specs=(P("groups", "row", "col"), P(None, "groups")),
        check_vma=False,
    )
```

```python
import functools

import jax
import jax.numpy as jnp
from jax import lax
from jax.experimental import pallas as pl
from jax.experimental.pallas import tpu as pltpu
from jax.sharding import PartitionSpec as P

DAMPING = 0.05
BF16 = jnp.bfloat16
F32 = jnp.float32


def candidate_lengths(example_ids, token_counts):
    pool_size = token_counts.shape[0]
    hits = example_ids[:, None] == jnp.arange(pool_size, dtype=jnp.int32)[None, :]
    return jnp.sum(jnp.where(hits, token_counts[None, :], 0), axis=1)


def local_activations(acts, act_basis, lengths):
    tok = acts.shape[1]
    positions = lax.axis_index("row") * tok + jnp.arange(tok, dtype=jnp.int32)
    live = (positions[None, :] < lengths[:, None]).astype(F32)
    rotated = jnp.einsum("ctd,dk->ctk", acts, act_basis, preferred_element_type=F32)
    return (rotated * live[:, :, None]).astype(BF16)


def final_kernel(layout, count, *refs):
    arrays = refs[:count]
    act_ref, eig_ref, query_ref, out_ref, score_ref = refs[count:]
    queries = query_ref.shape[0]
    damped = eig_ref[...] + DAMPING
    weights = [query_ref[q].astype(F32) / damped for q in range(queries)]
    rows = [[] for _ in range(queries)]
    for c, segments in enumerate(layout):
        tokens = jnp.concatenate([arrays[i][s : s + n] for i, s, n in segments], axis=0)
        tile = lax.dot_general(
            tokens, act_ref[c], (((0,), (0,)), ((), ())), preferred_element_type=F32
        )
        out_ref[c] = tile
        for q in range(queries):
            rows[q].append(jnp.sum(weights[q] * tile, axis=0, keepdims=True))
    score_ref[0] = jnp.concatenate([r for one in rows for r in one], axis=0)


def rotate_and_score(arrays, layout, act_rot, eigenvalues, query_rotated):
    cands, seq, width = act_rot.shape
    dirs = eigenvalues.shape[0]
    queries = query_rotated.shape[0]
    block = min(dirs, 256)
    steps = dirs // block
    rotated, partial_scores = pl.pallas_call(
        functools.partial(final_kernel, layout, len(arrays)),
        grid=(steps,),
        in_specs=[pl.BlockSpec((x.shape[0], block), lambda i: (0, i)) for x in arrays]
        + [
            pl.BlockSpec((cands, seq, width), lambda i: (0, 0, 0)),
            pl.BlockSpec((block, width), lambda i: (i, 0)),
            pl.BlockSpec((queries, block, width), lambda i: (0, i, 0)),
        ],
        out_specs=[
            pl.BlockSpec((cands, block, width), lambda i: (0, i, 0)),
            pl.BlockSpec((1, queries * cands, width), lambda i: (i, 0, 0)),
        ],
        out_shape=[
            jax.ShapeDtypeStruct((cands, dirs, width), F32),
            jax.ShapeDtypeStruct((steps, queries * cands, width), F32),
        ],
        compiler_params=pltpu.CompilerParams(vmem_limit_bytes=16 * 2**20),
    )(*arrays, act_rot, eigenvalues, query_rotated)
    return rotated, jnp.sum(partial_scores, axis=(0, 2)).reshape(queries, cands)


def gather_body(acts, grads, act_basis, grad_basis, eigenvalues, query_rotated, example_ids, token_counts):
    lengths = candidate_lengths(example_ids, token_counts)
    local_act = local_activations(acts, act_basis, lengths)
    partial_value = jnp.einsum(
        "ctd,dj->ctj",
        lax.all_gather(grads, "row", axis=1, tiled=True),
        grad_basis,
        preferred_element_type=F32,
    )
    every_act = lax.all_gather(local_act, "row", axis=1, tiled=True)
    rotated_grads = lax.psum(partial_value, "col").astype(BF16)
    cands, seq = rotated_grads.shape[:2]
    arrays = [rotated_grads[c] for c in range(cands)]
    layout = tuple(((c, 0, seq),) for c in range(cands))
    rotated, scores = rotate_and_score(arrays, layout, every_act, eigenvalues, query_rotated)
    return rotated, lax.psum(scores, ("row", "col"))


def after(value, *earlier):
    return lax.optimization_barrier((value, *earlier))[0]


def project_kernel(count, widths, *refs):
    flags, refs = refs[0], refs[1:]
    tokens, basis, out, acc = refs[:count], refs[count:-2], refs[-2], refs[-1]
    step = pl.program_id(0)
    rows = tokens[0][...]
    if count > 1:
        inner = [t[...] for t in tokens[1:]]
        rows = jnp.where(flags[0] == 1, rows, jnp.concatenate(inner, axis=0) if count > 2 else inner[0])
    start, spans = 0, []
    for width in widths:
        spans.append((start, start + width))
        start += width

    @pl.when(step == 0)
    def _():
        acc[...] = jnp.zeros_like(acc)

    for ref, (a, b) in zip(basis, spans):
        acc[:, a:b] += jnp.dot(rows, ref[...], preferred_element_type=F32)

    @pl.when(step == pl.num_programs(0) - 1)
    def _():
        if len(basis) == 1:
            out[...] = acc[...].astype(BF16)
        else:
            (c, d), (e, f) = spans[-2:]
            if c > 0:
                out[:, :c] = acc[:, :c].astype(BF16)

            @pl.when(flags[1] == 0)
            def _():
                out[:, c:f] = acc[:, c:f].astype(BF16)

            @pl.when(flags[1] != 0)
            def _():
                out[:, c:d] = acc[:, e:f].astype(BF16)
                out[:, e:f] = acc[:, c:d].astype(BF16)


def project(flags, tokens, bases):
    feats = bases[0].shape[0]
    widths = tuple(x.shape[1] for x in bases)
    block, total = 1024, sum(widths)
    rows = tokens[0][2]
    specs = []
    for _, start, n in tokens:
        assert start % n == 0
        specs.append(pl.BlockSpec((n, block), lambda k, i=start // n: (i, k)))
    return pl.pallas_call(
        functools.partial(project_kernel, len(tokens), widths),
        grid=(feats // block,),
        in_specs=[pl.BlockSpec(memory_space=pltpu.SMEM)]
        + specs
        + [pl.BlockSpec((block, w), lambda k: (k, 0)) for w in widths],
        out_specs=pl.BlockSpec((rows, total), lambda k: (0, 0)),
        out_shape=jax.ShapeDtypeStruct((rows, total), BF16),
        scratch_shapes=[pltpu.VMEM((rows, total), F32)],
        compiler_params=pltpu.CompilerParams(vmem_limit_bytes=18 * 2**20),
        cost_estimate=pl.CostEstimate(
            flops=rows * feats * total // 8,
            bytes_accessed=feats * (total + rows) // 8,
            transcendentals=0,
        ),
    )(flags, *[array for array, _, _ in tokens], *bases)


def after(value, *earlier):
    return lax.optimization_barrier((value, *earlier))[0]


def exchange_sum(value, axis, size):
    total = value
    for d in range(1, size):
        total = total + lax.ppermute(value, axis, [(i, i ^ d) for i in range(size)])
    return total


def chain_body(acts, grads, act_basis, grad_basis, eigenvalues, query_rotated, example_ids, token_counts):
    cands, tok, feats = grads.shape
    dirs = grad_basis.shape[1]
    group, row, col = (lax.axis_index(a) for a in ("groups", "row", "col"))
    sides, planes, parts = 2, 4, 4
    middle, ends = [(1, 2), (2, 1)], [(0, 3), (3, 0)]
    beside = [(i, i ^ 1) for i in range(planes)]
    at_end = (row == 0) | (row == planes - 1)
    flags = jnp.stack([at_end.astype(jnp.int32), group.astype(jnp.int32)])

    half, flat = dirs // sides, grads.reshape(cands * tok, feats)
    units, deep, slab = 8, feats // 8, cands * tok // 8
    near, far, other = [], [], []
    spans = [(0, 1), (1, 3), (3, 5), (5, 7), (7, units)]
    inner = [(0, 1), (1, 4), (4, units)]
    own_own = project(flags, [(flat, 0, cands * tok)], [grad_basis])
    for i, (a, b) in enumerate(spans):
        if i < len(inner):
            tie = [near[0]] if i == 2 else []
            rows = after(flat, *tie)[inner[i][0] * slab : inner[i][1] * slab]
            other.append(lax.ppermute(rows, "row", middle))
        tie = []
        if i == 2:
            tie = [near[0], own_own, other[0]]
        if i == 3:
            tie = [near[1], local_act, other[1]]
        if i == 4:
            tie = [near[2]]
        piece = lax.dynamic_slice(after(grad_basis, *tie), (a * deep, group * half), ((b - a) * deep, half))
        near.append(lax.ppermute(piece, "row", beside))
        far.append(lax.ppermute(near[i], "groups", [(0, 1), (1, 0)]))
        if i == 0:
            lengths = candidate_lengths(example_ids, token_counts)
            local_act = local_activations(acts, after(act_basis, near[0]), lengths)
            every_act = lax.all_gather(local_act, "row", axis=0)
    near_basis = jnp.concatenate(near, axis=0)
    far_basis = jnp.concatenate(far, axis=0)
    own_end = project(flags, [(flat, 0, cands * tok)], [near_basis, far_basis])

    ranges = [(0, 4 * slab), (4 * slab, 6 * slab), (6 * slab, units * slab)]
    partner = []
    for i, (a, b) in enumerate(ranges):
        tie = [[near[3], far[1], every_act], [near[4], far[2], other[2]], [own_end]][i]
        if i == 2:
            tie += partner
        partner.append(lax.ppermute(after(flat, *tie)[a:b], "row", ends))

    def scatter_sum(value):
        value = value.reshape(parts, -1, 2 * dirs)
        total = lax.dynamic_index_in_dim(value, col, 0, keepdims=False).astype(F32)
        for d in range(1, parts):
            sent = lax.dynamic_index_in_dim(value, col ^ d, 0, keepdims=False)
            total = total + lax.ppermute(sent, "col", [(i, i ^ d) for i in range(parts)]).astype(F32)
        total = total.astype(BF16)
        return jnp.stack([total[:, :dirs], lax.ppermute(total[:, dirs:], "row", beside)])

    act = [
        lax.dynamic_index_in_dim(every_act, i, 0, keepdims=False)
        for i in (row, row ^ 1, planes - 1 - row, planes - 1 - (row ^ 1))
    ]
    sums, arrays, segments, act_order = [], [], [[] for _ in range(cands)], [[] for _ in range(cands)]

    def place(value, start, sources):
        sums.append(scatter_sum(value))
        every = lax.all_gather(sums[-1], "col", axis=0)
        n = every.shape[2]
        for p in range(parts):
            for j, source in enumerate(sources):
                at, row_at = start + p * n, (p * 2 + j) * n
                while at < start + (p + 1) * n:
                    c, s = at // tok, at % tok
                    length = min(tok - s, start + (p + 1) * n - at)
                    segments[c].append((len(arrays), row_at, length))
                    act_order[c].append(source[c, s : s + length])
                    at, row_at = at + length, row_at + length
        arrays.append(every.reshape(parts * 2 * n, dirs))

    place(jnp.concatenate([own_own, own_end], axis=1), 0, act[:2])
    later = {
        0: [(other[0], 0, slab), (other[1], 0, 3 * slab)],
        1: [(other[2], 0, 2 * slab)],
        2: [(other[2], 2 * slab, 2 * slab)],
    }
    for i in (1, 0, 2):
        a, b = ranges[i]
        far_later = after(far_basis, arrays[0], *(sums if i == 2 else []))
        tokens = [(partner[i], 0, b - a)] + later[i]
        place(project(flags, tokens, [grad_basis, near_basis, far_later]), a, act[2:])
    act_rot = jnp.stack([jnp.concatenate(x, axis=0) for x in act_order])
    layout = tuple(tuple(s) for s in segments)
    rotated, scores = rotate_and_score(arrays, layout, act_rot, eigenvalues, query_rotated)
    scores = exchange_sum(exchange_sum(scores, "col", parts), "row", planes)
    return rotated, scores


def solution(mesh):
    placed = (
        P("groups", "row", None),
        P("groups", "row", "col"),
        P(None, "col"),
        P("col", "row"),
        P("row", "col"),
        P(None, "row", "col"),
        P("groups"),
        P(),
    )
    chain = mesh.shape["groups"] == 2 and mesh.shape["row"] == 4 and mesh.shape["col"] == 4
    return jax.shard_map(
        chain_body if chain else gather_body,
        mesh=mesh,
        in_specs=placed,
        out_specs=(P("groups", "row", "col"), P(None, "groups")),
        check_vma=False,
    )
```

```python
import functools

import jax
import jax.numpy as jnp
from jax import lax
from jax.experimental import pallas as pl
from jax.experimental.pallas import tpu as pltpu
from jax.sharding import PartitionSpec as P

DAMPING = 0.05
BF16 = jnp.bfloat16
F32 = jnp.float32


def candidate_lengths(example_ids, token_counts):
    pool_size = token_counts.shape[0]
    hits = example_ids[:, None] == jnp.arange(pool_size, dtype=jnp.int32)[None, :]
    return jnp.sum(jnp.where(hits, token_counts[None, :], 0), axis=1)


def local_activations(acts, act_basis, lengths):
    tok = acts.shape[1]
    positions = lax.axis_index("row") * tok + jnp.arange(tok, dtype=jnp.int32)
    live = (positions[None, :] < lengths[:, None]).astype(F32)
    rotated = jnp.einsum("ctd,dk->ctk", acts, act_basis, preferred_element_type=F32)
    return (rotated * live[:, :, None]).astype(BF16)


def final_kernel(layout, count, *refs):
    arrays = refs[:count]
    act_ref, eig_ref, query_ref, out_ref, score_ref = refs[count:]
    queries = query_ref.shape[0]
    damped = eig_ref[...] + DAMPING
    weights = [query_ref[q].astype(F32) / damped for q in range(queries)]
    rows = [[] for _ in range(queries)]
    for c, segments in enumerate(layout):
        tokens = jnp.concatenate([arrays[i][s : s + n] for i, s, n in segments], axis=0)
        tile = lax.dot_general(
            tokens, act_ref[c], (((0,), (0,)), ((), ())), preferred_element_type=F32
        )
        out_ref[c] = tile
        for q in range(queries):
            rows[q].append(jnp.sum(weights[q] * tile, axis=0, keepdims=True))
    score_ref[0] = jnp.concatenate([r for one in rows for r in one], axis=0)


def rotate_and_score(arrays, layout, act_rot, eigenvalues, query_rotated):
    cands, seq, width = act_rot.shape
    dirs = eigenvalues.shape[0]
    queries = query_rotated.shape[0]
    block = min(dirs, 256)
    steps = dirs // block
    rotated, partial_scores = pl.pallas_call(
        functools.partial(final_kernel, layout, len(arrays)),
        grid=(steps,),
        in_specs=[pl.BlockSpec((x.shape[0], block), lambda i: (0, i)) for x in arrays]
        + [
            pl.BlockSpec((cands, seq, width), lambda i: (0, 0, 0)),
            pl.BlockSpec((block, width), lambda i: (i, 0)),
            pl.BlockSpec((queries, block, width), lambda i: (0, i, 0)),
        ],
        out_specs=[
            pl.BlockSpec((cands, block, width), lambda i: (0, i, 0)),
            pl.BlockSpec((1, queries * cands, width), lambda i: (i, 0, 0)),
        ],
        out_shape=[
            jax.ShapeDtypeStruct((cands, dirs, width), F32),
            jax.ShapeDtypeStruct((steps, queries * cands, width), F32),
        ],
        compiler_params=pltpu.CompilerParams(vmem_limit_bytes=16 * 2**20),
    )(*arrays, act_rot, eigenvalues, query_rotated)
    return rotated, jnp.sum(partial_scores, axis=(0, 2)).reshape(queries, cands)


def gather_body(acts, grads, act_basis, grad_basis, eigenvalues, query_rotated, example_ids, token_counts):
    lengths = candidate_lengths(example_ids, token_counts)
    local_act = local_activations(acts, act_basis, lengths)
    partial_value = jnp.einsum(
        "ctd,dj->ctj",
        lax.all_gather(grads, "row", axis=1, tiled=True),
        grad_basis,
        preferred_element_type=F32,
    )
    every_act = lax.all_gather(local_act, "row", axis=1, tiled=True)
    rotated_grads = lax.psum(partial_value, "col").astype(BF16)
    cands, seq = rotated_grads.shape[:2]
    arrays = [rotated_grads[c] for c in range(cands)]
    layout = tuple(((c, 0, seq),) for c in range(cands))
    rotated, scores = rotate_and_score(arrays, layout, every_act, eigenvalues, query_rotated)
    return rotated, lax.psum(scores, ("row", "col"))


def after(value, *earlier):
    return lax.optimization_barrier((value, *earlier))[0]


def project_kernel(ends, count, widths, *refs):
    flags, refs = refs[0], refs[1:]
    tokens, basis, out, acc = refs[:count], refs[count:-2], refs[-2], refs[-1]
    step = pl.program_id(0)
    def joined(refs):
        return jnp.concatenate([t[...] for t in refs], axis=0) if len(refs) > 1 else refs[0][...]

    rows = joined(tokens[:ends])
    if count > ends:
        rows = jnp.where(flags[0] == 1, rows, joined(tokens[ends:]))
    start, spans = 0, []
    for width in widths:
        spans.append((start, start + width))
        start += width

    @pl.when(step == 0)
    def _():
        acc[...] = jnp.zeros_like(acc)

    for ref, (a, b) in zip(basis, spans):
        acc[:, a:b] += jnp.dot(rows, ref[...], preferred_element_type=F32)

    @pl.when(step == pl.num_programs(0) - 1)
    def _():
        if len(basis) == 1:
            out[...] = acc[...].astype(BF16)
        else:
            (c, d), (e, f) = spans[-2:]
            if c > 0:
                out[:, :c] = acc[:, :c].astype(BF16)

            @pl.when(flags[1] == 0)
            def _():
                out[:, c:f] = acc[:, c:f].astype(BF16)

            @pl.when(flags[1] != 0)
            def _():
                out[:, c:d] = acc[:, e:f].astype(BF16)
                out[:, e:f] = acc[:, c:d].astype(BF16)


def project(flags, ends, middles, bases):
    tokens = ends + middles
    feats = bases[0].shape[0]
    widths = tuple(x.shape[1] for x in bases)
    block, total = 1024, sum(widths)
    rows = sum(n for _, _, n in ends)
    specs = []
    for _, start, n in tokens:
        assert start % n == 0
        specs.append(pl.BlockSpec((n, block), lambda k, i=start // n: (i, k)))
    return pl.pallas_call(
        functools.partial(project_kernel, len(ends), len(tokens), widths),
        grid=(feats // block,),
        in_specs=[pl.BlockSpec(memory_space=pltpu.SMEM)]
        + specs
        + [pl.BlockSpec((block, w), lambda k: (k, 0)) for w in widths],
        out_specs=pl.BlockSpec((rows, total), lambda k: (0, 0)),
        out_shape=jax.ShapeDtypeStruct((rows, total), BF16),
        scratch_shapes=[pltpu.VMEM((rows, total), F32)],
        compiler_params=pltpu.CompilerParams(vmem_limit_bytes=18 * 2**20),
        cost_estimate=pl.CostEstimate(
            flops=rows * feats * total // 8,
            bytes_accessed=feats * (total + rows) // 8,
            transcendentals=0,
        ),
    )(flags, *[array for array, _, _ in tokens], *bases)


def after(value, *earlier):
    return lax.optimization_barrier((value, *earlier))[0]


def exchange_sum(value, axis, size):
    total = value
    for d in range(1, size):
        total = total + lax.ppermute(value, axis, [(i, i ^ d) for i in range(size)])
    return total


def chain_body(acts, grads, act_basis, grad_basis, eigenvalues, query_rotated, example_ids, token_counts):
    cands, tok, feats = grads.shape
    dirs = grad_basis.shape[1]
    group, row, col = (lax.axis_index(a) for a in ("groups", "row", "col"))
    sides, planes, parts = 2, 4, 4
    middle, ends = [(1, 2), (2, 1)], [(0, 3), (3, 0)]
    beside = [(i, i ^ 1) for i in range(planes)]
    at_end = (row == 0) | (row == planes - 1)
    flags = jnp.stack([at_end.astype(jnp.int32), group.astype(jnp.int32)])

    half, flat = dirs // sides, grads.reshape(cands * tok, feats)
    units, deep, slab = 8, feats // 8, cands * tok // 8
    lengths = candidate_lengths(example_ids, token_counts)
    local_act = local_activations(acts, act_basis, lengths)
    every_act = lax.all_gather(local_act, "row", axis=0)
    near, far, other = [], [], []
    spans = [(0, 1), (1, 3), (3, 5), (5, 7), (7, units)]
    own_own = project(flags, [(flat, 0, cands * tok)], [], [grad_basis])
    for i, (a, b) in enumerate(spans):
        piece = lax.dynamic_slice(grad_basis, (a * deep, group * half), ((b - a) * deep, half))
        if i >= 2:
            early = {2: [own_own, local_act], 3: [other[0]], 4: [every_act]}[i]
            piece = after(piece, near[i - 2], *early)
        if i in (0, 2):
            part = flat[: 4 * slab] if i == 0 else after(flat[4 * slab :], near[0])
            other.append(lax.ppermute(part, "row", middle))
        near.append(lax.ppermute(piece, "row", beside))
        far.append(lax.ppermute(near[i], "groups", [(0, 1), (1, 0)]))
    near_basis = jnp.concatenate(near, axis=0)
    far_basis = jnp.concatenate(far, axis=0)
    own_end = project(flags, [(flat, 0, cands * tok)], [], [near_basis, far_basis])

    ranges = [(0, 3), (3, 5), (5, 7), (7, units)]
    ready = [near[4], far[2], *other]
    partner = []
    for k, (a, b) in enumerate(ranges):
        tie = [ready, ready, [own_end], []][k] + ([partner[k - 2]] if k >= 2 else [])
        piece = flat[a * slab : b * slab]
        partner.append(lax.ppermute(after(piece, *tie), "row", ends))

    def scatter_sum(value):
        value = value.reshape(parts, -1, 2 * dirs)
        total = lax.dynamic_index_in_dim(value, col, 0, keepdims=False).astype(F32)
        for d in range(1, parts):
            sent = lax.dynamic_index_in_dim(value, col ^ d, 0, keepdims=False)
            total = total + lax.ppermute(sent, "col", [(i, i ^ d) for i in range(parts)]).astype(F32)
        total = total.astype(BF16)
        return jnp.stack([total[:, :dirs], lax.ppermute(total[:, dirs:], "row", beside)])

    act = [
        lax.dynamic_index_in_dim(every_act, i, 0, keepdims=False)
        for i in (row, row ^ 1, planes - 1 - row, planes - 1 - (row ^ 1))
    ]
    sums, arrays, segments, act_order = [], [], [[] for _ in range(cands)], [[] for _ in range(cands)]

    def place(value, start, sources):
        sums.append(scatter_sum(value))
        every = lax.all_gather(sums[-1], "col", axis=0)
        n = every.shape[2]
        for p in range(parts):
            for j, source in enumerate(sources):
                at, row_at = start + p * n, (p * 2 + j) * n
                while at < start + (p + 1) * n:
                    c, s = at // tok, at % tok
                    length = min(tok - s, start + (p + 1) * n - at)
                    segments[c].append((len(arrays), row_at, length))
                    act_order[c].append(source[c, s : s + length])
                    at, row_at = at + length, row_at + length
        arrays.append(every.reshape(parts * 2 * n, dirs))

    place(jnp.concatenate([own_own, own_end], axis=1), 0, act[:2])
    batches = [
        ((0,), [(other[0], 0, 3 * slab)], []),
        ((1,), [(other[0], 3 * slab, slab), (other[1], 0, slab)], arrays[:1]),
        ((2, 3), [(other[1], slab, slab), (other[1], 2 * slab, 2 * slab)], arrays),
    ]
    for batch, middles, earlier in batches:
        tokens = [(partner[k], 0, (ranges[k][1] - ranges[k][0]) * slab) for k in batch]
        product = project(flags, tokens, middles, [grad_basis, near_basis, after(far_basis, *earlier)])
        place(product, ranges[batch[0]][0] * slab, act[2:])
    act_rot = jnp.stack([jnp.concatenate(x, axis=0) for x in act_order])
    layout = tuple(tuple(s) for s in segments)
    rotated, scores = rotate_and_score(arrays, layout, act_rot, eigenvalues, query_rotated)
    scores = exchange_sum(exchange_sum(scores, "col", parts), "row", planes)
    return rotated, scores


def solution(mesh):
    placed = (
        P("groups", "row", None),
        P("groups", "row", "col"),
        P(None, "col"),
        P("col", "row"),
        P("row", "col"),
        P(None, "row", "col"),
        P("groups"),
        P(),
    )
    chain = mesh.shape["groups"] == 2 and mesh.shape["row"] == 4 and mesh.shape["col"] == 4
    return jax.shard_map(
        chain_body if chain else gather_body,
        mesh=mesh,
        in_specs=placed,
        out_specs=(P("groups", "row", "col"), P(None, "groups")),
        check_vma=False,
    )
```

```python
import functools

import jax
import jax.numpy as jnp
from jax import lax
from jax.experimental import pallas as pl
from jax.experimental.pallas import tpu as pltpu
from jax.sharding import PartitionSpec as P

DAMPING = 0.05
BF16 = jnp.bfloat16
F32 = jnp.float32


def candidate_lengths(example_ids, token_counts):
    pool_size = token_counts.shape[0]
    hits = example_ids[:, None] == jnp.arange(pool_size, dtype=jnp.int32)[None, :]
    return jnp.sum(jnp.where(hits, token_counts[None, :], 0), axis=1)


def local_activations(acts, act_basis, lengths):
    tok = acts.shape[1]
    positions = lax.axis_index("row") * tok + jnp.arange(tok, dtype=jnp.int32)
    live = (positions[None, :] < lengths[:, None]).astype(F32)
    rotated = jnp.einsum("ctd,dk->ctk", acts, act_basis, preferred_element_type=F32)
    return (rotated * live[:, :, None]).astype(BF16)


def final_kernel(layout, count, *refs):
    arrays = refs[:count]
    act_ref, eig_ref, query_ref, out_ref, score_ref = refs[count:]
    queries = query_ref.shape[0]
    damped = eig_ref[...] + DAMPING
    weights = [query_ref[q].astype(F32) / damped for q in range(queries)]
    rows = [[] for _ in range(queries)]
    for c, segments in enumerate(layout):
        tokens = jnp.concatenate([arrays[i][s : s + n] for i, s, n in segments], axis=0)
        tile = lax.dot_general(
            tokens, act_ref[c], (((0,), (0,)), ((), ())), preferred_element_type=F32
        )
        out_ref[c] = tile
        for q in range(queries):
            rows[q].append(jnp.sum(weights[q] * tile, axis=0, keepdims=True))
    score_ref[0] = jnp.concatenate([r for one in rows for r in one], axis=0)


def rotate_and_score(arrays, layout, act_rot, eigenvalues, query_rotated):
    cands, seq, width = act_rot.shape
    dirs = eigenvalues.shape[0]
    queries = query_rotated.shape[0]
    block = min(dirs, 256)
    steps = dirs // block
    rotated, partial_scores = pl.pallas_call(
        functools.partial(final_kernel, layout, len(arrays)),
        grid=(steps,),
        in_specs=[pl.BlockSpec((x.shape[0], block), lambda i: (0, i)) for x in arrays]
        + [
            pl.BlockSpec((cands, seq, width), lambda i: (0, 0, 0)),
            pl.BlockSpec((block, width), lambda i: (i, 0)),
            pl.BlockSpec((queries, block, width), lambda i: (0, i, 0)),
        ],
        out_specs=[
            pl.BlockSpec((cands, block, width), lambda i: (0, i, 0)),
            pl.BlockSpec((1, queries * cands, width), lambda i: (i, 0, 0)),
        ],
        out_shape=[
            jax.ShapeDtypeStruct((cands, dirs, width), F32),
            jax.ShapeDtypeStruct((steps, queries * cands, width), F32),
        ],
        compiler_params=pltpu.CompilerParams(vmem_limit_bytes=16 * 2**20),
    )(*arrays, act_rot, eigenvalues, query_rotated)
    return rotated, jnp.sum(partial_scores, axis=(0, 2)).reshape(queries, cands)


def gather_body(acts, grads, act_basis, grad_basis, eigenvalues, query_rotated, example_ids, token_counts):
    lengths = candidate_lengths(example_ids, token_counts)
    local_act = local_activations(acts, act_basis, lengths)
    partial_value = jnp.einsum(
        "ctd,dj->ctj",
        lax.all_gather(grads, "row", axis=1, tiled=True),
        grad_basis,
        preferred_element_type=F32,
    )
    every_act = lax.all_gather(local_act, "row", axis=1, tiled=True)
    rotated_grads = lax.psum(partial_value, "col").astype(BF16)
    cands, seq = rotated_grads.shape[:2]
    arrays = [rotated_grads[c] for c in range(cands)]
    layout = tuple(((c, 0, seq),) for c in range(cands))
    rotated, scores = rotate_and_score(arrays, layout, every_act, eigenvalues, query_rotated)
    return rotated, lax.psum(scores, ("row", "col"))


def after(value, *earlier):
    return lax.optimization_barrier((value, *earlier))[0]


def project_kernel(ends, count, widths, *refs):
    flags, refs = refs[0], refs[1:]
    tokens, basis, out, acc = refs[:count], refs[count:-2], refs[-2], refs[-1]
    step = pl.program_id(0)
    def joined(refs):
        return jnp.concatenate([t[...] for t in refs], axis=0) if len(refs) > 1 else refs[0][...]

    rows = joined(tokens[:ends])
    if count > ends:
        rows = jnp.where(flags[0] == 1, rows, joined(tokens[ends:]))
    start, spans = 0, []
    for width in widths:
        spans.append((start, start + width))
        start += width

    @pl.when(step == 0)
    def _():
        acc[...] = jnp.zeros_like(acc)

    for ref, (a, b) in zip(basis, spans):
        acc[:, a:b] += jnp.dot(rows, ref[...], preferred_element_type=F32)

    @pl.when(step == pl.num_programs(0) - 1)
    def _():
        if len(basis) == 1:
            out[...] = acc[...].astype(BF16)
        else:
            (c, d), (e, f) = spans[-2:]
            if c > 0:
                out[:, :c] = acc[:, :c].astype(BF16)

            @pl.when(flags[1] == 0)
            def _():
                out[:, c:f] = acc[:, c:f].astype(BF16)

            @pl.when(flags[1] != 0)
            def _():
                out[:, c:d] = acc[:, e:f].astype(BF16)
                out[:, e:f] = acc[:, c:d].astype(BF16)


def project(flags, ends, middles, bases):
    tokens = ends + middles
    feats = bases[0].shape[0]
    widths = tuple(x.shape[1] for x in bases)
    block, total = 1024, sum(widths)
    rows = sum(n for _, _, n in ends)
    specs = []
    for _, start, n in tokens:
        assert start % n == 0
        specs.append(pl.BlockSpec((n, block), lambda k, i=start // n: (i, k)))
    return pl.pallas_call(
        functools.partial(project_kernel, len(ends), len(tokens), widths),
        grid=(feats // block,),
        in_specs=[pl.BlockSpec(memory_space=pltpu.SMEM)]
        + specs
        + [pl.BlockSpec((block, w), lambda k: (k, 0)) for w in widths],
        out_specs=pl.BlockSpec((rows, total), lambda k: (0, 0)),
        out_shape=jax.ShapeDtypeStruct((rows, total), BF16),
        scratch_shapes=[pltpu.VMEM((rows, total), F32)],
        compiler_params=pltpu.CompilerParams(vmem_limit_bytes=18 * 2**20),
        cost_estimate=pl.CostEstimate(
            flops=rows * feats * total // 8,
            bytes_accessed=feats * (total + rows) // 8,
            transcendentals=0,
        ),
    )(flags, *[array for array, _, _ in tokens], *bases)


def after(value, *earlier):
    return lax.optimization_barrier((value, *earlier))[0]


def exchange_sum(value, axis, size):
    total = value
    for d in range(1, size):
        total = total + lax.ppermute(value, axis, [(i, i ^ d) for i in range(size)])
    return total


def chain_body(acts, grads, act_basis, grad_basis, eigenvalues, query_rotated, example_ids, token_counts):
    cands, tok, feats = grads.shape
    dirs = grad_basis.shape[1]
    group, row, col = (lax.axis_index(a) for a in ("groups", "row", "col"))
    sides, planes, parts = 2, 4, 4
    middle, ends = [(1, 2), (2, 1)], [(0, 3), (3, 0)]
    beside = [(i, i ^ 1) for i in range(planes)]
    at_end = (row == 0) | (row == planes - 1)
    flags = jnp.stack([at_end.astype(jnp.int32), group.astype(jnp.int32)])

    half, flat = dirs // sides, grads.reshape(cands * tok, feats)
    units, deep, slab = 8, feats // 8, cands * tok // 8
    lengths = candidate_lengths(example_ids, token_counts)
    local_act = local_activations(acts, act_basis, lengths)
    every_act = lax.all_gather(local_act, "row", axis=0)
    near, far, other = [], [], []
    spans = [(0, 1), (1, 3), (3, 5), (5, 7), (7, units)]
    own_own = project(flags, [(flat, 0, cands * tok)], [], [grad_basis])
    for i, (a, b) in enumerate(spans):
        piece = lax.dynamic_slice(grad_basis, (a * deep, group * half), ((b - a) * deep, half))
        if i >= 2:
            early = {2: [own_own, local_act], 3: [other[0]], 4: []}[i]
            piece = after(piece, near[i - 2], *early)
        if i in (0, 2):
            part = flat[: 4 * slab] if i == 0 else after(flat[4 * slab :], near[0])
            other.append(lax.ppermute(part, "row", middle))
        near.append(lax.ppermute(piece, "row", beside))
        far.append(lax.ppermute(near[i], "groups", [(0, 1), (1, 0)]))
    near_basis = jnp.concatenate(near, axis=0)
    far_basis = jnp.concatenate(far, axis=0)

    ranges = [(0, 2), (2, 4), (4, units)]
    ties = [[near[4], far[1], other[1]], [near[4], far[2], other[1]], []]
    partner = []
    for k, (a, b) in enumerate(ranges):
        tie = ties[k] + ([partner[k - 2]] if k >= 2 else [])
        piece = flat[a * slab : b * slab]
        partner.append(lax.ppermute(after(piece, *tie), "row", ends))

    own_end = project(flags, [(flat, 0, cands * tok)], [], [near_basis, after(far_basis, partner[0])])
    bases = [grad_basis, near_basis, far_basis]
    sub, full = tok // parts, cands * tok
    products = [
        jnp.concatenate([own_own, own_end], axis=1),
        project(flags, [(partner[0], 0, 2 * slab), (partner[1], 0, 2 * slab)], [(other[0], 0, full // 2)], bases),
        project(flags, [(partner[2], 0, full // 2)], [(other[1], 0, full // 2)], bases),
    ]

    def swap(value, axis, d):
        size = planes if axis == "row" else parts
        return lax.ppermute(value, axis, [(i, i ^ d) for i in range(size)])

    def scatter_sum(value):
        value = value.reshape(-1, parts, sub, 2 * dirs)
        total = lax.dynamic_index_in_dim(value, col, 1, keepdims=False).astype(F32)
        for d in range(1, parts):
            sent = lax.dynamic_index_in_dim(value, col ^ d, 1, keepdims=False)
            total = total + swap(sent, "col", d).astype(F32)
        return total.astype(BF16).reshape(-1, 2 * dirs)

    def gather(total, *earlier):
        got = swap(total[:, dirs:], "row", 1)
        mine = jnp.concatenate([after(total[:, :dirs], *earlier), got], axis=0)
        pair = jnp.concatenate([mine, swap(mine, "col", 2)], axis=0)
        return [pair, swap(pair, "col", 1)]

    sums = [scatter_sum(x) for x in products]
    early, last = jnp.concatenate(sums[:2], axis=0), sums[2]
    arrays = gather(early, partner[2]) + gather(last)
    segments = [[] for _ in range(cands)]
    for kind in (0, 1):
        for c in range(cands):
            for j in (0, 1):
                for side in (0, 1):
                    for plane in (0, 1):
                        base = (side * 2 + plane) * early.shape[0]
                        if kind == 0:
                            segments[c].append((j, base + c * sub, sub))
                        elif c < cands // 2:
                            segments[c].append((j, base + (cands + c) * sub, sub))
                        else:
                            base = (side * 2 + plane) * last.shape[0]
                            segments[c].append((2 + j, base + (c - cands // 2) * sub, sub))
    layout = tuple(tuple(s) for s in segments)

    def by_part(block):
        split = block.reshape(cands, parts, sub, -1)
        split = jnp.where((col & 1) == 1, split[:, jnp.array([1, 0, 3, 2])], split)
        split = jnp.where((col & 2) == 2, split[:, jnp.array([2, 3, 0, 1])], split)
        return jnp.moveaxis(split[:, jnp.array([0, 2, 1, 3])], 1, 0)

    act = [
        by_part(lax.dynamic_index_in_dim(every_act, i, 0, keepdims=False))
        for i in (row, row ^ 1, planes - 1 - row, planes - 1 - (row ^ 1))
    ]
    act_rot = [jnp.stack(act[i : i + 2], axis=1) for i in (0, 2)]
    act_rot = [jnp.moveaxis(x, 2, 0).reshape(cands, 2 * tok, -1) for x in act_rot]
    act_rot = jnp.concatenate(act_rot, axis=1)
    rotated, scores = rotate_and_score(arrays, layout, act_rot, eigenvalues, query_rotated)
    scores = exchange_sum(exchange_sum(scores, "col", parts), "row", planes)
    return rotated, scores


def solution(mesh):
    placed = (
        P("groups", "row", None),
        P("groups", "row", "col"),
        P(None, "col"),
        P("col", "row"),
        P("row", "col"),
        P(None, "row", "col"),
        P("groups"),
        P(),
    )
    chain = mesh.shape["groups"] == 2 and mesh.shape["row"] == 4 and mesh.shape["col"] == 4
    return jax.shard_map(
        chain_body if chain else gather_body,
        mesh=mesh,
        in_specs=placed,
        out_specs=(P("groups", "row", "col"), P(None, "groups")),
        check_vma=False,
    )
```

```python
import functools

import jax
import jax.numpy as jnp
from jax import lax
from jax.experimental import pallas as pl
from jax.experimental.pallas import tpu as pltpu
from jax.sharding import PartitionSpec as P

DAMPING = 0.05
BF16 = jnp.bfloat16
F32 = jnp.float32


def candidate_lengths(example_ids, token_counts):
    pool_size = token_counts.shape[0]
    hits = example_ids[:, None] == jnp.arange(pool_size, dtype=jnp.int32)[None, :]
    return jnp.sum(jnp.where(hits, token_counts[None, :], 0), axis=1)


def local_activations(acts, act_basis, lengths):
    tok = acts.shape[1]
    positions = lax.axis_index("row") * tok + jnp.arange(tok, dtype=jnp.int32)
    live = (positions[None, :] < lengths[:, None]).astype(F32)
    rotated = jnp.einsum("ctd,dk->ctk", acts, act_basis, preferred_element_type=F32)
    return (rotated * live[:, :, None]).astype(BF16)


def final_kernel(layout, count, *refs):
    arrays = refs[:count]
    act_ref, eig_ref, query_ref, out_ref, score_ref = refs[count:]
    queries = query_ref.shape[0]
    damped = eig_ref[...] + DAMPING
    weights = [query_ref[q].astype(F32) / damped for q in range(queries)]
    rows = [[] for _ in range(queries)]
    for c, segments in enumerate(layout):
        tokens = jnp.concatenate([arrays[i][s : s + n] for i, s, n in segments], axis=0)
        tile = lax.dot_general(
            tokens, act_ref[c], (((0,), (0,)), ((), ())), preferred_element_type=F32
        )
        out_ref[c] = tile
        for q in range(queries):
            rows[q].append(jnp.sum(weights[q] * tile, axis=0, keepdims=True))
    score_ref[0] = jnp.concatenate([r for one in rows for r in one], axis=0)


def rotate_and_score(arrays, layout, act_rot, eigenvalues, query_rotated):
    cands, seq, width = act_rot.shape
    dirs = eigenvalues.shape[0]
    queries = query_rotated.shape[0]
    block = min(dirs, 256)
    steps = dirs // block
    rotated, partial_scores = pl.pallas_call(
        functools.partial(final_kernel, layout, len(arrays)),
        grid=(steps,),
        in_specs=[pl.BlockSpec((x.shape[0], block), lambda i: (0, i)) for x in arrays]
        + [
            pl.BlockSpec((cands, seq, width), lambda i: (0, 0, 0)),
            pl.BlockSpec((block, width), lambda i: (i, 0)),
            pl.BlockSpec((queries, block, width), lambda i: (0, i, 0)),
        ],
        out_specs=[
            pl.BlockSpec((cands, block, width), lambda i: (0, i, 0)),
            pl.BlockSpec((1, queries * cands, width), lambda i: (i, 0, 0)),
        ],
        out_shape=[
            jax.ShapeDtypeStruct((cands, dirs, width), F32),
            jax.ShapeDtypeStruct((steps, queries * cands, width), F32),
        ],
        compiler_params=pltpu.CompilerParams(vmem_limit_bytes=16 * 2**20),
    )(*arrays, act_rot, eigenvalues, query_rotated)
    return rotated, jnp.sum(partial_scores, axis=(0, 2)).reshape(queries, cands)


def gather_body(acts, grads, act_basis, grad_basis, eigenvalues, query_rotated, example_ids, token_counts):
    lengths = candidate_lengths(example_ids, token_counts)
    local_act = local_activations(acts, act_basis, lengths)
    partial_value = jnp.einsum(
        "ctd,dj->ctj",
        lax.all_gather(grads, "row", axis=1, tiled=True),
        grad_basis,
        preferred_element_type=F32,
    )
    every_act = lax.all_gather(local_act, "row", axis=1, tiled=True)
    rotated_grads = lax.psum(partial_value, "col").astype(BF16)
    cands, seq = rotated_grads.shape[:2]
    arrays = [rotated_grads[c] for c in range(cands)]
    layout = tuple(((c, 0, seq),) for c in range(cands))
    rotated, scores = rotate_and_score(arrays, layout, every_act, eigenvalues, query_rotated)
    return rotated, lax.psum(scores, ("row", "col"))


def after(value, *earlier):
    return lax.optimization_barrier((value, *earlier))[0]


def project_kernel(ends, count, widths, *refs):
    flags, refs = refs[0], refs[1:]
    tokens, basis, out, acc = refs[:count], refs[count:-2], refs[-2], refs[-1]
    step = pl.program_id(0)
    def joined(refs):
        return jnp.concatenate([t[...] for t in refs], axis=0) if len(refs) > 1 else refs[0][...]

    rows = joined(tokens[:ends])
    if count > ends:
        rows = jnp.where(flags[0] == 1, rows, joined(tokens[ends:]))
    start, spans = 0, []
    for width in widths:
        spans.append((start, start + width))
        start += width

    @pl.when(step == 0)
    def _():
        acc[...] = jnp.zeros_like(acc)

    for ref, (a, b) in zip(basis, spans):
        acc[:, a:b] += jnp.dot(rows, ref[...], preferred_element_type=F32)

    @pl.when(step == pl.num_programs(0) - 1)
    def _():
        if len(basis) == 1:
            out[...] = acc[...].astype(BF16)
        else:
            (c, d), (e, f) = spans[-2:]
            if c > 0:
                out[:, :c] = acc[:, :c].astype(BF16)

            @pl.when(flags[1] == 0)
            def _():
                out[:, c:f] = acc[:, c:f].astype(BF16)

            @pl.when(flags[1] != 0)
            def _():
                out[:, c:d] = acc[:, e:f].astype(BF16)
                out[:, e:f] = acc[:, c:d].astype(BF16)


def project(flags, ends, middles, bases):
    tokens = ends + middles
    feats = bases[0].shape[0]
    widths = tuple(x.shape[1] for x in bases)
    block, total = 1024, sum(widths)
    rows = sum(n for _, _, n in ends)
    specs = []
    for _, start, n in tokens:
        assert start % n == 0
        specs.append(pl.BlockSpec((n, block), lambda k, i=start // n: (i, k)))
    return pl.pallas_call(
        functools.partial(project_kernel, len(ends), len(tokens), widths),
        grid=(feats // block,),
        in_specs=[pl.BlockSpec(memory_space=pltpu.SMEM)]
        + specs
        + [pl.BlockSpec((block, w), lambda k: (k, 0)) for w in widths],
        out_specs=pl.BlockSpec((rows, total), lambda k: (0, 0)),
        out_shape=jax.ShapeDtypeStruct((rows, total), BF16),
        scratch_shapes=[pltpu.VMEM((rows, total), F32)],
        compiler_params=pltpu.CompilerParams(vmem_limit_bytes=56 * 2**20),
        cost_estimate=pl.CostEstimate(
            flops=rows * feats * total // 8,
            bytes_accessed=feats * (total + rows) // 8,
            transcendentals=0,
        ),
    )(flags, *[array for array, _, _ in tokens], *bases)


def after(value, *earlier):
    return lax.optimization_barrier((value, *earlier))[0]


def exchange_sum(value, axis, size):
    total = value
    for d in range(1, size):
        total = total + lax.ppermute(value, axis, [(i, i ^ d) for i in range(size)])
    return total


def chain_body(acts, grads, act_basis, grad_basis, eigenvalues, query_rotated, example_ids, token_counts):
    cands, tok, feats = grads.shape
    dirs = grad_basis.shape[1]
    group, row, col = (lax.axis_index(a) for a in ("groups", "row", "col"))
    sides, planes, parts = 2, 4, 4
    middle, ends = [(1, 2), (2, 1)], [(0, 3), (3, 0)]
    beside = [(i, i ^ 1) for i in range(planes)]
    at_end = (row == 0) | (row == planes - 1)
    flags = jnp.stack([at_end.astype(jnp.int32), group.astype(jnp.int32)])

    half, flat = dirs // sides, grads.reshape(cands * tok, feats)
    units, deep, slab = 8, feats // 8, cands * tok // 8
    lengths = candidate_lengths(example_ids, token_counts)
    local_act = local_activations(acts, act_basis, lengths)
    every_act = lax.all_gather(local_act, "row", axis=0)
    near, far, other = [], [], []
    spans = [(0, 1), (1, 3), (3, 5), (5, 7), (7, units)]
    own_own = project(flags, [(flat, 0, cands * tok)], [], [grad_basis])
    for i, (a, b) in enumerate(spans):
        piece = lax.dynamic_slice(grad_basis, (a * deep, group * half), ((b - a) * deep, half))
        if i >= 2:
            early = {2: [own_own, local_act], 3: [other[0], every_act], 4: [every_act]}[i]
            piece = after(piece, near[i - 2], *early)
        if i in (0, 2):
            part = flat[: 4 * slab] if i == 0 else after(flat[4 * slab :], near[0])
            other.append(lax.ppermute(part, "row", middle))
        near.append(lax.ppermute(piece, "row", beside))
        far.append(lax.ppermute(near[i], "groups", [(0, 1), (1, 0)]))
    near_basis = jnp.concatenate(near, axis=0)
    far_basis = jnp.concatenate(far, axis=0)

    ranges = [(0, 2), (2, 4), (4, units)]
    phase = [near[3], near[4], other[1]]
    ties = [[*phase, far[0], far[1]], [*phase, far[2], far[4]], []]
    partner = []
    for k, (a, b) in enumerate(ranges):
        tie = ties[k] + ([partner[k - 2]] if k >= 2 else [])
        piece = flat[a * slab : b * slab]
        partner.append(lax.ppermute(after(piece, *tie), "row", ends))

    own_end = project(flags, [(flat, 0, cands * tok)], [], [near_basis, after(far_basis, partner[0])])
    bases = [grad_basis, near_basis, far_basis]
    sub, full = tok // parts, cands * tok
    products = [
        jnp.concatenate([own_own, own_end], axis=1),
        project(flags, [(partner[0], 0, 2 * slab), (partner[1], 0, 2 * slab)], [(other[0], 0, full // 2)], bases),
        project(flags, [(partner[2], 0, full // 2)], [(other[1], 0, full // 2)], bases),
    ]

    def swap(value, axis, d):
        size = planes if axis == "row" else parts
        return lax.ppermute(value, axis, [(i, i ^ d) for i in range(size)])

    def scatter_sum(value):
        value = value.reshape(-1, parts, sub, 2 * dirs)
        total = lax.dynamic_index_in_dim(value, col, 1, keepdims=False).astype(F32)
        for d in range(1, parts):
            sent = lax.dynamic_index_in_dim(value, col ^ d, 1, keepdims=False)
            total = total + swap(sent, "col", d).astype(F32)
        return total.astype(BF16).reshape(-1, 2 * dirs)

    def gather(total, *earlier):
        got = swap(total[:, dirs:], "row", 1)
        mine = jnp.concatenate([after(total[:, :dirs], *earlier), got], axis=0)
        pair = jnp.concatenate([mine, swap(mine, "col", 2)], axis=0)
        return [pair, swap(pair, "col", 1)]

    sums = [scatter_sum(x) for x in products]
    early, last = jnp.concatenate(sums[:2], axis=0), sums[2]
    arrays = gather(early, partner[2]) + gather(last)
    segments = [[] for _ in range(cands)]
    for kind in (0, 1):
        for c in range(cands):
            for j in (0, 1):
                for side in (0, 1):
                    for plane in (0, 1):
                        base = (side * 2 + plane) * early.shape[0]
                        if kind == 0:
                            segments[c].append((j, base + c * sub, sub))
                        elif c < cands // 2:
                            segments[c].append((j, base + (cands + c) * sub, sub))
                        else:
                            base = (side * 2 + plane) * last.shape[0]
                            segments[c].append((2 + j, base + (c - cands // 2) * sub, sub))
    layout = tuple(tuple(s) for s in segments)

    def by_part(block):
        split = block.reshape(cands, parts, sub, -1)
        split = jnp.where((col & 1) == 1, split[:, jnp.array([1, 0, 3, 2])], split)
        split = jnp.where((col & 2) == 2, split[:, jnp.array([2, 3, 0, 1])], split)
        return jnp.moveaxis(split[:, jnp.array([0, 2, 1, 3])], 1, 0)

    act = [
        by_part(lax.dynamic_index_in_dim(every_act, i, 0, keepdims=False))
        for i in (row, row ^ 1, planes - 1 - row, planes - 1 - (row ^ 1))
    ]
    act_rot = [jnp.stack(act[i : i + 2], axis=1) for i in (0, 2)]
    act_rot = [jnp.moveaxis(x, 2, 0).reshape(cands, 2 * tok, -1) for x in act_rot]
    act_rot = jnp.concatenate(act_rot, axis=1)
    rotated, scores = rotate_and_score(arrays, layout, act_rot, eigenvalues, query_rotated)
    scores = exchange_sum(exchange_sum(scores, "col", parts), "row", planes)
    return rotated, scores


def solution(mesh):
    placed = (
        P("groups", "row", None),
        P("groups", "row", "col"),
        P(None, "col"),
        P("col", "row"),
        P("row", "col"),
        P(None, "row", "col"),
        P("groups"),
        P(),
    )
    chain = mesh.shape["groups"] == 2 and mesh.shape["row"] == 4 and mesh.shape["col"] == 4
    return jax.shard_map(
        chain_body if chain else gather_body,
        mesh=mesh,
        in_specs=placed,
        out_specs=(P("groups", "row", "col"), P(None, "groups")),
        check_vma=False,
    )
```

```python
import functools

import jax
import jax.numpy as jnp
from jax import lax
from jax.experimental import pallas as pl
from jax.experimental.pallas import tpu as pltpu
from jax.sharding import PartitionSpec as P

DAMPING = 0.05
BF16 = jnp.bfloat16
F32 = jnp.float32


def candidate_lengths(example_ids, token_counts):
    pool_size = token_counts.shape[0]
    hits = example_ids[:, None] == jnp.arange(pool_size, dtype=jnp.int32)[None, :]
    return jnp.sum(jnp.where(hits, token_counts[None, :], 0), axis=1)


def local_activations(acts, act_basis, lengths):
    tok = acts.shape[1]
    positions = lax.axis_index("row") * tok + jnp.arange(tok, dtype=jnp.int32)
    live = (positions[None, :] < lengths[:, None]).astype(F32)
    rotated = jnp.einsum("ctd,dk->ctk", acts, act_basis, preferred_element_type=F32)
    return (rotated * live[:, :, None]).astype(BF16)


def final_kernel(layout, count, *refs):
    arrays = refs[:count]
    act_ref, eig_ref, query_ref, out_ref, score_ref = refs[count:]
    queries = query_ref.shape[0]
    damped = eig_ref[...] + DAMPING
    weights = [query_ref[q].astype(F32) / damped for q in range(queries)]
    rows = [[] for _ in range(queries)]
    for c, segments in enumerate(layout):
        tokens = jnp.concatenate([arrays[i][s : s + n] for i, s, n in segments], axis=0)
        tile = lax.dot_general(
            tokens, act_ref[c], (((0,), (0,)), ((), ())), preferred_element_type=F32
        )
        out_ref[c] = tile
        for q in range(queries):
            rows[q].append(jnp.sum(weights[q] * tile, axis=0, keepdims=True))
    score_ref[0] = jnp.concatenate([r for one in rows for r in one], axis=0)


def rotate_and_score(arrays, layout, act_rot, eigenvalues, query_rotated):
    cands, seq, width = act_rot.shape
    dirs = eigenvalues.shape[0]
    queries = query_rotated.shape[0]
    block = min(dirs, 256)
    steps = dirs // block
    rotated, partial_scores = pl.pallas_call(
        functools.partial(final_kernel, layout, len(arrays)),
        grid=(steps,),
        in_specs=[pl.BlockSpec((x.shape[0], block), lambda i: (0, i)) for x in arrays]
        + [
            pl.BlockSpec((cands, seq, width), lambda i: (0, 0, 0)),
            pl.BlockSpec((block, width), lambda i: (i, 0)),
            pl.BlockSpec((queries, block, width), lambda i: (0, i, 0)),
        ],
        out_specs=[
            pl.BlockSpec((cands, block, width), lambda i: (0, i, 0)),
            pl.BlockSpec((1, queries * cands, width), lambda i: (i, 0, 0)),
        ],
        out_shape=[
            jax.ShapeDtypeStruct((cands, dirs, width), F32),
            jax.ShapeDtypeStruct((steps, queries * cands, width), F32),
        ],
        compiler_params=pltpu.CompilerParams(vmem_limit_bytes=16 * 2**20),
    )(*arrays, act_rot, eigenvalues, query_rotated)
    return rotated, jnp.sum(partial_scores, axis=(0, 2)).reshape(queries, cands)


def gather_body(acts, grads, act_basis, grad_basis, eigenvalues, query_rotated, example_ids, token_counts):
    lengths = candidate_lengths(example_ids, token_counts)
    local_act = local_activations(acts, act_basis, lengths)
    partial_value = jnp.einsum(
        "ctd,dj->ctj",
        lax.all_gather(grads, "row", axis=1, tiled=True),
        grad_basis,
        preferred_element_type=F32,
    )
    every_act = lax.all_gather(local_act, "row", axis=1, tiled=True)
    rotated_grads = lax.psum(partial_value, "col").astype(BF16)
    cands, seq = rotated_grads.shape[:2]
    arrays = [rotated_grads[c] for c in range(cands)]
    layout = tuple(((c, 0, seq),) for c in range(cands))
    rotated, scores = rotate_and_score(arrays, layout, every_act, eigenvalues, query_rotated)
    return rotated, lax.psum(scores, ("row", "col"))


def after(value, *earlier):
    return lax.optimization_barrier((value, *earlier))[0]


def project_kernel(ends, count, widths, *refs):
    flags, refs = refs[0], refs[1:]
    tokens, basis, out, acc = refs[:count], refs[count:-2], refs[-2], refs[-1]
    step = pl.program_id(0)
    def joined(refs):
        return jnp.concatenate([t[...] for t in refs], axis=0) if len(refs) > 1 else refs[0][...]

    rows = joined(tokens[:ends])
    if count > ends:
        rows = jnp.where(flags[0] == 1, rows, joined(tokens[ends:]))
    start, spans = 0, []
    for width in widths:
        spans.append((start, start + width))
        start += width

    @pl.when(step == 0)
    def _():
        acc[...] = jnp.zeros_like(acc)

    for ref, (a, b) in zip(basis, spans):
        acc[:, a:b] += jnp.dot(rows, ref[...], preferred_element_type=F32)

    @pl.when(step == pl.num_programs(0) - 1)
    def _():
        if len(basis) == 1:
            out[...] = acc[...].astype(BF16)
        else:
            (c, d), (e, f) = spans[-2:]
            if c > 0:
                out[:, :c] = acc[:, :c].astype(BF16)

            @pl.when(flags[1] == 0)
            def _():
                out[:, c:f] = acc[:, c:f].astype(BF16)

            @pl.when(flags[1] != 0)
            def _():
                out[:, c:d] = acc[:, e:f].astype(BF16)
                out[:, e:f] = acc[:, c:d].astype(BF16)


def project(flags, ends, middles, bases):
    tokens = ends + middles
    feats = bases[0].shape[0]
    widths = tuple(x.shape[1] for x in bases)
    block, total = 1024, sum(widths)
    rows = sum(n for _, _, n in ends)
    specs = []
    for _, start, n in tokens:
        assert start % n == 0
        specs.append(pl.BlockSpec((n, block), lambda k, i=start // n: (i, k)))
    return pl.pallas_call(
        functools.partial(project_kernel, len(ends), len(tokens), widths),
        grid=(feats // block,),
        in_specs=[pl.BlockSpec(memory_space=pltpu.SMEM)]
        + specs
        + [pl.BlockSpec((block, w), lambda k: (k, 0)) for w in widths],
        out_specs=pl.BlockSpec((rows, total), lambda k: (0, 0)),
        out_shape=jax.ShapeDtypeStruct((rows, total), BF16),
        scratch_shapes=[pltpu.VMEM((rows, total), F32)],
        compiler_params=pltpu.CompilerParams(vmem_limit_bytes=56 * 2**20),
        cost_estimate=pl.CostEstimate(
            flops=rows * feats * total // 8,
            bytes_accessed=feats * (total + rows) // 8,
            transcendentals=0,
        ),
    )(flags, *[array for array, _, _ in tokens], *bases)


def after(value, *earlier):
    return lax.optimization_barrier((value, *earlier))[0]


def exchange_sum(value, axis, size):
    total = value
    for d in range(1, size):
        total = total + lax.ppermute(value, axis, [(i, i ^ d) for i in range(size)])
    return total


def chain_body(acts, grads, act_basis, grad_basis, eigenvalues, query_rotated, example_ids, token_counts):
    cands, tok, feats = grads.shape
    dirs = grad_basis.shape[1]
    group, row, col = (lax.axis_index(a) for a in ("groups", "row", "col"))
    sides, planes, parts = 2, 4, 4
    middle, ends = [(1, 2), (2, 1)], [(0, 3), (3, 0)]
    beside = [(i, i ^ 1) for i in range(planes)]
    at_end = (row == 0) | (row == planes - 1)
    flags = jnp.stack([at_end.astype(jnp.int32), group.astype(jnp.int32)])

    half, flat = dirs // sides, grads.reshape(cands * tok, feats)
    units, deep, slab = 8, feats // 8, cands * tok // 8
    lengths = candidate_lengths(example_ids, token_counts)
    local_act = local_activations(acts, act_basis, lengths)
    every_act = lax.all_gather(local_act, "row", axis=0)
    near, far, other = [], [], []
    spans = [(0, 1), (1, 3), (3, 5), (5, 7), (7, units)]
    own_own = project(flags, [(flat, 0, cands * tok)], [], [grad_basis])
    for i, (a, b) in enumerate(spans):
        piece = lax.dynamic_slice(grad_basis, (a * deep, group * half), ((b - a) * deep, half))
        if i >= 2:
            early = {2: [own_own, local_act], 3: [other[0], every_act], 4: [every_act]}[i]
            piece = after(piece, near[i - 2], *early)
        if i in (0, 2):
            part = flat[: 4 * slab] if i == 0 else after(flat[4 * slab :], near[0])
            other.append(lax.ppermute(part, "row", middle))
        near.append(lax.ppermute(piece, "row", beside))
        far.append(lax.ppermute(near[i], "groups", [(0, 1), (1, 0)]))
    near_basis = jnp.concatenate(near, axis=0)
    far_basis = jnp.concatenate(far, axis=0)

    ranges = [(0, 2), (2, 4), (4, units)]
    phase = [near[3], near[4], other[1]]
    ties = [[*phase, far[0], far[1]], [*phase, far[2], far[4]], []]
    partner = []
    for k, (a, b) in enumerate(ranges):
        tie = ties[k] + ([partner[k - 2]] if k >= 2 else [])
        piece = flat[a * slab : b * slab]
        partner.append(lax.ppermute(after(piece, *tie), "row", ends))

    sub, full = tok // parts, cands * tok

    def by_part(block):
        split = block.reshape(cands, parts, sub, -1)
        return jnp.stack(
            [lax.dynamic_index_in_dim(split, col ^ d, 1, keepdims=False) for d in (0, 2, 1, 3)]
        )

    act = [
        by_part(lax.dynamic_index_in_dim(every_act, i, 0, keepdims=False))
        for i in (row, row ^ 1, planes - 1 - row, planes - 1 - (row ^ 1))
    ]
    act_rot = [jnp.stack(act[i : i + 2], axis=1) for i in (0, 2)]
    act_rot = [jnp.moveaxis(x, 2, 0).reshape(cands, 2 * tok, -1) for x in act_rot]
    act_rot = jnp.concatenate(act_rot, axis=1)

    own_end = project(flags, [(flat, 0, full)], [], [near_basis, after(far_basis, partner[0], act_rot)])
    outer = project(
        flags,
        [(partner[0], 0, 2 * slab), (partner[1], 0, 2 * slab)],
        [(other[0], 0, full // 2)],
        [grad_basis, near_basis, after(far_basis, own_end)],
    )

    def swap(value, axis, d):
        size = planes if axis == "row" else parts
        return lax.ppermute(value, axis, [(i, i ^ d) for i in range(size)])

    def scatter_sum(value):
        value = value.reshape(-1, parts, sub, 2 * dirs)
        total = lax.dynamic_index_in_dim(value, col, 1, keepdims=False).astype(F32)
        for d in range(1, parts):
            sent = lax.dynamic_index_in_dim(value, col ^ d, 1, keepdims=False)
            total = total + swap(sent, "col", d).astype(F32)
        return total.astype(BF16).reshape(-1, 2 * dirs)

    def to_neighbour(total):
        return jnp.concatenate([total[:, :dirs], swap(total[:, dirs:], "row", 1)], axis=0)

    def gather(mine):
        pair = jnp.concatenate([mine, swap(mine, "col", 2)], axis=0)
        return [pair, swap(pair, "col", 1)]

    own = scatter_sum(jnp.concatenate([own_own, own_end], axis=1))
    early = to_neighbour(jnp.concatenate([own, scatter_sum(outer)], axis=0))
    product = project(
        flags,
        [(partner[2], 0, full // 2)],
        [(other[1], 0, full // 2)],
        [grad_basis, near_basis, after(far_basis, early)],
    )
    last = to_neighbour(scatter_sum(product))
    arrays = gather(early) + gather(last)
    segments = [[] for _ in range(cands)]
    for kind in (0, 1):
        for c in range(cands):
            for j in (0, 1):
                for side in (0, 1):
                    for plane in (0, 1):
                        base = (side * 2 + plane) * early.shape[0] // 2
                        if kind == 0:
                            segments[c].append((j, base + c * sub, sub))
                        elif c < cands // 2:
                            segments[c].append((j, base + (cands + c) * sub, sub))
                        else:
                            base = (side * 2 + plane) * last.shape[0] // 2
                            segments[c].append((2 + j, base + (c - cands // 2) * sub, sub))
    layout = tuple(tuple(s) for s in segments)

    rotated, scores = rotate_and_score(arrays, layout, act_rot, eigenvalues, query_rotated)
    scores = exchange_sum(exchange_sum(scores, "col", parts), "row", planes)
    return rotated, scores


def solution(mesh):
    placed = (
        P("groups", "row", None),
        P("groups", "row", "col"),
        P(None, "col"),
        P("col", "row"),
        P("row", "col"),
        P(None, "row", "col"),
        P("groups"),
        P(),
    )
    chain = mesh.shape["groups"] == 2 and mesh.shape["row"] == 4 and mesh.shape["col"] == 4
    return jax.shard_map(
        chain_body if chain else gather_body,
        mesh=mesh,
        in_specs=placed,
        out_specs=(P("groups", "row", "col"), P(None, "groups")),
        check_vma=False,
    )
```

```python
import functools

import jax
import jax.numpy as jnp
from jax import lax
from jax.experimental import pallas as pl
from jax.experimental.pallas import tpu as pltpu
from jax.sharding import PartitionSpec as P

DAMPING = 0.05
BF16 = jnp.bfloat16
F32 = jnp.float32


def candidate_lengths(example_ids, token_counts):
    pool_size = token_counts.shape[0]
    hits = example_ids[:, None] == jnp.arange(pool_size, dtype=jnp.int32)[None, :]
    return jnp.sum(jnp.where(hits, token_counts[None, :], 0), axis=1)


def local_activations(acts, act_basis, lengths):
    tok = acts.shape[1]
    positions = lax.axis_index("row") * tok + jnp.arange(tok, dtype=jnp.int32)
    live = (positions[None, :] < lengths[:, None]).astype(F32)
    rotated = jnp.einsum("ctd,dk->ctk", acts, act_basis, preferred_element_type=F32)
    return (rotated * live[:, :, None]).astype(BF16)


def final_kernel(layout, count, *refs):
    arrays = refs[:count]
    act_ref, eig_ref, query_ref, out_ref, score_ref = refs[count:]
    queries = query_ref.shape[0]
    damped = eig_ref[...] + DAMPING
    weights = [query_ref[q].astype(F32) / damped for q in range(queries)]
    rows = [[] for _ in range(queries)]
    for c, segments in enumerate(layout):
        tokens = jnp.concatenate([arrays[i][s : s + n] for i, s, n in segments], axis=0)
        tile = lax.dot_general(
            tokens, act_ref[c], (((0,), (0,)), ((), ())), preferred_element_type=F32
        )
        out_ref[c] = tile
        for q in range(queries):
            rows[q].append(jnp.sum(weights[q] * tile, axis=0, keepdims=True))
    score_ref[0] = jnp.concatenate([r for one in rows for r in one], axis=0)


def rotate_and_score(arrays, layout, act_rot, eigenvalues, query_rotated):
    cands, seq, width = act_rot.shape
    dirs = eigenvalues.shape[0]
    queries = query_rotated.shape[0]
    block = min(dirs, 256)
    steps = dirs // block
    rotated, partial_scores = pl.pallas_call(
        functools.partial(final_kernel, layout, len(arrays)),
        grid=(steps,),
        in_specs=[pl.BlockSpec((x.shape[0], block), lambda i: (0, i)) for x in arrays]
        + [
            pl.BlockSpec((cands, seq, width), lambda i: (0, 0, 0)),
            pl.BlockSpec((block, width), lambda i: (i, 0)),
            pl.BlockSpec((queries, block, width), lambda i: (0, i, 0)),
        ],
        out_specs=[
            pl.BlockSpec((cands, block, width), lambda i: (0, i, 0)),
            pl.BlockSpec((1, queries * cands, width), lambda i: (i, 0, 0)),
        ],
        out_shape=[
            jax.ShapeDtypeStruct((cands, dirs, width), F32),
            jax.ShapeDtypeStruct((steps, queries * cands, width), F32),
        ],
        compiler_params=pltpu.CompilerParams(vmem_limit_bytes=16 * 2**20),
    )(*arrays, act_rot, eigenvalues, query_rotated)
    return rotated, jnp.sum(partial_scores, axis=(0, 2)).reshape(queries, cands)


def gather_body(acts, grads, act_basis, grad_basis, eigenvalues, query_rotated, example_ids, token_counts):
    lengths = candidate_lengths(example_ids, token_counts)
    local_act = local_activations(acts, act_basis, lengths)
    partial_value = jnp.einsum(
        "ctd,dj->ctj",
        lax.all_gather(grads, "row", axis=1, tiled=True),
        grad_basis,
        preferred_element_type=F32,
    )
    every_act = lax.all_gather(local_act, "row", axis=1, tiled=True)
    rotated_grads = lax.psum(partial_value, "col").astype(BF16)
    cands, seq = rotated_grads.shape[:2]
    arrays = [rotated_grads[c] for c in range(cands)]
    layout = tuple(((c, 0, seq),) for c in range(cands))
    rotated, scores = rotate_and_score(arrays, layout, every_act, eigenvalues, query_rotated)
    return rotated, lax.psum(scores, ("row", "col"))


def after(value, *earlier):
    return lax.optimization_barrier((value, *earlier))[0]


def project_kernel(ends, count, widths, *refs):
    flags, refs = refs[0], refs[1:]
    tokens, basis, out, acc = refs[:count], refs[count:-2], refs[-2], refs[-1]
    step = pl.program_id(0)
    def joined(refs):
        return jnp.concatenate([t[...] for t in refs], axis=0) if len(refs) > 1 else refs[0][...]

    rows = joined(tokens[:ends])
    if count > ends:
        rows = jnp.where(flags[0] == 1, rows, joined(tokens[ends:]))
    start, spans = 0, []
    for width in widths:
        spans.append((start, start + width))
        start += width

    @pl.when(step == 0)
    def _():
        acc[...] = jnp.zeros_like(acc)

    for ref, (a, b) in zip(basis, spans):
        acc[:, a:b] += jnp.dot(rows, ref[...], preferred_element_type=F32)

    @pl.when(step == pl.num_programs(0) - 1)
    def _():
        if len(basis) == 1:
            out[...] = acc[...].astype(BF16)
        else:
            (c, d), (e, f) = spans[-2:]
            if c > 0:
                out[:, :c] = acc[:, :c].astype(BF16)

            @pl.when(flags[1] == 0)
            def _():
                out[:, c:f] = acc[:, c:f].astype(BF16)

            @pl.when(flags[1] != 0)
            def _():
                out[:, c:d] = acc[:, e:f].astype(BF16)
                out[:, e:f] = acc[:, c:d].astype(BF16)


def project(flags, ends, middles, bases):
    tokens = ends + middles
    feats = bases[0].shape[0]
    widths = tuple(x.shape[1] for x in bases)
    block, total = 1024, sum(widths)
    rows = sum(n for _, _, n in ends)
    specs = []
    for _, start, n in tokens:
        assert start % n == 0
        specs.append(pl.BlockSpec((n, block), lambda k, i=start // n: (i, k)))
    return pl.pallas_call(
        functools.partial(project_kernel, len(ends), len(tokens), widths),
        grid=(feats // block,),
        in_specs=[pl.BlockSpec(memory_space=pltpu.SMEM)]
        + specs
        + [pl.BlockSpec((block, w), lambda k: (k, 0)) for w in widths],
        out_specs=pl.BlockSpec((rows, total), lambda k: (0, 0)),
        out_shape=jax.ShapeDtypeStruct((rows, total), BF16),
        scratch_shapes=[pltpu.VMEM((rows, total), F32)],
        compiler_params=pltpu.CompilerParams(vmem_limit_bytes=56 * 2**20),
        cost_estimate=pl.CostEstimate(
            flops=rows * feats * total // 8,
            bytes_accessed=feats * (total + rows) // 8,
            transcendentals=0,
        ),
    )(flags, *[array for array, _, _ in tokens], *bases)


def after(value, *earlier):
    return lax.optimization_barrier((value, *earlier))[0]


def exchange_sum(value, axis, size):
    total = value
    for d in range(1, size):
        total = total + lax.ppermute(value, axis, [(i, i ^ d) for i in range(size)])
    return total


def chain_body(acts, grads, act_basis, grad_basis, eigenvalues, query_rotated, example_ids, token_counts):
    cands, tok, feats = grads.shape
    dirs = grad_basis.shape[1]
    group, row, col = (lax.axis_index(a) for a in ("groups", "row", "col"))
    sides, planes, parts = 2, 4, 4
    middle, ends = [(1, 2), (2, 1)], [(0, 3), (3, 0)]
    beside = [(i, i ^ 1) for i in range(planes)]
    at_end = (row == 0) | (row == planes - 1)
    flags = jnp.stack([at_end.astype(jnp.int32), group.astype(jnp.int32)])

    half, flat = dirs // sides, grads.reshape(cands * tok, feats)
    units, deep, slab = 8, feats // 8, cands * tok // 8
    lengths = candidate_lengths(example_ids, token_counts)
    local_act = local_activations(acts, act_basis, lengths)
    near, far, other = [], [], []
    spans = [(0, 2), (2, 4), (4, 6), (6, 7), (7, units)]
    own_own = project(flags, [(flat, 0, cands * tok)], [], [grad_basis])
    for i, (a, b) in enumerate(spans):
        piece = lax.dynamic_slice(grad_basis, (a * deep, group * half), ((b - a) * deep, half))
        if i >= 2:
            early = {2: [own_own, local_act], 3: [other[0]], 4: []}[i]
            piece = after(piece, near[i - 2], *early)
        if i in (0, 2):
            part = flat[: 4 * slab] if i == 0 else after(flat[4 * slab :], near[0])
            other.append(lax.ppermute(part, "row", middle))
        near.append(lax.ppermute(piece, "row", beside))
        far.append(lax.ppermute(near[i], "groups", [(0, 1), (1, 0)]))
    near_basis = jnp.concatenate(near, axis=0)
    far_basis = jnp.concatenate(far, axis=0)

    ranges = [(0, 2), (2, 4), (4, 6), (6, units)]
    phase = [near[3], near[4], other[1]]
    ties = [[*phase, far[0], far[1]], [*phase, far[2], far[4]], [], []]
    partner = []
    for k, (a, b) in enumerate(ranges):
        tie = ties[k] + ([partner[k - 2]] if k >= 2 else [])
        piece = flat[a * slab : b * slab]
        partner.append(lax.ppermute(after(piece, *tie), "row", ends))

    sub, full = tok // parts, cands * tok

    def by_part(block):
        split = block.reshape(cands, parts, sub, -1)
        return jnp.stack(
            [lax.dynamic_index_in_dim(split, col ^ d, 1, keepdims=False) for d in (0, 2, 1, 3)]
        )

    every_act = lax.all_gather(after(local_act, partner[2]), "row", axis=0)
    act = [
        by_part(lax.dynamic_index_in_dim(every_act, i, 0, keepdims=False))
        for i in (row, row ^ 1, planes - 1 - row, planes - 1 - (row ^ 1))
    ]
    act_rot = [jnp.stack(act[i : i + 2], axis=1) for i in (0, 2)]
    act_rot = [jnp.moveaxis(x, 2, 0).reshape(cands, 2 * tok, -1) for x in act_rot]
    act_rot = jnp.concatenate(act_rot, axis=1)

    own_end = project(flags, [(flat, 0, full)], [], [near_basis, after(far_basis, partner[0])])
    outer = project(
        flags,
        [(partner[0], 0, 2 * slab), (partner[1], 0, 2 * slab)],
        [(other[0], 0, full // 2)],
        [grad_basis, near_basis, after(far_basis, own_end)],
    )

    def swap(value, axis, d):
        size = planes if axis == "row" else parts
        return lax.ppermute(value, axis, [(i, i ^ d) for i in range(size)])

    def scatter_sum(value):
        value = value.reshape(-1, parts, sub, 2 * dirs)
        total = lax.dynamic_index_in_dim(value, col, 1, keepdims=False).astype(F32)
        for d in range(1, parts):
            sent = lax.dynamic_index_in_dim(value, col ^ d, 1, keepdims=False)
            total = total + swap(sent, "col", d).astype(F32)
        return total.astype(BF16).reshape(-1, 2 * dirs)

    def gather(mine):
        pair = jnp.concatenate([mine, swap(mine, "col", 2)], axis=0)
        return [pair, swap(pair, "col", 1)]

    sums = [scatter_sum(jnp.concatenate([own_own, own_end], axis=1)), scatter_sum(outer)]
    for k in (2, 3):
        product = project(
            flags,
            [(partner[k], 0, tok)],
            [(other[1], (k - 2) * tok, tok)],
            [grad_basis, near_basis, after(far_basis, sums[-1])],
        )
        if k == 2:
            sums.append(scatter_sum(product))
            early = jnp.concatenate(sums, axis=0)
            got = swap(early[:, dirs:], "row", 1)
    early = jnp.concatenate([early[:, :dirs], after(got, product)], axis=0)
    last = scatter_sum(after(product, early))
    last = jnp.concatenate([last[:, :dirs], swap(last[:, dirs:], "row", 1)], axis=0)
    arrays = gather(early) + gather(last)
    segments = [[] for _ in range(cands)]
    for kind in (0, 1):
        for c in range(cands):
            for j in (0, 1):
                for side in (0, 1):
                    for plane in (0, 1):
                        base = (side * 2 + plane) * early.shape[0] // 2
                        if kind == 0:
                            segments[c].append((j, base + c * sub, sub))
                        elif c < cands - 1:
                            segments[c].append((j, base + (cands + c) * sub, sub))
                        else:
                            base = (side * 2 + plane) * last.shape[0] // 2
                            segments[c].append((2 + j, base, sub))
    layout = tuple(tuple(s) for s in segments)

    rotated, scores = rotate_and_score(arrays, layout, act_rot, eigenvalues, query_rotated)
    scores = exchange_sum(exchange_sum(scores, "col", parts), "row", planes)
    return rotated, scores


def solution(mesh):
    placed = (
        P("groups", "row", None),
        P("groups", "row", "col"),
        P(None, "col"),
        P("col", "row"),
        P("row", "col"),
        P(None, "row", "col"),
        P("groups"),
        P(),
    )
    chain = mesh.shape["groups"] == 2 and mesh.shape["row"] == 4 and mesh.shape["col"] == 4
    return jax.shard_map(
        chain_body if chain else gather_body,
        mesh=mesh,
        in_specs=placed,
        out_specs=(P("groups", "row", "col"), P(None, "groups")),
        check_vma=False,
    )
```

```python
import functools

import jax
import jax.numpy as jnp
from jax import lax
from jax.experimental import pallas as pl
from jax.experimental.pallas import tpu as pltpu
from jax.sharding import PartitionSpec as P

DAMPING = 0.05
BF16 = jnp.bfloat16
F32 = jnp.float32


def candidate_lengths(example_ids, token_counts):
    pool_size = token_counts.shape[0]
    hits = example_ids[:, None] == jnp.arange(pool_size, dtype=jnp.int32)[None, :]
    return jnp.sum(jnp.where(hits, token_counts[None, :], 0), axis=1)


def local_activations(acts, act_basis, lengths):
    tok = acts.shape[1]
    positions = lax.axis_index("row") * tok + jnp.arange(tok, dtype=jnp.int32)
    live = (positions[None, :] < lengths[:, None]).astype(F32)
    rotated = jnp.einsum("ctd,dk->ctk", acts, act_basis, preferred_element_type=F32)
    return (rotated * live[:, :, None]).astype(BF16)


def final_kernel(layout, count, *refs):
    arrays = refs[:count]
    act_ref, eig_ref, query_ref, out_ref, score_ref = refs[count:]
    queries = query_ref.shape[0]
    damped = eig_ref[...] + DAMPING
    weights = [query_ref[q].astype(F32) / damped for q in range(queries)]
    rows = [[] for _ in range(queries)]
    for c, segments in enumerate(layout):
        tokens = jnp.concatenate([arrays[i][s : s + n] for i, s, n in segments], axis=0)
        tile = lax.dot_general(
            tokens, act_ref[c], (((0,), (0,)), ((), ())), preferred_element_type=F32
        )
        out_ref[c] = tile
        for q in range(queries):
            rows[q].append(jnp.sum(weights[q] * tile, axis=0, keepdims=True))
    score_ref[0] = jnp.concatenate([r for one in rows for r in one], axis=0)


def rotate_and_score(arrays, layout, act_rot, eigenvalues, query_rotated):
    cands, seq, width = act_rot.shape
    dirs = eigenvalues.shape[0]
    queries = query_rotated.shape[0]
    block = min(dirs, 256)
    steps = dirs // block
    rotated, partial_scores = pl.pallas_call(
        functools.partial(final_kernel, layout, len(arrays)),
        grid=(steps,),
        in_specs=[pl.BlockSpec((x.shape[0], block), lambda i: (0, i)) for x in arrays]
        + [
            pl.BlockSpec((cands, seq, width), lambda i: (0, 0, 0)),
            pl.BlockSpec((block, width), lambda i: (i, 0)),
            pl.BlockSpec((queries, block, width), lambda i: (0, i, 0)),
        ],
        out_specs=[
            pl.BlockSpec((cands, block, width), lambda i: (0, i, 0)),
            pl.BlockSpec((1, queries * cands, width), lambda i: (i, 0, 0)),
        ],
        out_shape=[
            jax.ShapeDtypeStruct((cands, dirs, width), F32),
            jax.ShapeDtypeStruct((steps, queries * cands, width), F32),
        ],
        compiler_params=pltpu.CompilerParams(vmem_limit_bytes=16 * 2**20),
    )(*arrays, act_rot, eigenvalues, query_rotated)
    return rotated, jnp.sum(partial_scores, axis=(0, 2)).reshape(queries, cands)


def gather_body(acts, grads, act_basis, grad_basis, eigenvalues, query_rotated, example_ids, token_counts):
    lengths = candidate_lengths(example_ids, token_counts)
    local_act = local_activations(acts, act_basis, lengths)
    partial_value = jnp.einsum(
        "ctd,dj->ctj",
        lax.all_gather(grads, "row", axis=1, tiled=True),
        grad_basis,
        preferred_element_type=F32,
    )
    every_act = lax.all_gather(local_act, "row", axis=1, tiled=True)
    rotated_grads = lax.psum(partial_value, "col").astype(BF16)
    cands, seq = rotated_grads.shape[:2]
    arrays = [rotated_grads[c] for c in range(cands)]
    layout = tuple(((c, 0, seq),) for c in range(cands))
    rotated, scores = rotate_and_score(arrays, layout, every_act, eigenvalues, query_rotated)
    return rotated, lax.psum(scores, ("row", "col"))


def after(value, *earlier):
    return lax.optimization_barrier((value, *earlier))[0]


def project_kernel(ends, count, widths, *refs):
    flags, refs = refs[0], refs[1:]
    tokens, basis, out, acc = refs[:count], refs[count:-2], refs[-2], refs[-1]
    step = pl.program_id(0)
    def joined(refs):
        return jnp.concatenate([t[...] for t in refs], axis=0) if len(refs) > 1 else refs[0][...]

    rows = joined(tokens[:ends])
    if count > ends:
        rows = jnp.where(flags[0] == 1, rows, joined(tokens[ends:]))
    start, spans = 0, []
    for width in widths:
        spans.append((start, start + width))
        start += width

    @pl.when(step == 0)
    def _():
        acc[...] = jnp.zeros_like(acc)

    for ref, (a, b) in zip(basis, spans):
        acc[:, a:b] += jnp.dot(rows, ref[...], preferred_element_type=F32)

    @pl.when(step == pl.num_programs(0) - 1)
    def _():
        if len(basis) == 1:
            out[...] = acc[...].astype(BF16)
        else:
            (c, d), (e, f) = spans[-2:]
            if c > 0:
                out[:, :c] = acc[:, :c].astype(BF16)

            @pl.when(flags[1] == 0)
            def _():
                out[:, c:f] = acc[:, c:f].astype(BF16)

            @pl.when(flags[1] != 0)
            def _():
                out[:, c:d] = acc[:, e:f].astype(BF16)
                out[:, e:f] = acc[:, c:d].astype(BF16)


def project(flags, ends, middles, bases):
    tokens = ends + middles
    feats = bases[0].shape[0]
    widths = tuple(x.shape[1] for x in bases)
    block, total = 1024, sum(widths)
    rows = sum(n for _, _, n in ends)
    specs = []
    for _, start, n in tokens:
        assert start % n == 0
        specs.append(pl.BlockSpec((n, block), lambda k, i=start // n: (i, k)))
    return pl.pallas_call(
        functools.partial(project_kernel, len(ends), len(tokens), widths),
        grid=(feats // block,),
        in_specs=[pl.BlockSpec(memory_space=pltpu.SMEM)]
        + specs
        + [pl.BlockSpec((block, w), lambda k: (k, 0)) for w in widths],
        out_specs=pl.BlockSpec((rows, total), lambda k: (0, 0)),
        out_shape=jax.ShapeDtypeStruct((rows, total), BF16),
        scratch_shapes=[pltpu.VMEM((rows, total), F32)],
        compiler_params=pltpu.CompilerParams(vmem_limit_bytes=56 * 2**20),
        cost_estimate=pl.CostEstimate(
            flops=rows * feats * total // 8,
            bytes_accessed=feats * (total + rows) // 8,
            transcendentals=0,
        ),
    )(flags, *[array for array, _, _ in tokens], *bases)


def after(value, *earlier):
    return lax.optimization_barrier((value, *earlier))[0]


def exchange_sum(value, axis, size):
    total = value
    for d in range(1, size):
        total = total + lax.ppermute(value, axis, [(i, i ^ d) for i in range(size)])
    return total


def chain_body(acts, grads, act_basis, grad_basis, eigenvalues, query_rotated, example_ids, token_counts):
    cands, tok, feats = grads.shape
    dirs = grad_basis.shape[1]
    group, row, col = (lax.axis_index(a) for a in ("groups", "row", "col"))
    sides, planes, parts = 2, 4, 4
    middle, ends = [(1, 2), (2, 1)], [(0, 3), (3, 0)]
    beside = [(i, i ^ 1) for i in range(planes)]
    at_end = (row == 0) | (row == planes - 1)
    flags = jnp.stack([at_end.astype(jnp.int32), group.astype(jnp.int32)])

    half, flat = dirs // sides, grads.reshape(cands * tok, feats)
    units, deep, slab = 8, feats // 8, cands * tok // 8
    lengths = candidate_lengths(example_ids, token_counts)
    local_act = local_activations(acts, act_basis, lengths)
    near, far, other = [], [], []
    spans = [(0, 2), (2, 4), (4, 6), (6, 7), (7, units)]
    own_own = project(flags, [(flat, 0, cands * tok)], [], [grad_basis])
    for i, (a, b) in enumerate(spans):
        piece = lax.dynamic_slice(grad_basis, (a * deep, group * half), ((b - a) * deep, half))
        if i >= 2:
            early = {2: [own_own, local_act], 3: [other[0], far[0]], 4: [far[1]]}[i]
            piece = after(piece, near[i - 2], *early)
        if i in (0, 2):
            part = flat[: 4 * slab] if i == 0 else after(flat[4 * slab :], near[0])
            other.append(lax.ppermute(part, "row", middle))
        near.append(lax.ppermute(piece, "row", beside))
        far.append(lax.ppermute(near[i], "groups", [(0, 1), (1, 0)]))
    near_basis = jnp.concatenate(near, axis=0)
    far_basis = jnp.concatenate(far, axis=0)

    ranges = [(0, 2), (2, 4), (4, 6), (6, units)]
    phase = [near[3], near[4], other[1]]
    ties = [[*phase, far[0]], [*phase, far[2]], [far[3], far[4]], []]
    partner = []
    for k, (a, b) in enumerate(ranges):
        tie = ties[k] + ([partner[k - 2]] if k >= 2 else [])
        piece = flat[a * slab : b * slab]
        partner.append(lax.ppermute(after(piece, *tie), "row", ends))

    sub, full = tok // parts, cands * tok

    every_act = lax.all_gather(after(local_act, partner[2]), "row", axis=0)

    own_end = project(flags, [(flat, 0, full)], [], [near_basis, after(far_basis, partner[0])])
    outer = project(
        flags,
        [(partner[0], 0, 2 * slab), (partner[1], 0, 2 * slab)],
        [(other[0], 0, full // 2)],
        [grad_basis, near_basis, after(far_basis, own_end)],
    )

    def swap(value, axis, d):
        size = planes if axis == "row" else parts
        return lax.ppermute(value, axis, [(i, i ^ d) for i in range(size)])

    def scatter_sum(value):
        value = value.reshape(-1, parts, sub, 2 * dirs)
        total = lax.dynamic_index_in_dim(value, col, 1, keepdims=False).astype(F32)
        for d in range(1, parts):
            sent = lax.dynamic_index_in_dim(value, col ^ d, 1, keepdims=False)
            total = total + swap(sent, "col", d).astype(F32)
        return total.astype(BF16).reshape(-1, 2 * dirs)

    def gather(mine, *earlier):
        pair = jnp.concatenate([mine, after(swap(mine, "col", 2), *earlier)], axis=0)
        return [pair, swap(pair, "col", 1)]

    sums = [scatter_sum(jnp.concatenate([own_own, own_end], axis=1)), scatter_sum(outer)]
    for k in (2, 3):
        product = project(
            flags,
            [(partner[k], 0, tok)],
            [(other[1], (k - 2) * tok, tok)],
            [grad_basis, near_basis, after(far_basis, sums[-1])],
        )
        if k == 2:
            sums.append(scatter_sum(product))
            early = jnp.concatenate(sums, axis=0)
            got = swap(early[:, dirs:], "row", 1)
    early_own = gather(early[:, :dirs])
    last = scatter_sum(after(product, got, *early_own))
    got = after(got, last)
    last = after(last, every_act)
    last = jnp.concatenate([last[:, :dirs], swap(last[:, dirs:], "row", 1)], axis=0)
    early_got = gather(got, last)
    arrays = early_own + early_got + gather(last)
    every_act = after(every_act, last)

    def by_part(block):
        split = block.reshape(cands, parts, sub, -1)
        return jnp.stack(
            [lax.dynamic_index_in_dim(split, col ^ d, 1, keepdims=False) for d in (0, 2, 1, 3)]
        )

    act = [
        by_part(lax.dynamic_index_in_dim(every_act, i, 0, keepdims=False))
        for i in (row, row ^ 1, planes - 1 - row, planes - 1 - (row ^ 1))
    ]
    act_rot = [jnp.stack(act[i : i + 2], axis=1) for i in (0, 2)]
    act_rot = [jnp.moveaxis(x, 2, 0).reshape(cands, 2 * tok, -1) for x in act_rot]
    act_rot = jnp.concatenate(act_rot, axis=1)

    segments = [[] for _ in range(cands)]
    for kind in (0, 1):
        for c in range(cands):
            for j in (0, 1):
                for side in (0, 1):
                    for plane in (0, 1):
                        base = side * early.shape[0]
                        if kind == 0:
                            segments[c].append((2 * plane + j, base + c * sub, sub))
                        elif c < cands - 1:
                            segments[c].append((2 * plane + j, base + (cands + c) * sub, sub))
                        else:
                            segments[c].append((4 + j, (side * 2 + plane) * sub, sub))
    layout = tuple(tuple(s) for s in segments)

    rotated, scores = rotate_and_score(arrays, layout, act_rot, eigenvalues, query_rotated)
    scores = exchange_sum(exchange_sum(scores, "col", parts), "row", planes)
    return rotated, scores


def solution(mesh):
    placed = (
        P("groups", "row", None),
        P("groups", "row", "col"),
        P(None, "col"),
        P("col", "row"),
        P("row", "col"),
        P(None, "row", "col"),
        P("groups"),
        P(),
    )
    chain = mesh.shape["groups"] == 2 and mesh.shape["row"] == 4 and mesh.shape["col"] == 4
    return jax.shard_map(
        chain_body if chain else gather_body,
        mesh=mesh,
        in_specs=placed,
        out_specs=(P("groups", "row", "col"), P(None, "groups")),
        check_vma=False,
    )
```

```python
import functools

import jax
import jax.numpy as jnp
from jax import lax
from jax.experimental import pallas as pl
from jax.experimental.pallas import tpu as pltpu
from jax.sharding import PartitionSpec as P

DAMPING = 0.05
BF16 = jnp.bfloat16
F32 = jnp.float32


def candidate_lengths(example_ids, token_counts):
    pool_size = token_counts.shape[0]
    hits = example_ids[:, None] == jnp.arange(pool_size, dtype=jnp.int32)[None, :]
    return jnp.sum(jnp.where(hits, token_counts[None, :], 0), axis=1)


def local_activations(acts, act_basis, lengths):
    tok = acts.shape[1]
    positions = lax.axis_index("row") * tok + jnp.arange(tok, dtype=jnp.int32)
    live = (positions[None, :] < lengths[:, None]).astype(F32)
    rotated = jnp.einsum("ctd,dk->ctk", acts, act_basis, preferred_element_type=F32)
    return (rotated * live[:, :, None]).astype(BF16)


def final_kernel(layout, count, *refs):
    arrays = refs[:count]
    act_ref, eig_ref, query_ref, out_ref, score_ref = refs[count:]
    queries = query_ref.shape[0]
    damped = eig_ref[...] + DAMPING
    weights = [query_ref[q].astype(F32) / damped for q in range(queries)]
    rows = [[] for _ in range(queries)]
    for c, segments in enumerate(layout):
        tokens = jnp.concatenate([arrays[i][s : s + n] for i, s, n in segments], axis=0)
        tile = lax.dot_general(
            tokens, act_ref[c], (((0,), (0,)), ((), ())), preferred_element_type=F32
        )
        out_ref[c] = tile
        for q in range(queries):
            rows[q].append(jnp.sum(weights[q] * tile, axis=0, keepdims=True))
    score_ref[0] = jnp.concatenate([r for one in rows for r in one], axis=0)


def rotate_and_score(arrays, layout, act_rot, eigenvalues, query_rotated):
    cands, seq, width = act_rot.shape
    dirs = eigenvalues.shape[0]
    queries = query_rotated.shape[0]
    block = min(dirs, 256)
    steps = dirs // block
    rotated, partial_scores = pl.pallas_call(
        functools.partial(final_kernel, layout, len(arrays)),
        grid=(steps,),
        in_specs=[pl.BlockSpec((x.shape[0], block), lambda i: (0, i)) for x in arrays]
        + [
            pl.BlockSpec((cands, seq, width), lambda i: (0, 0, 0)),
            pl.BlockSpec((block, width), lambda i: (i, 0)),
            pl.BlockSpec((queries, block, width), lambda i: (0, i, 0)),
        ],
        out_specs=[
            pl.BlockSpec((cands, block, width), lambda i: (0, i, 0)),
            pl.BlockSpec((1, queries * cands, width), lambda i: (i, 0, 0)),
        ],
        out_shape=[
            jax.ShapeDtypeStruct((cands, dirs, width), F32),
            jax.ShapeDtypeStruct((steps, queries * cands, width), F32),
        ],
        compiler_params=pltpu.CompilerParams(vmem_limit_bytes=16 * 2**20),
    )(*arrays, act_rot, eigenvalues, query_rotated)
    return rotated, jnp.sum(partial_scores, axis=(0, 2)).reshape(queries, cands)


def gather_body(acts, grads, act_basis, grad_basis, eigenvalues, query_rotated, example_ids, token_counts):
    lengths = candidate_lengths(example_ids, token_counts)
    local_act = local_activations(acts, act_basis, lengths)
    partial_value = jnp.einsum(
        "ctd,dj->ctj",
        lax.all_gather(grads, "row", axis=1, tiled=True),
        grad_basis,
        preferred_element_type=F32,
    )
    every_act = lax.all_gather(local_act, "row", axis=1, tiled=True)
    rotated_grads = lax.psum(partial_value, "col").astype(BF16)
    cands, seq = rotated_grads.shape[:2]
    arrays = [rotated_grads[c] for c in range(cands)]
    layout = tuple(((c, 0, seq),) for c in range(cands))
    rotated, scores = rotate_and_score(arrays, layout, every_act, eigenvalues, query_rotated)
    return rotated, lax.psum(scores, ("row", "col"))


def after(value, *earlier):
    return lax.optimization_barrier((value, *earlier))[0]


def project_kernel(ends, count, widths, *refs):
    flags, refs = refs[0], refs[1:]
    tokens, basis, out, acc = refs[:count], refs[count:-2], refs[-2], refs[-1]
    step = pl.program_id(0)
    def joined(refs):
        return jnp.concatenate([t[...] for t in refs], axis=0) if len(refs) > 1 else refs[0][...]

    rows = joined(tokens[:ends])
    if count > ends:
        rows = jnp.where(flags[0] == 1, rows, joined(tokens[ends:]))
    start, spans = 0, []
    for width in widths:
        spans.append((start, start + width))
        start += width

    @pl.when(step == 0)
    def _():
        acc[...] = jnp.zeros_like(acc)

    for ref, (a, b) in zip(basis, spans):
        acc[:, a:b] += jnp.dot(rows, ref[...], preferred_element_type=F32)

    @pl.when(step == pl.num_programs(0) - 1)
    def _():
        if len(basis) == 1:
            out[...] = acc[...].astype(BF16)
        else:
            (c, d), (e, f) = spans[-2:]
            if c > 0:
                out[:, :c] = acc[:, :c].astype(BF16)

            @pl.when(flags[1] == 0)
            def _():
                out[:, c:f] = acc[:, c:f].astype(BF16)

            @pl.when(flags[1] != 0)
            def _():
                out[:, c:d] = acc[:, e:f].astype(BF16)
                out[:, e:f] = acc[:, c:d].astype(BF16)


def project(flags, ends, middles, bases):
    tokens = ends + middles
    feats = bases[0].shape[0]
    widths = tuple(x.shape[1] for x in bases)
    block, total = 1024, sum(widths)
    rows = sum(n for _, _, n in ends)
    specs = []
    for _, start, n in tokens:
        assert start % n == 0
        specs.append(pl.BlockSpec((n, block), lambda k, i=start // n: (i, k)))
    return pl.pallas_call(
        functools.partial(project_kernel, len(ends), len(tokens), widths),
        grid=(feats // block,),
        in_specs=[pl.BlockSpec(memory_space=pltpu.SMEM)]
        + specs
        + [pl.BlockSpec((block, w), lambda k: (k, 0)) for w in widths],
        out_specs=pl.BlockSpec((rows, total), lambda k: (0, 0)),
        out_shape=jax.ShapeDtypeStruct((rows, total), BF16),
        scratch_shapes=[pltpu.VMEM((rows, total), F32)],
        compiler_params=pltpu.CompilerParams(vmem_limit_bytes=56 * 2**20),
        cost_estimate=pl.CostEstimate(
            flops=rows * feats * total // 8,
            bytes_accessed=feats * (total + rows) // 8,
            transcendentals=0,
        ),
    )(flags, *[array for array, _, _ in tokens], *bases)


def after(value, *earlier):
    return lax.optimization_barrier((value, *earlier))[0]


def exchange_sum(value, axis, size):
    total = value
    for d in range(1, size):
        total = total + lax.ppermute(value, axis, [(i, i ^ d) for i in range(size)])
    return total


def chain_body(acts, grads, act_basis, grad_basis, eigenvalues, query_rotated, example_ids, token_counts):
    cands, tok, feats = grads.shape
    dirs = grad_basis.shape[1]
    group, row, col = (lax.axis_index(a) for a in ("groups", "row", "col"))
    sides, planes, parts = 2, 4, 4
    middle, ends = [(1, 2), (2, 1)], [(0, 3), (3, 0)]
    beside = [(i, i ^ 1) for i in range(planes)]
    at_end = (row == 0) | (row == planes - 1)
    flags = jnp.stack([at_end.astype(jnp.int32), group.astype(jnp.int32)])

    half, flat = dirs // sides, grads.reshape(cands * tok, feats)
    units, deep, slab = 8, feats // 8, cands * tok // 8
    lengths = candidate_lengths(example_ids, token_counts)
    local_act = local_activations(acts, act_basis, lengths)
    near, far, other = [], [], []
    spans = [(0, 1), (1, 3), (3, 5), (5, 7), (7, units)]
    own_own = project(flags, [(flat, 0, cands * tok)], [], [grad_basis])
    for i, (a, b) in enumerate(spans):
        piece = lax.dynamic_slice(grad_basis, (a * deep, group * half), ((b - a) * deep, half))
        if i >= 2:
            early = {2: [own_own, local_act], 3: [other[0]], 4: []}[i]
            piece = after(piece, near[i - 2], *early)
        if i in (0, 2):
            part = flat[: 4 * slab] if i == 0 else after(flat[4 * slab :], near[0])
            other.append(lax.ppermute(part, "row", middle))
        near.append(lax.ppermute(piece, "row", beside))
        far.append(lax.ppermute(near[i], "groups", [(0, 1), (1, 0)]))
    near_basis = jnp.concatenate(near, axis=0)
    far_basis = jnp.concatenate(far, axis=0)

    ranges = [(0, 2), (2, 4), (4, 6), (6, units)]
    phase = [near[3], near[4], other[1]]
    ties = [[*phase, far[0], far[1]], [*phase, far[2]], [far[4]], []]
    partner = []
    for k, (a, b) in enumerate(ranges):
        tie = ties[k] + ([partner[k - 2]] if k >= 2 else [])
        piece = flat[a * slab : b * slab]
        partner.append(lax.ppermute(after(piece, *tie), "row", ends))

    sub, full = tok // parts, cands * tok

    every_act = lax.all_gather(after(local_act, partner[2]), "row", axis=0)

    own_end = project(flags, [(flat, 0, full)], [], [near_basis, after(far_basis, partner[0])])
    outer = project(
        flags,
        [(partner[0], 0, 2 * slab), (partner[1], 0, 2 * slab)],
        [(other[0], 0, full // 2)],
        [grad_basis, near_basis, after(far_basis, own_end)],
    )

    def swap(value, axis, d):
        size = planes if axis == "row" else parts
        return lax.ppermute(value, axis, [(i, i ^ d) for i in range(size)])

    def scatter_sum(value):
        value = value.reshape(-1, parts, sub, 2 * dirs)
        total = lax.dynamic_index_in_dim(value, col, 1, keepdims=False).astype(F32)
        for d in range(1, parts):
            sent = lax.dynamic_index_in_dim(value, col ^ d, 1, keepdims=False)
            total = total + swap(sent, "col", d).astype(F32)
        return total.astype(BF16).reshape(-1, 2 * dirs)

    def gather(mine, *earlier):
        pair = jnp.concatenate([mine, after(swap(mine, "col", 2), *earlier)], axis=0)
        return [pair, swap(pair, "col", 1)]

    sums = [scatter_sum(jnp.concatenate([own_own, own_end], axis=1)), scatter_sum(outer)]
    for k in (2, 3):
        product = project(
            flags,
            [(partner[k], 0, tok)],
            [(other[1], (k - 2) * tok, tok)],
            [grad_basis, near_basis, after(far_basis, sums[-1])],
        )
        if k == 2:
            sums.append(scatter_sum(product))
            early = jnp.concatenate(sums, axis=0)
            got = swap(early[:, dirs:], "row", 1)
    early_own = gather(early[:, :dirs])
    last = scatter_sum(after(product, got, *early_own))
    got = after(got, last)
    last = after(last, every_act)
    last = jnp.concatenate([last[:, :dirs], swap(last[:, dirs:], "row", 1)], axis=0)
    early_got = gather(got, last)
    arrays = early_own + early_got + gather(last)
    every_act = after(every_act, last)

    def by_part(block):
        split = block.reshape(cands, parts, sub, -1)
        return jnp.stack(
            [lax.dynamic_index_in_dim(split, col ^ d, 1, keepdims=False) for d in (0, 2, 1, 3)]
        )

    act = [
        by_part(lax.dynamic_index_in_dim(every_act, i, 0, keepdims=False))
        for i in (row, row ^ 1, planes - 1 - row, planes - 1 - (row ^ 1))
    ]
    act_rot = [jnp.stack(act[i : i + 2], axis=1) for i in (0, 2)]
    act_rot = [jnp.moveaxis(x, 2, 0).reshape(cands, 2 * tok, -1) for x in act_rot]
    act_rot = jnp.concatenate(act_rot, axis=1)

    segments = [[] for _ in range(cands)]
    for kind in (0, 1):
        for c in range(cands):
            for j in (0, 1):
                for side in (0, 1):
                    for plane in (0, 1):
                        base = side * early.shape[0]
                        if kind == 0:
                            segments[c].append((2 * plane + j, base + c * sub, sub))
                        elif c < cands - 1:
                            segments[c].append((2 * plane + j, base + (cands + c) * sub, sub))
                        else:
                            segments[c].append((4 + j, (side * 2 + plane) * sub, sub))
    layout = tuple(tuple(s) for s in segments)

    rotated, scores = rotate_and_score(arrays, layout, act_rot, eigenvalues, query_rotated)
    scores = exchange_sum(exchange_sum(scores, "col", parts), "row", planes)
    return rotated, scores


def solution(mesh):
    placed = (
        P("groups", "row", None),
        P("groups", "row", "col"),
        P(None, "col"),
        P("col", "row"),
        P("row", "col"),
        P(None, "row", "col"),
        P("groups"),
        P(),
    )
    chain = mesh.shape["groups"] == 2 and mesh.shape["row"] == 4 and mesh.shape["col"] == 4
    return jax.shard_map(
        chain_body if chain else gather_body,
        mesh=mesh,
        in_specs=placed,
        out_specs=(P("groups", "row", "col"), P(None, "groups")),
        check_vma=False,
    )
```

```python
import functools

import jax
import jax.numpy as jnp
from jax import lax
from jax.experimental import pallas as pl
from jax.experimental.pallas import tpu as pltpu
from jax.sharding import PartitionSpec as P

DAMPING = 0.05
BF16 = jnp.bfloat16
F32 = jnp.float32


def candidate_lengths(example_ids, token_counts):
    pool_size = token_counts.shape[0]
    hits = example_ids[:, None] == jnp.arange(pool_size, dtype=jnp.int32)[None, :]
    return jnp.sum(jnp.where(hits, token_counts[None, :], 0), axis=1)


def local_activations(acts, act_basis, lengths):
    tok = acts.shape[1]
    positions = lax.axis_index("row") * tok + jnp.arange(tok, dtype=jnp.int32)
    live = (positions[None, :] < lengths[:, None]).astype(F32)
    rotated = jnp.einsum("ctd,dk->ctk", acts, act_basis, preferred_element_type=F32)
    return (rotated * live[:, :, None]).astype(BF16)


def final_kernel(layout, count, *refs):
    arrays = refs[:count]
    act_ref, eig_ref, query_ref, out_ref, score_ref = refs[count:]
    queries = query_ref.shape[0]
    damped = eig_ref[...] + DAMPING
    weights = [query_ref[q].astype(F32) / damped for q in range(queries)]
    rows = [[] for _ in range(queries)]
    for c, segments in enumerate(layout):
        tokens = jnp.concatenate([arrays[i][s : s + n] for i, s, n in segments], axis=0)
        tile = lax.dot_general(
            tokens, act_ref[c], (((0,), (0,)), ((), ())), preferred_element_type=F32
        )
        out_ref[c] = tile
        for q in range(queries):
            rows[q].append(jnp.sum(weights[q] * tile, axis=0, keepdims=True))
    score_ref[0] = jnp.concatenate([r for one in rows for r in one], axis=0)


def rotate_and_score(arrays, layout, act_rot, eigenvalues, query_rotated):
    cands, seq, width = act_rot.shape
    dirs = eigenvalues.shape[0]
    queries = query_rotated.shape[0]
    block = min(dirs, 256)
    steps = dirs // block
    rotated, partial_scores = pl.pallas_call(
        functools.partial(final_kernel, layout, len(arrays)),
        grid=(steps,),
        in_specs=[pl.BlockSpec((x.shape[0], block), lambda i: (0, i)) for x in arrays]
        + [
            pl.BlockSpec((cands, seq, width), lambda i: (0, 0, 0)),
            pl.BlockSpec((block, width), lambda i: (i, 0)),
            pl.BlockSpec((queries, block, width), lambda i: (0, i, 0)),
        ],
        out_specs=[
            pl.BlockSpec((cands, block, width), lambda i: (0, i, 0)),
            pl.BlockSpec((1, queries * cands, width), lambda i: (i, 0, 0)),
        ],
        out_shape=[
            jax.ShapeDtypeStruct((cands, dirs, width), F32),
            jax.ShapeDtypeStruct((steps, queries * cands, width), F32),
        ],
        compiler_params=pltpu.CompilerParams(vmem_limit_bytes=16 * 2**20),
    )(*arrays, act_rot, eigenvalues, query_rotated)
    return rotated, jnp.sum(partial_scores, axis=(0, 2)).reshape(queries, cands)


def gather_body(acts, grads, act_basis, grad_basis, eigenvalues, query_rotated, example_ids, token_counts):
    lengths = candidate_lengths(example_ids, token_counts)
    local_act = local_activations(acts, act_basis, lengths)
    partial_value = jnp.einsum(
        "ctd,dj->ctj",
        lax.all_gather(grads, "row", axis=1, tiled=True),
        grad_basis,
        preferred_element_type=F32,
    )
    every_act = lax.all_gather(local_act, "row", axis=1, tiled=True)
    rotated_grads = lax.psum(partial_value, "col").astype(BF16)
    cands, seq = rotated_grads.shape[:2]
    arrays = [rotated_grads[c] for c in range(cands)]
    layout = tuple(((c, 0, seq),) for c in range(cands))
    rotated, scores = rotate_and_score(arrays, layout, every_act, eigenvalues, query_rotated)
    return rotated, lax.psum(scores, ("row", "col"))


def after(value, *earlier):
    return lax.optimization_barrier((value, *earlier))[0]


def project_kernel(ends, count, widths, *refs):
    flags, refs = refs[0], refs[1:]
    tokens, basis, out, acc = refs[:count], refs[count:-2], refs[-2], refs[-1]
    step = pl.program_id(0)
    def joined(refs):
        return jnp.concatenate([t[...] for t in refs], axis=0) if len(refs) > 1 else refs[0][...]

    rows = joined(tokens[:ends])
    if count > ends:
        rows = jnp.where(flags[0] == 1, rows, joined(tokens[ends:]))
    start, spans = 0, []
    for width in widths:
        spans.append((start, start + width))
        start += width

    @pl.when(step == 0)
    def _():
        acc[...] = jnp.zeros_like(acc)

    for ref, (a, b) in zip(basis, spans):
        acc[:, a:b] += jnp.dot(rows, ref[...], preferred_element_type=F32)

    @pl.when(step == pl.num_programs(0) - 1)
    def _():
        if len(basis) == 1:
            out[...] = acc[...].astype(BF16)
        else:
            (c, d), (e, f) = spans[-2:]
            if c > 0:
                out[:, :c] = acc[:, :c].astype(BF16)

            @pl.when(flags[1] == 0)
            def _():
                out[:, c:f] = acc[:, c:f].astype(BF16)

            @pl.when(flags[1] != 0)
            def _():
                out[:, c:d] = acc[:, e:f].astype(BF16)
                out[:, e:f] = acc[:, c:d].astype(BF16)


def project(flags, ends, middles, bases, weight=8):
    tokens = ends + middles
    feats = bases[0].shape[0]
    widths = tuple(x.shape[1] for x in bases)
    block, total = 1024, sum(widths)
    rows = sum(n for _, _, n in ends)
    specs = []
    for _, start, n in tokens:
        assert start % n == 0
        specs.append(pl.BlockSpec((n, block), lambda k, i=start // n: (i, k)))
    return pl.pallas_call(
        functools.partial(project_kernel, len(ends), len(tokens), widths),
        grid=(feats // block,),
        in_specs=[pl.BlockSpec(memory_space=pltpu.SMEM)]
        + specs
        + [pl.BlockSpec((block, w), lambda k: (k, 0)) for w in widths],
        out_specs=pl.BlockSpec((rows, total), lambda k: (0, 0)),
        out_shape=jax.ShapeDtypeStruct((rows, total), BF16),
        scratch_shapes=[pltpu.VMEM((rows, total), F32)],
        compiler_params=pltpu.CompilerParams(vmem_limit_bytes=56 * 2**20),
        cost_estimate=pl.CostEstimate(
            flops=rows * feats * total // weight,
            bytes_accessed=feats * (total + rows) // weight,
            transcendentals=0,
        ),
    )(flags, *[array for array, _, _ in tokens], *bases)


def after(value, *earlier):
    return lax.optimization_barrier((value, *earlier))[0]


def exchange_sum(value, axis, size):
    total = value
    for d in range(1, size):
        total = total + lax.ppermute(value, axis, [(i, i ^ d) for i in range(size)])
    return total


def chain_body(acts, grads, act_basis, grad_basis, eigenvalues, query_rotated, example_ids, token_counts):
    cands, tok, feats = grads.shape
    dirs = grad_basis.shape[1]
    group, row, col = (lax.axis_index(a) for a in ("groups", "row", "col"))
    sides, planes, parts = 2, 4, 4
    middle, ends = [(1, 2), (2, 1)], [(0, 3), (3, 0)]
    beside = [(i, i ^ 1) for i in range(planes)]
    at_end = (row == 0) | (row == planes - 1)
    flags = jnp.stack([at_end.astype(jnp.int32), group.astype(jnp.int32)])

    half, flat = dirs // sides, grads.reshape(cands * tok, feats)
    units, deep, slab = 8, feats // 8, cands * tok // 8
    lengths = candidate_lengths(example_ids, token_counts)
    local_act = local_activations(acts, act_basis, lengths)
    near, far, other = [], [], []
    spans = [(0, 1), (1, 3), (3, 5), (5, 7), (7, units)]
    own_own = project(flags, [(flat, 0, cands * tok)], [], [grad_basis])
    for i, (a, b) in enumerate(spans):
        piece = lax.dynamic_slice(grad_basis, (a * deep, group * half), ((b - a) * deep, half))
        if i >= 2:
            early = {2: [own_own, local_act], 3: [other[0]], 4: []}[i]
            piece = after(piece, near[i - 2], *early)
        if i in (0, 2):
            part = flat[: 4 * slab] if i == 0 else after(flat, near[0])[4 * slab :]
            other.append(lax.ppermute(part, "row", middle))
        near.append(lax.ppermute(piece, "row", beside))
        far.append(lax.ppermute(near[i], "groups", [(0, 1), (1, 0)]))
    near_basis = jnp.concatenate(near, axis=0)
    far_basis = jnp.concatenate(far, axis=0)

    ranges = [(0, 2), (2, 4), (4, 6), (6, units)]
    phase = [near[3], near[4], other[1]]
    ties = [[*phase, far[0], far[1]], [*phase, far[2]], [far[4]], []]
    partner = []
    for k, (a, b) in enumerate(ranges):
        tie = ties[k] + ([partner[k - 2]] if k >= 2 else [])
        piece = flat[a * slab : b * slab]
        partner.append(lax.ppermute(after(piece, *tie), "row", ends))

    sub, full = tok // parts, cands * tok

    every_act = lax.all_gather(after(local_act, partner[2]), "row", axis=0)

    own_end = project(flags, [(flat, 0, full)], [], [near_basis, after(far_basis, partner[0])])
    outer = project(
        flags,
        [(partner[0], 0, 2 * slab), (partner[1], 0, 2 * slab)],
        [(other[0], 0, full // 2)],
        [grad_basis, near_basis, after(far_basis, own_end)],
    )

    def swap(value, axis, d):
        size = planes if axis == "row" else parts
        return lax.ppermute(value, axis, [(i, i ^ d) for i in range(size)])

    def scatter_sum(value):
        value = value.reshape(-1, parts, sub, 2 * dirs)
        total = lax.dynamic_index_in_dim(value, col, 1, keepdims=False).astype(F32)
        for d in range(1, parts):
            sent = lax.dynamic_index_in_dim(value, col ^ d, 1, keepdims=False)
            total = total + swap(sent, "col", d).astype(F32)
        return total.astype(BF16).reshape(-1, 2 * dirs)

    def gather(mine, *earlier):
        pair = jnp.concatenate([mine, after(swap(mine, "col", 2), *earlier)], axis=0)
        return [pair, swap(pair, "col", 1)]

    sums = [scatter_sum(jnp.concatenate([own_own, own_end], axis=1)), scatter_sum(outer)]
    waits = sums[-1:]
    for k in (2, 3):
        product = project(
            flags,
            [(partner[k], 0, tok)],
            [(other[1], (k - 2) * tok, tok)],
            [grad_basis, near_basis, after(far_basis, *waits)],
            weight=8 if k == 2 else 8192,
        )
        if k == 2:
            sums.append(scatter_sum(product))
            early = jnp.concatenate(sums, axis=0)
            got = swap(early[:, dirs:], "row", 1)
            waits = [swap(early[:, :dirs], "col", 2)]
    pair = jnp.concatenate([early[:, :dirs], *waits], axis=0)
    early_own = [pair, swap(pair, "col", 1)]
    last = scatter_sum(after(product, got))
    got = after(got, last)
    last = after(last, every_act)
    last = jnp.concatenate([last[:, :dirs], swap(last[:, dirs:], "row", 1)], axis=0)
    early_got = gather(got, last)
    arrays = early_own + early_got + gather(last)
    every_act = after(every_act, last)

    def by_part(block):
        split = block.reshape(cands, parts, sub, -1)
        return jnp.stack(
            [lax.dynamic_index_in_dim(split, col ^ d, 1, keepdims=False) for d in (0, 2, 1, 3)]
        )

    act = [
        by_part(lax.dynamic_index_in_dim(every_act, i, 0, keepdims=False))
        for i in (row, row ^ 1, planes - 1 - row, planes - 1 - (row ^ 1))
    ]
    act_rot = [jnp.stack(act[i : i + 2], axis=1) for i in (0, 2)]
    act_rot = [jnp.moveaxis(x, 2, 0).reshape(cands, 2 * tok, -1) for x in act_rot]
    act_rot = jnp.concatenate(act_rot, axis=1)

    segments = [[] for _ in range(cands)]
    for kind in (0, 1):
        for c in range(cands):
            for j in (0, 1):
                for side in (0, 1):
                    for plane in (0, 1):
                        base = side * early.shape[0]
                        if kind == 0:
                            segments[c].append((2 * plane + j, base + c * sub, sub))
                        elif c < cands - 1:
                            segments[c].append((2 * plane + j, base + (cands + c) * sub, sub))
                        else:
                            segments[c].append((4 + j, (side * 2 + plane) * sub, sub))
    layout = tuple(tuple(s) for s in segments)

    rotated, scores = rotate_and_score(arrays, layout, act_rot, eigenvalues, query_rotated)
    scores = exchange_sum(exchange_sum(scores, "col", parts), "row", planes)
    return rotated, scores


def solution(mesh):
    placed = (
        P("groups", "row", None),
        P("groups", "row", "col"),
        P(None, "col"),
        P("col", "row"),
        P("row", "col"),
        P(None, "row", "col"),
        P("groups"),
        P(),
    )
    chain = mesh.shape["groups"] == 2 and mesh.shape["row"] == 4 and mesh.shape["col"] == 4
    return jax.shard_map(
        chain_body if chain else gather_body,
        mesh=mesh,
        in_specs=placed,
        out_specs=(P("groups", "row", "col"), P(None, "groups")),
        check_vma=False,
    )
```

```python
import functools

import jax
import jax.numpy as jnp
from jax import lax
from jax.experimental import pallas as pl
from jax.experimental.pallas import tpu as pltpu
from jax.sharding import PartitionSpec as P

DAMPING = 0.05
BF16 = jnp.bfloat16
F32 = jnp.float32


def candidate_lengths(example_ids, token_counts):
    pool_size = token_counts.shape[0]
    hits = example_ids[:, None] == jnp.arange(pool_size, dtype=jnp.int32)[None, :]
    return jnp.sum(jnp.where(hits, token_counts[None, :], 0), axis=1)


def local_activations(acts, act_basis, lengths):
    tok = acts.shape[1]
    positions = lax.axis_index("row") * tok + jnp.arange(tok, dtype=jnp.int32)
    live = (positions[None, :] < lengths[:, None]).astype(F32)
    rotated = jnp.einsum("ctd,dk->ctk", acts, act_basis, preferred_element_type=F32)
    return (rotated * live[:, :, None]).astype(BF16)


def final_kernel(layout, count, *refs):
    arrays = refs[:count]
    act_ref, eig_ref, query_ref, out_ref, score_ref = refs[count:]
    queries = query_ref.shape[0]
    damped = eig_ref[...] + DAMPING
    weights = [query_ref[q].astype(F32) / damped for q in range(queries)]
    rows = [[] for _ in range(queries)]
    for c, segments in enumerate(layout):
        tokens = jnp.concatenate([arrays[i][s : s + n] for i, s, n in segments], axis=0)
        tile = lax.dot_general(
            tokens, act_ref[c], (((0,), (0,)), ((), ())), preferred_element_type=F32
        )
        out_ref[c] = tile
        for q in range(queries):
            rows[q].append(jnp.sum(weights[q] * tile, axis=0, keepdims=True))
    score_ref[0] = jnp.concatenate([r for one in rows for r in one], axis=0)


def rotate_and_score(arrays, layout, act_rot, eigenvalues, query_rotated):
    cands, seq, width = act_rot.shape
    dirs = eigenvalues.shape[0]
    queries = query_rotated.shape[0]
    block = min(dirs, 256)
    steps = dirs // block
    rotated, partial_scores = pl.pallas_call(
        functools.partial(final_kernel, layout, len(arrays)),
        grid=(steps,),
        in_specs=[pl.BlockSpec((x.shape[0], block), lambda i: (0, i)) for x in arrays]
        + [
            pl.BlockSpec((cands, seq, width), lambda i: (0, 0, 0)),
            pl.BlockSpec((block, width), lambda i: (i, 0)),
            pl.BlockSpec((queries, block, width), lambda i: (0, i, 0)),
        ],
        out_specs=[
            pl.BlockSpec((cands, block, width), lambda i: (0, i, 0)),
            pl.BlockSpec((1, queries * cands, width), lambda i: (i, 0, 0)),
        ],
        out_shape=[
            jax.ShapeDtypeStruct((cands, dirs, width), F32),
            jax.ShapeDtypeStruct((steps, queries * cands, width), F32),
        ],
        compiler_params=pltpu.CompilerParams(vmem_limit_bytes=16 * 2**20),
    )(*arrays, act_rot, eigenvalues, query_rotated)
    return rotated, jnp.sum(partial_scores, axis=(0, 2)).reshape(queries, cands)


def gather_body(acts, grads, act_basis, grad_basis, eigenvalues, query_rotated, example_ids, token_counts):
    lengths = candidate_lengths(example_ids, token_counts)
    local_act = local_activations(acts, act_basis, lengths)
    partial_value = jnp.einsum(
        "ctd,dj->ctj",
        lax.all_gather(grads, "row", axis=1, tiled=True),
        grad_basis,
        preferred_element_type=F32,
    )
    every_act = lax.all_gather(local_act, "row", axis=1, tiled=True)
    rotated_grads = lax.psum(partial_value, "col").astype(BF16)
    cands, seq = rotated_grads.shape[:2]
    arrays = [rotated_grads[c] for c in range(cands)]
    layout = tuple(((c, 0, seq),) for c in range(cands))
    rotated, scores = rotate_and_score(arrays, layout, every_act, eigenvalues, query_rotated)
    return rotated, lax.psum(scores, ("row", "col"))


def after(value, *earlier):
    return lax.optimization_barrier((value, *earlier))[0]


def project_kernel(ends, count, widths, *refs):
    flags, refs = refs[0], refs[1:]
    tokens, basis, out, acc = refs[:count], refs[count:-2], refs[-2], refs[-1]
    step = pl.program_id(0)
    def joined(refs):
        return jnp.concatenate([t[...] for t in refs], axis=0) if len(refs) > 1 else refs[0][...]

    rows = joined(tokens[:ends])
    if count > ends:
        rows = jnp.where(flags[0] == 1, rows, joined(tokens[ends:]))
    start, spans = 0, []
    for width in widths:
        spans.append((start, start + width))
        start += width

    @pl.when(step == 0)
    def _():
        acc[...] = jnp.zeros_like(acc)

    for ref, (a, b) in zip(basis, spans):
        acc[:, a:b] += jnp.dot(rows, ref[...], preferred_element_type=F32)

    @pl.when(step == pl.num_programs(0) - 1)
    def _():
        if len(basis) == 1:
            out[...] = acc[...].astype(BF16)
        else:
            (c, d), (e, f) = spans[-2:]
            if c > 0:
                out[:, :c] = acc[:, :c].astype(BF16)

            @pl.when(flags[1] == 0)
            def _():
                out[:, c:f] = acc[:, c:f].astype(BF16)

            @pl.when(flags[1] != 0)
            def _():
                out[:, c:d] = acc[:, e:f].astype(BF16)
                out[:, e:f] = acc[:, c:d].astype(BF16)


def project(flags, ends, middles, bases, weight=8):
    tokens = ends + middles
    feats = bases[0].shape[0]
    widths = tuple(x.shape[1] for x in bases)
    block, total = 1024, sum(widths)
    rows = sum(n for _, _, n in ends)
    specs = []
    for _, start, n in tokens:
        assert start % n == 0
        specs.append(pl.BlockSpec((n, block), lambda k, i=start // n: (i, k)))
    return pl.pallas_call(
        functools.partial(project_kernel, len(ends), len(tokens), widths),
        grid=(feats // block,),
        in_specs=[pl.BlockSpec(memory_space=pltpu.SMEM)]
        + specs
        + [pl.BlockSpec((block, w), lambda k: (k, 0)) for w in widths],
        out_specs=pl.BlockSpec((rows, total), lambda k: (0, 0)),
        out_shape=jax.ShapeDtypeStruct((rows, total), BF16),
        scratch_shapes=[pltpu.VMEM((rows, total), F32)],
        compiler_params=pltpu.CompilerParams(vmem_limit_bytes=56 * 2**20),
        cost_estimate=pl.CostEstimate(
            flops=rows * feats * total // weight,
            bytes_accessed=feats * (total + rows) // weight,
            transcendentals=0,
        ),
    )(flags, *[array for array, _, _ in tokens], *bases)


def after(value, *earlier):
    return lax.optimization_barrier((value, *earlier))[0]


def exchange_sum(value, axis, size):
    total = value
    for d in range(1, size):
        total = total + lax.ppermute(value, axis, [(i, i ^ d) for i in range(size)])
    return total


def chain_body(acts, grads, act_basis, grad_basis, eigenvalues, query_rotated, example_ids, token_counts):
    cands, tok, feats = grads.shape
    dirs = grad_basis.shape[1]
    group, row, col = (lax.axis_index(a) for a in ("groups", "row", "col"))
    sides, planes, parts = 2, 4, 4
    middle, ends = [(1, 2), (2, 1)], [(0, 3), (3, 0)]
    beside = [(i, i ^ 1) for i in range(planes)]
    at_end = (row == 0) | (row == planes - 1)
    flags = jnp.stack([at_end.astype(jnp.int32), group.astype(jnp.int32)])

    half, flat = dirs // sides, grads.reshape(cands * tok, feats)
    units, deep, slab = 8, feats // 8, cands * tok // 8
    lengths = candidate_lengths(example_ids, token_counts)
    local_act = local_activations(acts, act_basis, lengths)
    near, far, other = [], [], []
    spans = [(0, 1), (1, 3), (3, 5), (5, 7), (7, units)]
    own_own = project(flags, [(flat, 0, cands * tok)], [], [grad_basis])
    for i, (a, b) in enumerate(spans):
        piece = lax.dynamic_slice(grad_basis, (a * deep, group * half), ((b - a) * deep, half))
        if i >= 2:
            early = {2: [own_own, local_act], 3: [other[0]], 4: []}[i]
            piece = after(piece, near[i - 2], *early)
        if i in (0, 2):
            part = flat[: 4 * slab] if i == 0 else after(flat, near[0])[4 * slab :]
            other.append(lax.ppermute(part, "row", middle))
        near.append(lax.ppermute(piece, "row", beside))
        far.append(lax.ppermute(near[i], "groups", [(0, 1), (1, 0)]))
    near_basis = jnp.concatenate(near, axis=0)
    far_basis = jnp.concatenate(far, axis=0)

    ranges = [(0, 2), (2, 4), (4, 6), (6, units)]
    phase = [near[3], near[4], other[1]]
    ties = [[*phase, far[0], far[1]], [*phase, far[2]], [far[4]], []]
    partner = []
    for k, (a, b) in enumerate(ranges):
        tie = ties[k] + ([partner[k - 2]] if k >= 2 else [])
        piece = flat[a * slab : b * slab]
        partner.append(lax.ppermute(after(piece, *tie), "row", ends))

    sub, full = tok // parts, cands * tok

    own_end = project(flags, [(flat, 0, full)], [], [near_basis, after(far_basis, partner[0])])
    outer = project(
        flags,
        [(partner[0], 0, 2 * slab), (partner[1], 0, 2 * slab)],
        [(other[0], 0, full // 2)],
        [grad_basis, near_basis, after(far_basis, own_end)],
    )

    def swap(value, axis, d):
        size = planes if axis == "row" else parts
        return lax.ppermute(value, axis, [(i, i ^ d) for i in range(size)])

    def scatter_sum(value):
        value = value.reshape(-1, parts, sub, 2 * dirs)
        total = lax.dynamic_index_in_dim(value, col, 1, keepdims=False).astype(F32)
        for d in range(1, parts):
            sent = lax.dynamic_index_in_dim(value, col ^ d, 1, keepdims=False)
            total = total + swap(sent, "col", d).astype(F32)
        return total.astype(BF16).reshape(-1, 2 * dirs)

    def gather(mine, *earlier):
        pair = jnp.concatenate([mine, after(swap(mine, "col", 2), *earlier)], axis=0)
        return [pair, swap(pair, "col", 1)]

    sums = [scatter_sum(jnp.concatenate([own_own, own_end], axis=1)), scatter_sum(outer)]
    waits = sums[-1:]
    for k in (2, 3):
        product = project(
            flags,
            [(partner[k], 0, tok)],
            [(other[1], (k - 2) * tok, tok)],
            [grad_basis, near_basis, after(far_basis, *waits)],
            weight=8 if k == 2 else 8192,
        )
        if k == 2:
            sums.append(scatter_sum(product))
            early = jnp.concatenate(sums, axis=0)
            got = swap(after(early[:, dirs:], partner[3]), "row", 1)
            waits = [swap(early[:, :dirs], "col", 2)]
    pair = jnp.concatenate([early[:, :dirs], *waits], axis=0)
    early_own = [pair, swap(pair, "col", 1)]
    last = scatter_sum(after(product, got))
    every_act = lax.all_gather(after(local_act, got), "row", axis=0)
    got = after(got, last)
    last = jnp.concatenate([last[:, :dirs], swap(last[:, dirs:], "row", 1)], axis=0)
    early_got = gather(got, last)
    arrays = early_own + early_got + gather(last)
    every_act = after(every_act, last)

    def by_part(block):
        split = block.reshape(cands, parts, sub, -1)
        return jnp.stack(
            [lax.dynamic_index_in_dim(split, col ^ d, 1, keepdims=False) for d in (0, 2, 1, 3)]
        )

    act = [
        by_part(lax.dynamic_index_in_dim(every_act, i, 0, keepdims=False))
        for i in (row, row ^ 1, planes - 1 - row, planes - 1 - (row ^ 1))
    ]
    act_rot = [jnp.stack(act[i : i + 2], axis=1) for i in (0, 2)]
    act_rot = [jnp.moveaxis(x, 2, 0).reshape(cands, 2 * tok, -1) for x in act_rot]
    act_rot = jnp.concatenate(act_rot, axis=1)

    segments = [[] for _ in range(cands)]
    for kind in (0, 1):
        for c in range(cands):
            for j in (0, 1):
                for side in (0, 1):
                    for plane in (0, 1):
                        base = side * early.shape[0]
                        if kind == 0:
                            segments[c].append((2 * plane + j, base + c * sub, sub))
                        elif c < cands - 1:
                            segments[c].append((2 * plane + j, base + (cands + c) * sub, sub))
                        else:
                            segments[c].append((4 + j, (side * 2 + plane) * sub, sub))
    layout = tuple(tuple(s) for s in segments)

    rotated, scores = rotate_and_score(arrays, layout, act_rot, eigenvalues, query_rotated)
    scores = exchange_sum(exchange_sum(scores, "col", parts), "row", planes)
    return rotated, scores


def solution(mesh):
    placed = (
        P("groups", "row", None),
        P("groups", "row", "col"),
        P(None, "col"),
        P("col", "row"),
        P("row", "col"),
        P(None, "row", "col"),
        P("groups"),
        P(),
    )
    chain = mesh.shape["groups"] == 2 and mesh.shape["row"] == 4 and mesh.shape["col"] == 4
    return jax.shard_map(
        chain_body if chain else gather_body,
        mesh=mesh,
        in_specs=placed,
        out_specs=(P("groups", "row", "col"), P(None, "groups")),
        check_vma=False,
    )
```

```python
import functools

import jax
import jax.numpy as jnp
from jax import lax
from jax.experimental import pallas as pl
from jax.experimental.pallas import tpu as pltpu
from jax.sharding import PartitionSpec as P

DAMPING = 0.05
BF16 = jnp.bfloat16
F32 = jnp.float32


def candidate_lengths(example_ids, token_counts):
    pool_size = token_counts.shape[0]
    hits = example_ids[:, None] == jnp.arange(pool_size, dtype=jnp.int32)[None, :]
    return jnp.sum(jnp.where(hits, token_counts[None, :], 0), axis=1)


def local_activations(acts, act_basis, lengths):
    tok = acts.shape[1]
    positions = lax.axis_index("row") * tok + jnp.arange(tok, dtype=jnp.int32)
    live = (positions[None, :] < lengths[:, None]).astype(F32)
    rotated = jnp.einsum("ctd,dk->ctk", acts, act_basis, preferred_element_type=F32)
    return (rotated * live[:, :, None]).astype(BF16)


def final_kernel(layout, count, *refs):
    arrays = refs[:count]
    act_ref, eig_ref, query_ref, out_ref, score_ref = refs[count:]
    queries = query_ref.shape[0]
    damped = eig_ref[...] + DAMPING
    weights = [query_ref[q].astype(F32) / damped for q in range(queries)]
    rows = [[] for _ in range(queries)]
    for c, segments in enumerate(layout):
        tokens = jnp.concatenate([arrays[i][s : s + n] for i, s, n in segments], axis=0)
        tile = lax.dot_general(
            tokens, act_ref[c], (((0,), (0,)), ((), ())), preferred_element_type=F32
        )
        out_ref[c] = tile
        for q in range(queries):
            rows[q].append(jnp.sum(weights[q] * tile, axis=0, keepdims=True))
    score_ref[0] = jnp.concatenate([r for one in rows for r in one], axis=0)


def rotate_and_score(arrays, layout, act_rot, eigenvalues, query_rotated):
    cands, seq, width = act_rot.shape
    dirs = eigenvalues.shape[0]
    queries = query_rotated.shape[0]
    block = min(dirs, 256)
    steps = dirs // block
    rotated, partial_scores = pl.pallas_call(
        functools.partial(final_kernel, layout, len(arrays)),
        grid=(steps,),
        in_specs=[pl.BlockSpec((x.shape[0], block), lambda i: (0, i)) for x in arrays]
        + [
            pl.BlockSpec((cands, seq, width), lambda i: (0, 0, 0)),
            pl.BlockSpec((block, width), lambda i: (i, 0)),
            pl.BlockSpec((queries, block, width), lambda i: (0, i, 0)),
        ],
        out_specs=[
            pl.BlockSpec((cands, block, width), lambda i: (0, i, 0)),
            pl.BlockSpec((1, queries * cands, width), lambda i: (i, 0, 0)),
        ],
        out_shape=[
            jax.ShapeDtypeStruct((cands, dirs, width), F32),
            jax.ShapeDtypeStruct((steps, queries * cands, width), F32),
        ],
        compiler_params=pltpu.CompilerParams(vmem_limit_bytes=16 * 2**20),
    )(*arrays, act_rot, eigenvalues, query_rotated)
    return rotated, jnp.sum(partial_scores, axis=(0, 2)).reshape(queries, cands)


def gather_body(acts, grads, act_basis, grad_basis, eigenvalues, query_rotated, example_ids, token_counts):
    lengths = candidate_lengths(example_ids, token_counts)
    local_act = local_activations(acts, act_basis, lengths)
    partial_value = jnp.einsum(
        "ctd,dj->ctj",
        lax.all_gather(grads, "row", axis=1, tiled=True),
        grad_basis,
        preferred_element_type=F32,
    )
    every_act = lax.all_gather(local_act, "row", axis=1, tiled=True)
    rotated_grads = lax.psum(partial_value, "col").astype(BF16)
    cands, seq = rotated_grads.shape[:2]
    arrays = [rotated_grads[c] for c in range(cands)]
    layout = tuple(((c, 0, seq),) for c in range(cands))
    rotated, scores = rotate_and_score(arrays, layout, every_act, eigenvalues, query_rotated)
    return rotated, lax.psum(scores, ("row", "col"))


def after(value, *earlier):
    return lax.optimization_barrier((value, *earlier))[0]


def project_kernel(ends, count, widths, *refs):
    flags, refs = refs[0], refs[1:]
    tokens, basis, out, acc = refs[:count], refs[count:-2], refs[-2], refs[-1]
    step = pl.program_id(0)
    def joined(refs):
        return jnp.concatenate([t[...] for t in refs], axis=0) if len(refs) > 1 else refs[0][...]

    rows = joined(tokens[:ends])
    if count > ends:
        rows = jnp.where(flags[0] == 1, rows, joined(tokens[ends:]))
    start, spans = 0, []
    for width in widths:
        spans.append((start, start + width))
        start += width

    @pl.when(step == 0)
    def _():
        acc[...] = jnp.zeros_like(acc)

    for ref, (a, b) in zip(basis, spans):
        acc[:, a:b] += jnp.dot(rows, ref[...], preferred_element_type=F32)

    @pl.when(step == pl.num_programs(0) - 1)
    def _():
        if len(basis) == 1:
            out[...] = acc[...].astype(BF16)
        else:
            (c, d), (e, f) = spans[-2:]
            if c > 0:
                out[:, :c] = acc[:, :c].astype(BF16)

            @pl.when(flags[1] == 0)
            def _():
                out[:, c:f] = acc[:, c:f].astype(BF16)

            @pl.when(flags[1] != 0)
            def _():
                out[:, c:d] = acc[:, e:f].astype(BF16)
                out[:, e:f] = acc[:, c:d].astype(BF16)


def project(flags, ends, middles, bases):
    tokens = ends + middles
    feats = bases[0].shape[0]
    widths = tuple(x.shape[1] for x in bases)
    block, total = 1024, sum(widths)
    rows = sum(n for _, _, n in ends)
    specs = []
    for _, start, n in tokens:
        assert start % n == 0
        specs.append(pl.BlockSpec((n, block), lambda k, i=start // n: (i, k)))
    return pl.pallas_call(
        functools.partial(project_kernel, len(ends), len(tokens), widths),
        grid=(feats // block,),
        in_specs=[pl.BlockSpec(memory_space=pltpu.SMEM)]
        + specs
        + [pl.BlockSpec((block, w), lambda k: (k, 0)) for w in widths],
        out_specs=pl.BlockSpec((rows, total), lambda k: (0, 0)),
        out_shape=jax.ShapeDtypeStruct((rows, total), BF16),
        scratch_shapes=[pltpu.VMEM((rows, total), F32)],
        compiler_params=pltpu.CompilerParams(vmem_limit_bytes=56 * 2**20),
        cost_estimate=pl.CostEstimate(
            flops=rows * feats * total // 8,
            bytes_accessed=feats * (total + rows) // 8,
            transcendentals=0,
        ),
    )(flags, *[array for array, _, _ in tokens], *bases)


def after(value, *earlier):
    return lax.optimization_barrier((value, *earlier))[0]


def exchange_sum(value, axis, size):
    total = value
    for d in range(1, size):
        total = total + lax.ppermute(value, axis, [(i, i ^ d) for i in range(size)])
    return total


def chain_body(acts, grads, act_basis, grad_basis, eigenvalues, query_rotated, example_ids, token_counts):
    cands, tok, feats = grads.shape
    dirs = grad_basis.shape[1]
    group, row, col = (lax.axis_index(a) for a in ("groups", "row", "col"))
    sides, planes, parts = 2, 4, 4
    middle, ends = [(1, 2), (2, 1)], [(0, 3), (3, 0)]
    beside = [(i, i ^ 1) for i in range(planes)]
    at_end = (row == 0) | (row == planes - 1)
    flags = jnp.stack([at_end.astype(jnp.int32), group.astype(jnp.int32)])

    half, flat = dirs // sides, grads.reshape(cands * tok, feats)
    units, deep, slab = 8, feats // 8, cands * tok // 8
    lengths = candidate_lengths(example_ids, token_counts)
    local_act = local_activations(acts, act_basis, lengths)
    near, far, other = [], [], []
    spans = [(0, 1), (1, 3), (3, 5), (5, 7), (7, units)]
    own_own = project(flags, [(flat, 0, cands * tok)], [], [grad_basis])
    for i, (a, b) in enumerate(spans):
        piece = lax.dynamic_slice(grad_basis, (a * deep, group * half), ((b - a) * deep, half))
        if i >= 2:
            early = {2: [own_own, local_act], 3: [other[0]], 4: []}[i]
            piece = after(piece, near[i - 2], *early)
        if i in (0, 2):
            part = flat[: 4 * slab] if i == 0 else after(flat[4 * slab :], near[0])
            other.append(lax.ppermute(part, "row", middle))
        near.append(lax.ppermute(piece, "row", beside))
        far.append(lax.ppermute(near[i], "groups", [(0, 1), (1, 0)]))
    near_basis = jnp.concatenate(near, axis=0)
    far_basis = jnp.concatenate(far, axis=0)

    ranges = [(0, 2), (2, 4), (4, 6), (6, units)]
    phase = [near[3], near[4], other[1]]
    ties = [[*phase, far[0], far[1]], [*phase, far[2]], [far[4]], []]
    partner = []
    for k, (a, b) in enumerate(ranges):
        tie = ties[k] + ([partner[k - 2]] if k >= 2 else [])
        piece = flat[a * slab : b * slab]
        partner.append(lax.ppermute(after(piece, *tie), "row", ends))

    sub, full = tok // parts, cands * tok

    own_end = project(flags, [(flat, 0, full)], [], [near_basis, after(far_basis, partner[0])])
    outer = project(
        flags,
        [(partner[0], 0, 2 * slab), (partner[1], 0, 2 * slab)],
        [(other[0], 0, full // 2)],
        [grad_basis, near_basis, after(far_basis, own_end)],
    )

    def swap(value, axis, d):
        size = planes if axis == "row" else parts
        return lax.ppermute(value, axis, [(i, i ^ d) for i in range(size)])

    def scatter_sum(value):
        value = value.reshape(-1, parts, sub, 2 * dirs)
        total = lax.dynamic_index_in_dim(value, col, 1, keepdims=False).astype(F32)
        for d in range(1, parts):
            sent = lax.dynamic_index_in_dim(value, col ^ d, 1, keepdims=False)
            total = total + swap(sent, "col", d).astype(F32)
        return total.astype(BF16).reshape(-1, 2 * dirs)

    def gather(mine, *earlier):
        pair = jnp.concatenate([mine, after(swap(mine, "col", 2), *earlier)], axis=0)
        return [pair, swap(pair, "col", 1)]

    sums = [scatter_sum(jnp.concatenate([own_own, own_end], axis=1)), scatter_sum(outer)]
    for k in (2, 3):
        product = project(
            flags,
            [(partner[k], 0, tok)],
            [(other[1], (k - 2) * tok, tok)],
            [grad_basis, near_basis, after(far_basis, sums[-1])],
        )
        if k == 2:
            sums.append(scatter_sum(product))
            early = jnp.concatenate(sums, axis=0)
            got = swap(early[:, dirs:], "row", 1)
    every_act = lax.all_gather(after(local_act, got), "row", axis=0)
    early_own = gather(early[:, :dirs])
    last = scatter_sum(after(product, got, *early_own))
    got = after(got, last)
    last = jnp.concatenate([last[:, :dirs], swap(last[:, dirs:], "row", 1)], axis=0)
    early_got = gather(got, last)
    arrays = early_own + early_got + gather(last)
    every_act = after(every_act, last)

    def by_part(block):
        split = block.reshape(cands, parts, sub, -1)
        return jnp.stack(
            [lax.dynamic_index_in_dim(split, col ^ d, 1, keepdims=False) for d in (0, 2, 1, 3)]
        )

    act = [
        by_part(lax.dynamic_index_in_dim(every_act, i, 0, keepdims=False))
        for i in (row, row ^ 1, planes - 1 - row, planes - 1 - (row ^ 1))
    ]
    act_rot = [jnp.stack(act[i : i + 2], axis=1) for i in (0, 2)]
    act_rot = [jnp.moveaxis(x, 2, 0).reshape(cands, 2 * tok, -1) for x in act_rot]
    act_rot = jnp.concatenate(act_rot, axis=1)

    segments = [[] for _ in range(cands)]
    for kind in (0, 1):
        for c in range(cands):
            for j in (0, 1):
                for side in (0, 1):
                    for plane in (0, 1):
                        base = side * early.shape[0]
                        if kind == 0:
                            segments[c].append((2 * plane + j, base + c * sub, sub))
                        elif c < cands - 1:
                            segments[c].append((2 * plane + j, base + (cands + c) * sub, sub))
                        else:
                            segments[c].append((4 + j, (side * 2 + plane) * sub, sub))
    layout = tuple(tuple(s) for s in segments)

    rotated, scores = rotate_and_score(arrays, layout, act_rot, eigenvalues, query_rotated)
    scores = exchange_sum(exchange_sum(scores, "col", parts), "row", planes)
    return rotated, scores


def solution(mesh):
    placed = (
        P("groups", "row", None),
        P("groups", "row", "col"),
        P(None, "col"),
        P("col", "row"),
        P("row", "col"),
        P(None, "row", "col"),
        P("groups"),
        P(),
    )
    chain = mesh.shape["groups"] == 2 and mesh.shape["row"] == 4 and mesh.shape["col"] == 4
    return jax.shard_map(
        chain_body if chain else gather_body,
        mesh=mesh,
        in_specs=placed,
        out_specs=(P("groups", "row", "col"), P(None, "groups")),
        check_vma=False,
    )
```
